32 devices in a mesh: dp: 4 (over y, core), fsdp: 8 (over z, x).
Axes of the slice: x: 2, y: 2, z: 4, core: 2. Of those that a mesh axis runs over, the one named last changes fastest.
Arguments:
- history: bfloat16 [9, 8192, 2048], P(None, ('dp', 'fsdp')), may hold values from -6 to 6
- out_grad: bfloat16 [8192, 2048], P(('dp', 'fsdp')), may hold values from -6 to 6
- doc_lengths: int32 [32, 3], P(('dp', 'fsdp')), may hold values from 1 to 170, 256 in all within a row
- doc_domain: int32 [32, 3], P(('dp', 'fsdp')), may hold values from 0 to 21
- domain_weight: int32 [22], replicated, may hold values from 64 to 511
- attn_weight: bfloat16 [4, 2048, 2048], P(None, 'fsdp')
- attn_master: float32 [4, 2048, 2048], P(None, 'fsdp', 'dp')
- attn_moment: float32 [4, 2048, 2048], P(None, 'fsdp', 'dp'), may hold values from -240 to 240
- mlp_weight: bfloat16 [2, 2048, 8192], P(None, 'fsdp'), may hold values from -0.125 to 0.125
- mlp_master: float32 [2, 2048, 8192], P(None, 'fsdp', 'dp'), may hold values from -0.125 to 0.125
- mlp_moment: float32 [2, 2048, 8192], P(None, 'fsdp', 'dp'), may hold values from -360 to 360
- params: float32 [53, 2048], P(None, 'fsdp')
- params_m: float32 [53, 2048], P(None, 'fsdp'), may hold values from -12 to 12
- params_v: float32 [53, 2048], P(None, 'fsdp'), may hold values from 4 to 400
- mix_out: float32 [37, 36], replicated, may hold values from -0.9 to 0.9
- mix_out_m: float32 [37, 36], replicated, may hold values from -12 to 12
- mix_out_v: float32 [37, 36], replicated, may hold values from 4 to 400
Outputs:
- layer_out: bfloat16 [8192, 2048], P(('dp', 'fsdp'))
- history_grad: bfloat16 [9, 8192, 2048], P(None, ('dp', 'fsdp'))
- attn_grad: float32 [4, 2048, 2048], P(None, 'fsdp', 'dp')
- attn_moment_new: float32 [4, 2048, 2048], P(None, 'fsdp', 'dp')
- attn_master_new: float32 [4, 2048, 2048], P(None, 'fsdp', 'dp')
- attn_copy: bfloat16 [4, 2048, 2048], P(None, 'fsdp')
- mlp_grad: float32 [2, 2048, 8192], P(None, 'fsdp', 'dp')
- mlp_moment_new: float32 [2, 2048, 8192], P(None, 'fsdp', 'dp')
- mlp_master_new: float32 [2, 2048, 8192], P(None, 'fsdp', 'dp')
- mlp_copy: bfloat16 [2, 2048, 8192], P(None, 'fsdp')
- params_grad: float32 [53, 2048], P(None, 'fsdp')
- residual_bias_grad: float32 [2, 2048], P(None, 'fsdp')
- params_m_new: float32 [53, 2048], P(None, 'fsdp')
- params_v_new: float32 [53, 2048], P(None, 'fsdp')
- params_new: float32 [53, 2048], P(None, 'fsdp')
- mix_out_grad: float32 [37, 36], replicated
- mix_out_m_new: float32 [37, 36], replicated
- mix_out_v_new: float32 [37, 36], replicated
- mix_out_new: float32 [37, 36], replicated
The draws below stay inside these ranges and needn't reach their ends.
Inputs may be any that keep to these rules, and one draw needn't show every extreme that they name: `doc_lengths`: each packed row holds 3 document lengths that sum to 256; the longest is exactly 170.
All inputs are finite; a program needn't handle non-finite values.
Results may differ from the reference program's by a relative error of at most 0.007.
The reference program's roundings to bfloat16 on the way count: a program that leaves them out, or rounds other values in their place, can miss the bound.
Values may be sent and summed in bfloat16 or wider, within the bound.
No kernel may reach another device: no remote copies, remote signals or barrier semaphores. Data moves between devices by JAX's collectives and lax.ppermute only.
A program may use at most 704 MiB of HBM per device.

```python
import math
import jax
import jax.numpy as jnp
import numpy as np
from jax import lax

D = 2048
HEADS = 16
HEAD = 128
FF = 8192
ROT = 32
HIST = 9
MIXW = 36
DOCS = 3
NDOM = 22
STEP = 6
TOK_DEV = 256
LONGEST = 170
PACKS = 32
TOKENS = 8192
BLOCK = 256


def attn_stack(key, salt):
    subkey = jax.random.fold_in(key, salt)
    base = jax.random.normal(subkey, (4, D, D), jnp.float32)
    factor = jnp.where(jnp.arange(4)[:, None, None] == 3, 4.0, 1.0)
    return base * factor * D ** (-0.5)


def draw_attn_weight(key, part):
    return attn_stack(key, 11).astype(jnp.bfloat16)


def draw_attn_master(key, part):
    return attn_stack(key, 12)


def draw_params(key, part):
    subkey = jax.random.fold_in(key, 21)
    base = jnp.clip(jax.random.normal(subkey, (17 + MIXW, D), jnp.float32), -4.0, 4.0)
    rows = jnp.arange(17 + MIXW)[:, None]
    gains = 1.0 + 0.12 * base
    return jnp.where(rows < 4, gains, jnp.where(rows < 17, 0.3 * base, base * D ** (-0.5)))


def set_ends(drawn, rng, least, high):
    place = [jax.random.randint(jax.random.fold_in(rng, axis), (), 0, length) for axis, length in enumerate(drawn.shape)]
    widest = drawn.shape.index(max(drawn.shape))
    neighbour = place[:widest] + [(place[widest] + 1) % drawn.shape[widest]] + place[widest + 1:]
    return drawn.at[tuple(place)].set(least).at[tuple(neighbour)].set(high)


def level_of(rng, dims, split, least, top_value):
    def one(axis_at, shards_of):
        steps = jax.random.uniform(jax.random.fold_in(jax.random.fold_in(rng, 6), axis_at), (shards_of,), jnp.float32, least / len(split), top_value / len(split))
        return jnp.repeat(jnp.exp(steps), dims[axis_at] // shards_of).reshape((-1,) + (1,) * (len(dims) - axis_at - 1))

    level = one(*split[0])
    for cut in split[1:]:
        level = level * one(*cut)
    return level


def split_up(amount, total, limit, lean):
    portions = [(1 << 20) // math.isqrt(grade ** lean) + 1 for grade in range(2, amount + 1)]
    surplus, given = total - limit - (amount - 1), [1] * (amount - 1)
    while surplus > 0:
        movable = [i for i in range(amount - 1) if given[i] < limit]
        whole, left = sum([portions[i] for i in movable]), surplus
        for i in movable:
            addition = min(limit - given[i], max(1, left * portions[i] // whole), surplus)
            given[i] = given[i] + addition
            surplus = surplus - addition
    return np.array([limit] + given)


def ragged(stream_key, count, total, bound, slope):
    if count == 2:
        one = jax.random.randint(stream_key, (), max(1, total - bound), min(bound, total - 1) + 1)
        return jnp.stack([one, total - one])
    tallies = jnp.asarray(split_up(count, total, bound, slope), jnp.int32)
    pairs = (count - 1) // 2
    source_of, sink = tallies[1:1 + 2 * pairs:2], tallies[2:2 + 2 * pairs:2]
    slack = jnp.minimum(source_of - 1, bound - sink)
    shifted = jax.random.randint(jax.random.fold_in(stream_key, 1), (pairs,), 0, 1 << 20) % (slack + 1)
    tallies = tallies.at[1:1 + 2 * pairs:2].set(source_of - shifted).at[2:2 + 2 * pairs:2].set(sink + shifted)
    return tallies[jax.random.permutation(jax.random.fold_in(stream_key, 2), count)]


def normal_values(rng, extent, spread, reach, pieces=(), kind=jnp.bfloat16):
    entries = spread * jax.random.normal(rng, extent, jnp.float32)
    if pieces:
        entries = entries * level_of(rng, extent, pieces, -0.22, 0.18)
    return jnp.clip(entries, -reach, reach).astype(kind)


def setup_inputs(seed: int = 0) -> dict:
    streams_of = jax.random.split(jax.random.key(seed), 18)
    history = normal_values(streams_of[0], (HIST, TOKENS, D), 1.0, 6.0, ((1, 32),))
    out_grad = normal_values(streams_of[1], (TOKENS, D), 1.0, 6.0, ((0, 32),))
    doc_lengths = jax.vmap(lambda own: ragged(own, DOCS, TOK_DEV, LONGEST, 2))(jax.random.split(streams_of[2], PACKS)).reshape((PACKS, DOCS)).astype(jnp.int32)
    doc_domain = set_ends(jax.random.randint(streams_of[3], (PACKS, DOCS), 0, NDOM), jax.random.fold_in(streams_of[3], 1), 0, NDOM - 1).astype(jnp.int32)
    domain_weight = set_ends(jax.random.randint(streams_of[4], (NDOM,), 64, 512), jax.random.fold_in(streams_of[4], 1), 64, 511).astype(jnp.int32)
    attn_weight = draw_attn_weight(jax.random.fold_in(streams_of[17], 71), 0)
    attn_master = draw_attn_master(jax.random.fold_in(streams_of[17], 71), 0)
    attn_moment = normal_values(streams_of[7], (4, D, D), 40.0, 240.0, ((1, 8), (2, 4)), jnp.float32)
    mlp_weight = normal_values(streams_of[8], (2, D, FF), D ** -0.5, 0.125, ((1, 8),))
    mlp_master = normal_values(streams_of[9], (2, D, FF), D ** -0.5, 0.125, ((1, 8), (2, 4)), jnp.float32)
    mlp_moment = normal_values(streams_of[10], (2, D, FF), 60.0, 360.0, ((1, 8), (2, 4)), jnp.float32)
    params = draw_params(jax.random.fold_in(streams_of[17], 71), 0)
    params_m = normal_values(streams_of[12], (17 + MIXW, D), 2.0, 12.0, ((1, 8),), jnp.float32)
    params_v = jnp.clip(jnp.exp(math.log(400.0) - 4.6051702 * jax.random.uniform(streams_of[13], (17 + MIXW, D), jnp.float32) ** level_of(streams_of[13], (17 + MIXW, D), ((1, 8),), -0.2, 0.2)), 4.0, 400.0)
    mix_out = normal_values(streams_of[14], (MIXW + 1, MIXW), 0.15, 0.9, (), jnp.float32)
    mix_out_m = normal_values(streams_of[15], (MIXW + 1, MIXW), 2.0, 12.0, (), jnp.float32)
    mix_out_v = jnp.clip(jnp.exp(jax.random.uniform(streams_of[16], (MIXW + 1, MIXW), jnp.float32, math.log(4.0), math.log(400.0))), 4.0, 400.0)
    return dict(history=history, out_grad=out_grad, doc_lengths=doc_lengths, doc_domain=doc_domain, domain_weight=domain_weight, attn_weight=attn_weight, attn_master=attn_master, attn_moment=attn_moment, mlp_weight=mlp_weight, mlp_master=mlp_master, mlp_moment=mlp_moment, params=params, params_m=params_m, params_v=params_v, mix_out=mix_out, mix_out_m=mix_out_m, mix_out_v=mix_out_v)


@jax.custom_vjp
def low(v):
    return lax.optimization_barrier(v.astype(jnp.bfloat16)).astype(jnp.float32)

@jax.custom_vjp
def low_back(v):
    return v

def low_keep(v):
    return (low(v), None)

def low_pass(kept, grad):
    return (grad,)

def back_keep(v):
    return (v, None)

def back_low(kept, grad):
    return (low(grad),)
low.defvjp(low_keep, low_pass)
low_back.defvjp(back_keep, back_low)
NS_A = 3.4445
NS_B = -4.775
NS_C = 2.0315
ROPE_BASE = 10000.0
LR_MUON = 0.1
LR_ADAM = 0.03
DECAY = 0.01
MOMENTUM = 0.95
BETA_ONE = 0.9
BETA_TWO = 0.95
HIGHEST = lax.Precision.HIGHEST

def matmul(left_side, right_side):
    return jnp.dot(left_side, right_side, precision=HIGHEST, preferred_element_type=jnp.float32)

def rope_tables(tok_count):
    half_rot = ROT // 2
    inverse_freq = ROPE_BASE ** (-(2.0 * jnp.arange(half_rot, dtype=jnp.float32)) / ROT)
    angles = jnp.arange(tok_count, dtype=jnp.float32)[:, None] * inverse_freq[None, :]
    return (jnp.cos(angles)[:, None, :], jnp.sin(angles)[:, None, :])

def rotate(values, cosine, sine_tab):
    half_rot = cosine.shape[-1]
    first_half = values[..., :half_rot]
    second_half = values[..., half_rot:2 * half_rot]
    remain = values[..., 2 * half_rot:]
    return jnp.concatenate([first_half * cosine - second_half * sine_tab, second_half * cosine + first_half * sine_tab, remain], -1)

def layer_norm(values, gain_row, shift_row):
    centred = values - lax.optimization_barrier(jnp.mean(values, -1, keepdims=True))
    return centred * lax.rsqrt(lax.optimization_barrier(jnp.mean(centred * centred, -1, keepdims=True)) + 1e-05) * gain_row + shift_row

def exact_gelu(values):
    return jax.nn.gelu(values, approximate=False)

def pack_info(lengths, domains, weight_table, tok_count):
    doc_ends = jnp.cumsum(lengths)
    positions = jnp.arange(tok_count, dtype=jnp.int32)
    doc_of = lax.optimization_barrier(jnp.sum((positions[:, None] >= doc_ends[None, :]).astype(jnp.int32), 1))
    allowed = (doc_of[:, None] == doc_of[None, :]) & (positions[:, None] >= positions[None, :])
    domain = lax.optimization_barrier(jnp.sum(jnp.where(doc_of[:, None] == jnp.arange(DOCS, dtype=jnp.int32)[None, :], domains[None, :], 0), 1))
    weight = lax.optimization_barrier(jnp.sum(jnp.where(domain[:, None] == jnp.arange(NDOM, dtype=jnp.int32)[None, :], weight_table[None, :], 0), 1))
    return (allowed, weight.astype(jnp.float32) / 256.0)

def forward(attn_mats, mlp_mats, params, mix_out, history, allowed):
    param_vals = low(params)
    mixing = low(mix_out)
    hist_count, tok_count, model_width = history.shape
    last_hist = history[hist_count - 1]
    unit_rms = last_hist * lax.rsqrt(lax.optimization_barrier(jnp.mean(last_hist * last_hist, -1, keepdims=True)) + 1e-06)
    inner_pre = low_back(matmul(low(unit_rms), param_vals[17:].T))
    hidden = exact_gelu(inner_pre)
    coeffs = (matmul(hidden, mixing[:MIXW]) + mixing[MIXW]).reshape(tok_count, 4, hist_count)
    streams = jnp.einsum('skj,jsd->ksd', coeffs, history, precision=HIGHEST)
    normed = [low(layer_norm(streams[member], param_vals[member], param_vals[4 + member])) for member in range(4)]
    cosine, sine_tab = rope_tables(tok_count)
    q_pre = low_back(matmul(normed[0], attn_mats[0]) + param_vals[8])
    k_pre = low_back(matmul(normed[1], attn_mats[1]) + param_vals[9])
    values = low(low_back(matmul(normed[2], attn_mats[2]) + param_vals[10])).reshape(tok_count, HEADS, HEAD)
    queries = low(rotate(q_pre.reshape(tok_count, HEADS, HEAD), cosine, sine_tab))
    key_rot = low(rotate(k_pre.reshape(tok_count, HEADS, HEAD), cosine, sine_tab))
    scores = jnp.einsum('qhd,khd->hqk', queries, key_rot, precision=HIGHEST) / math.sqrt(HEAD)
    scores = low_back(jnp.where(allowed[None], scores, -1000000000.0))
    attn_probs = low(jax.nn.softmax(scores, -1))
    context = jnp.einsum('hqk,khd->qhd', attn_probs, values, precision=HIGHEST).reshape(tok_count, model_width)
    context = low(low_back(context))
    attn_out = low_back(matmul(context, attn_mats[3]) + param_vals[11])
    up_pre = low_back(matmul(normed[3], mlp_mats[0]) + param_vals[13:17].reshape(-1))
    act_low = low(exact_gelu(up_pre))
    mlp_out = low_back(matmul(act_low, mlp_mats[1].T) + param_vals[12])
    return streams[3] + attn_out + mlp_out

def gram_of(blocks):
    return jnp.einsum('mik,mjk->mij', blocks, blocks, precision=HIGHEST)

def newton_step(current, gram_mat):
    poly_mat = NS_B * gram_mat + NS_C * jnp.einsum('mij,mjk->mik', gram_mat, gram_mat, precision=HIGHEST)
    return NS_A * current + jnp.einsum('mij,mjk->mik', poly_mat, current, precision=HIGHEST)

def muon(grad_in, moment, master, col_width):
    mom_new = MOMENTUM * moment + grad_in
    blocks = mom_new.reshape(-1, BLOCK, col_width)
    gram_mat = gram_of(blocks)
    block_norm = jnp.sqrt(jnp.trace(gram_mat, axis1=1, axis2=2)) + 1e-07
    current = blocks / block_norm[:, None, None]
    gram_mat = gram_mat / (block_norm * block_norm)[:, None, None]
    for ns_section in range(5):
        if ns_section > 0:
            gram_mat = gram_of(current)
        current = newton_step(current, gram_mat)
    master_new = master * (1.0 - LR_MUON * DECAY) - LR_MUON * 0.2 * math.sqrt(col_width) * current.reshape(master.shape)
    return (mom_new, master_new)

def adamw(current, grad_in, moment_one, moment_two):
    one_new = BETA_ONE * moment_one + (1.0 - BETA_ONE) * grad_in
    two_new = BETA_TWO * moment_two + (1.0 - BETA_TWO) * grad_in * grad_in
    one_hat = one_new / (1.0 - BETA_ONE ** STEP)
    two_hat = two_new / (1.0 - BETA_TWO ** STEP)
    updated = current * (1.0 - LR_ADAM * DECAY) - LR_ADAM * one_hat / (jnp.sqrt(two_hat) + 1e-08)
    return (one_new, two_new, updated)

def reference(history, out_grad, doc_lengths, doc_domain, domain_weight, attn_weight, attn_master, attn_moment, mlp_weight, mlp_master, mlp_moment, params, params_m, params_v, mix_out, mix_out_m, mix_out_v):
    attn_mats = attn_weight.astype(jnp.float32)
    mlp_mats = mlp_weight.astype(jnp.float32)
    hist_packs = jnp.moveaxis(history.reshape(HIST, PACKS, TOK_DEV, D), 1, 0)
    cot_packs = out_grad.reshape(PACKS, TOK_DEV, D)

    def pack_step(totals, pack_item):
        hist_pack, cot_pack, lengths, domains = pack_item
        allowed, weight = pack_info(lengths, domains, domain_weight, TOK_DEV)

        def pack_forward(attn_arg, mlp_arg, param_arg, mix_arg, hist_arg):
            return forward(attn_arg, mlp_arg, param_arg, mix_arg, hist_arg, allowed)
        layer_out, pullback = jax.vjp(pack_forward, attn_mats, mlp_mats, params, mix_out, hist_pack.astype(jnp.float32))
        pack_grads = pullback(cot_pack.astype(jnp.float32) * weight[:, None])
        new_totals = tuple((running + addend for running, addend in zip(totals, pack_grads[:4])))
        return (new_totals, (layer_out.astype(jnp.bfloat16), pack_grads[4].astype(jnp.bfloat16)))
    zeros_init = tuple((jnp.zeros(shaped.shape, jnp.float32) for shaped in (attn_mats, mlp_mats, params, mix_out)))
    totals, stacked = lax.scan(pack_step, zeros_init, (hist_packs, cot_packs, doc_lengths, doc_domain))
    attn_grad, mlp_grad, params_grad, mix_out_grad = totals
    layer_out = stacked[0].reshape(TOKENS, D)
    history_grad = jnp.moveaxis(stacked[1], 0, 1).reshape(HIST, TOKENS, D)
    attn_moment_new, attn_master_new = muon(attn_grad, attn_moment, attn_master, D)
    mlp_moment_new, mlp_master_new = muon(mlp_grad, mlp_moment, mlp_master, FF)
    params_m_new, params_v_new, params_new = adamw(params, params_grad, params_m, params_v)
    mix_out_m_new, mix_out_v_new, mix_out_new = adamw(mix_out, mix_out_grad, mix_out_m, mix_out_v)
    return (layer_out, history_grad, attn_grad, attn_moment_new, attn_master_new, attn_master_new.astype(jnp.bfloat16), mlp_grad, mlp_moment_new, mlp_master_new, mlp_master_new.astype(jnp.bfloat16), params_grad, params_grad[11:13], params_m_new, params_v_new, params_new, mix_out_grad, mix_out_m_new, mix_out_v_new, mix_out_new)
```

```python
import math

import jax
import jax.numpy as jnp
from jax import lax
from jax.sharding import PartitionSpec as P

HEADS = 16
HEAD = 128
FF = 8192
ROT = 32
MIXW = 36
DOCS = 3
NDOM = 22
STEP = 6


NS_A = 3.4445
NS_B = -4.775
NS_C = 2.0315
ROPE_BASE = 10000.0
LR_MUON = 0.1
LR_ADAM = 0.03
DECAY = 0.01
MOMENTUM = 0.95
BETA_ONE = 0.9
BETA_TWO = 0.95
HIGHEST = lax.Precision.HIGHEST


def exact_gelu(values):
    return jax.nn.gelu(values, approximate=False)


def rope_tables(tok_count):
    half_rot = ROT // 2
    inverse_freq = ROPE_BASE ** (-(2.0 * jnp.arange(half_rot, dtype=jnp.float32)) / ROT)
    angles = jnp.arange(tok_count, dtype=jnp.float32)[:, None] * inverse_freq[None, :]
    return (jnp.cos(angles)[:, None, :], jnp.sin(angles)[:, None, :])


def rotate(values, cosine, sine_tab):
    half_rot = cosine.shape[-1]
    first_half = values[..., :half_rot]
    second_half = values[..., half_rot : 2 * half_rot]
    remain = values[..., 2 * half_rot :]
    return jnp.concatenate(
        [
            first_half * cosine - second_half * sine_tab,
            second_half * cosine + first_half * sine_tab,
            remain,
        ],
        -1,
    )


def layer_norm(values, gain_row, shift_row):
    centred = values - jnp.mean(values, -1, keepdims=True)
    inv_std = lax.rsqrt(jnp.mean(centred * centred, -1, keepdims=True) + 1e-05)
    normed = centred * inv_std
    return (normed * gain_row + shift_row, normed, inv_std)


def norm_back(grad_out, normed, inv_std, gain_row):
    scaled = grad_out * gain_row
    grad_in = inv_std * (
        scaled
        - jnp.mean(scaled, -1, keepdims=True)
        - normed * jnp.mean(scaled * normed, -1, keepdims=True)
    )
    return (grad_in, jnp.sum(grad_out * normed, 0), jnp.sum(grad_out, 0))


def product_nt(left_side, right_side):
    return lax.dot_general(
        left_side, right_side, (((1,), (1,)), ((), ())), preferred_element_type=jnp.float32
    )


def product_tn(left_side, right_side):
    return lax.dot_general(
        left_side, right_side, (((0,), (0,)), ((), ())), preferred_element_type=jnp.float32
    )


def pack_info(lengths, domains, weight_table, tok_count):
    doc_ends = jnp.cumsum(lengths)
    positions = jnp.arange(tok_count, dtype=jnp.int32)
    doc_of = jnp.sum((positions[:, None] >= doc_ends[None, :]).astype(jnp.int32), 1)
    allowed = (doc_of[:, None] == doc_of[None, :]) & (positions[:, None] >= positions[None, :])
    domain = jnp.sum(
        jnp.where(
            doc_of[:, None] == jnp.arange(DOCS, dtype=jnp.int32)[None, :], domains[None, :], 0
        ),
        1,
    )
    weight = jnp.sum(
        jnp.where(
            domain[:, None] == jnp.arange(NDOM, dtype=jnp.int32)[None, :], weight_table[None, :], 0
        ),
        1,
    )
    return (allowed, weight.astype(jnp.float32) / 256.0)


def swap_core(values):
    return lax.ppermute(values, "dp", [(at, at ^ 1) for at in range(4)])


def swap_y(values):
    return lax.ppermute(values, "dp", [(at, at ^ 2) for at in range(4)])


def swap_x(values):
    count = lax.axis_size("fsdp")
    return lax.ppermute(values, "fsdp", [(at, at ^ 1) for at in range(count)])


def shift_z(values, hops):
    count = lax.axis_size("fsdp")
    return lax.ppermute(values, "fsdp", [(at, (at + 2 * hops) % count) for at in range(count)])


def gather_rows(shard):
    depth = lax.axis_size("fsdp") // 2
    z_at = lax.axis_index("fsdp") // 2
    x_at = lax.axis_index("fsdp") % 2
    ring = [shard] + [shift_z(shard, hops) for hops in range(1, depth)]
    whole = jnp.zeros((depth, 2) + shard.shape, shard.dtype)
    rest = (0,) * shard.ndim
    for hops in range(depth):
        owner = (z_at + depth - hops) % depth
        whole = lax.dynamic_update_slice(whole, ring[hops][None, None], (owner, x_at) + rest)
        other = swap_x(ring[hops])
        whole = lax.dynamic_update_slice(whole, other[None, None], (owner, 1 - x_at) + rest)
    return whole.reshape((2 * depth,) + shard.shape)


def scatter_rows(whole, link_type):
    count = lax.axis_size("fsdp")
    depth = count // 2
    z_at = lax.axis_index("fsdp") // 2
    x_at = lax.axis_index("fsdp") % 2
    paired = whole.reshape((depth, 2) + whole.shape[1:])

    def half(which):
        return lax.dynamic_index_in_dim(paired, which, 1, keepdims=False)

    arrived = swap_x(half(1 - x_at).astype(link_type))
    summed = half(x_at).astype(jnp.float32) + arrived.astype(jnp.float32)
    total = lax.dynamic_index_in_dim(summed, z_at, 0, keepdims=False)
    low_sum = summed.astype(link_type)
    for hops in range(1, depth):
        outgoing = lax.dynamic_index_in_dim(low_sum, (z_at + hops) % depth, 0, keepdims=False)
        total = total + shift_z(outgoing, hops).astype(jnp.float32)
    return total


def gather_group(values):
    across = swap_y(values)
    return [values, swap_core(values), across, swap_core(across)]


def scatter_group(parts):
    first = parts[0] + swap_core(parts[1].astype(jnp.bfloat16)).astype(jnp.float32)
    second = parts[2] + swap_core(parts[3].astype(jnp.bfloat16)).astype(jnp.float32)
    return first + swap_y(second.astype(jnp.bfloat16)).astype(jnp.float32)


def flip(values, step):
    blocks = values.reshape((4, values.shape[0] // 4) + values.shape[1:])
    return jnp.stack([blocks[at ^ step] for at in range(4)]).reshape(values.shape)


def gather_columns(values):
    across = flip(swap_y(values), 2)
    return [values, flip(swap_core(values), 1), across, flip(swap_core(across), 1)]


def scatter_columns(parts):
    first = parts[0] + swap_core(flip(parts[1].astype(jnp.bfloat16), 1)).astype(jnp.float32)
    second = parts[2] + swap_core(flip(parts[3].astype(jnp.bfloat16), 1)).astype(jnp.float32)
    return first + swap_y(flip(second.astype(jnp.bfloat16), 2)).astype(jnp.float32)


def sum_group(values):
    values = values + swap_core(values)
    return values + swap_y(values)


def sum_all(values):
    values = sum_group(values)
    count = lax.axis_size("fsdp")
    step = 1
    while step < count:
        values = values + lax.ppermute(
            values, "fsdp", [(at, at ^ step) for at in range(count)]
        )
        step *= 2
    return values


def by_member(parts, member):
    odd_core = member % 2 == 1
    high_y = member >= 2
    near = [jnp.where(odd_core, parts[1], parts[0]), jnp.where(odd_core, parts[0], parts[1])]
    far = [jnp.where(odd_core, parts[3], parts[2]), jnp.where(odd_core, parts[2], parts[3])]
    low_pair = [jnp.where(high_y, b, a) for a, b in zip(near, far)]
    high_pair = [jnp.where(high_y, a, b) for a, b in zip(near, far)]
    return low_pair + high_pair


def high_dot(equation, left_side, right_side):
    return jnp.einsum(
        equation, left_side, right_side, precision=HIGHEST, preferred_element_type=jnp.float32
    )


def orthogonal(moments):
    gram = jnp.concatenate([high_dot("mik,mjk->mij", part, part) for part in moments], 0)
    gram = sum_group(gram)
    norm = jnp.sqrt(jnp.trace(gram, axis1=1, axis2=2)) + 1e-07
    gram = gram / (norm * norm)[:, None, None]
    eye = jnp.eye(gram.shape[-1], dtype=jnp.float32)[None]
    chain = None
    for turn in range(5):
        square = high_dot("mij,mjk->mik", gram, gram)
        factor = NS_A * eye + NS_B * gram + NS_C * square
        chain = factor if chain is None else high_dot("mij,mjk->mik", factor, chain)
        if turn < 4:
            gram = high_dot("mij,mjk->mik", high_dot("mij,mjk->mik", factor, gram), factor)
    chain = chain / norm[:, None, None]
    results = []
    start = 0
    for part in moments:
        count = part.shape[0]
        results.append(high_dot("mij,mjk->mik", chain[start : start + count], part))
        start += count
    return results


def adamw(current, grad_in, moment_one, moment_two):
    one_new = BETA_ONE * moment_one + (1.0 - BETA_ONE) * grad_in
    two_new = BETA_TWO * moment_two + (1.0 - BETA_TWO) * grad_in * grad_in
    one_hat = one_new / (1.0 - BETA_ONE**STEP)
    two_hat = two_new / (1.0 - BETA_TWO**STEP)
    updated = current * (1.0 - LR_ADAM * DECAY) - LR_ADAM * one_hat / (jnp.sqrt(two_hat) + 1e-08)
    return (one_new, two_new, updated)


def columns_of(values, member, width, axis):
    return lax.dynamic_slice_in_dim(values, member * width, width, axis)


def body(
    history,
    out_grad,
    doc_lengths,
    doc_domain,
    domain_weight,
    attn_weight,
    attn_master,
    attn_moment,
    mlp_weight,
    mlp_master,
    mlp_moment,
    params,
    params_m,
    params_v,
    mix_out,
    mix_out_m,
    mix_out_v,
):
    hist_count, tok_count, model_width = history.shape
    members = lax.axis_size("fsdp")
    rows = attn_weight.shape[1]
    group = lax.axis_size("dp")
    member = lax.axis_index("dp")
    attn_cols = attn_weight.shape[2] // group
    mlp_cols = mlp_weight.shape[2] // group
    heads = HEADS // group
    group_tok = group * tok_count
    head_scale = 1.0 / math.sqrt(HEAD)

    param_pieces = gather_rows(params.astype(jnp.bfloat16))
    param_vals_low = jnp.moveaxis(param_pieces, 0, 1).reshape(params.shape[0], model_width)
    param_vals = param_vals_low.astype(jnp.float32)
    mix_weight = param_vals_low[17:]
    full_up = gather_rows(columns_of(mlp_weight[0], member, mlp_cols, 1)).reshape(
        model_width, mlp_cols
    )
    full_down = gather_rows(columns_of(mlp_weight[1], member, mlp_cols, 1)).reshape(
        model_width, mlp_cols
    )
    full_attn = gather_rows(columns_of(attn_weight, member, attn_cols, 2))
    full_attn = jnp.moveaxis(full_attn, 0, 1).reshape(4, model_width, attn_cols)

    mixing = lax.optimization_barrier(mix_out.astype(jnp.bfloat16)).astype(jnp.float32)
    _, tok_weight = pack_info(doc_lengths[0], doc_domain[0], domain_weight, tok_count)
    group_lengths = gather_group(doc_lengths)
    allowed = jnp.stack(
        [
            pack_info(lengths[0], doc_domain[0], domain_weight, tok_count)[0]
            for lengths in group_lengths
        ]
    )
    out_cot = out_grad.astype(jnp.float32) * tok_weight[:, None]
    cot_low = out_cot.astype(jnp.bfloat16)
    group_cot = jnp.concatenate(gather_group(cot_low), 0)

    last_hist = history[hist_count - 1].astype(jnp.float32)
    inv_rms = lax.rsqrt(jnp.mean(last_hist * last_hist, -1, keepdims=True) + 1e-06)
    unit_rms = last_hist * inv_rms
    unit_low = unit_rms.astype(jnp.bfloat16)
    inner_pre = product_nt(unit_low, mix_weight)
    hidden, gelu_inner = jax.vjp(exact_gelu, inner_pre)
    coeffs = (
        jnp.dot(hidden, mixing[:MIXW], precision=HIGHEST, preferred_element_type=jnp.float32)
        + mixing[MIXW]
    ).reshape(tok_count, 4, hist_count)
    streams = []
    for index in range(4):
        running = coeffs[:, index, 0, None] * history[0].astype(jnp.float32)
        for source in range(1, hist_count):
            running = running + coeffs[:, index, source, None] * history[source].astype(
                jnp.float32
            )
        streams.append(running)
    norm_keep = []
    group_normed = []
    for index in (3, 0, 1, 2):
        result, normed, inv_std = layer_norm(
            streams[index], param_vals[index], param_vals[4 + index]
        )
        group_normed.append(
            jnp.concatenate(gather_group(result.astype(jnp.bfloat16)), 0)
        )
        norm_keep.append((normed, inv_std))
    group_normed = group_normed[1:] + group_normed[:1]
    norm_keep = norm_keep[1:] + norm_keep[:1]

    up_bias = lax.dynamic_index_in_dim(param_vals, 13 + member, 0)
    up_pre = jnp.dot(group_normed[3], full_up, preferred_element_type=jnp.float32) + up_bias
    act_val, gelu_up = jax.vjp(exact_gelu, up_pre)
    act_low = act_val.astype(jnp.bfloat16)
    act_grad = jnp.dot(group_cot, full_down, preferred_element_type=jnp.float32)
    up_grad = gelu_up(act_grad)[0].astype(jnp.bfloat16)
    down_weight_grad = scatter_rows(
        product_tn(group_cot, act_low).astype(jnp.bfloat16).reshape(members, rows, mlp_cols),
        jnp.bfloat16,
    )
    up_weight_grad = scatter_rows(
        product_tn(group_normed[3], up_grad)
        .astype(jnp.bfloat16)
        .reshape(members, rows, mlp_cols),
        jnp.bfloat16,
    )
    mlp_in_grad = product_nt(up_grad, full_up)
    mlp_part = product_nt(act_low, full_down)

    def scatter_tokens(part):
        return scatter_group(
            [part[at * tok_count : (at + 1) * tok_count] for at in range(group)]
        )

    in_grads = [None, None, None, scatter_tokens(mlp_in_grad)]

    cosine, sine_tab = rope_tables(tok_count)

    def split_heads(values):
        return values.reshape(group, tok_count, heads, HEAD)

    def bias_piece(row):
        return lax.dynamic_slice(param_vals, (row, member * attn_cols), (1, attn_cols))

    q_pre = jnp.dot(group_normed[0], full_attn[0], preferred_element_type=jnp.float32) + bias_piece(8)
    k_pre = jnp.dot(group_normed[1], full_attn[1], preferred_element_type=jnp.float32) + bias_piece(9)
    value_low = split_heads(
        (
            jnp.dot(group_normed[2], full_attn[2], preferred_element_type=jnp.float32)
            + bias_piece(10)
        ).astype(jnp.bfloat16)
    )
    query_low = rotate(split_heads(q_pre), cosine, sine_tab).astype(jnp.bfloat16)
    key_low = rotate(split_heads(k_pre), cosine, sine_tab).astype(jnp.bfloat16)

    def pair(left_side, right_side):
        return jnp.einsum(
            "bqhd,bkhd->bhqk", left_side, right_side, preferred_element_type=jnp.float32
        )

    def take(weights, right_side):
        return jnp.einsum(
            "bhqk,bkhd->bqhd", weights, right_side, preferred_element_type=jnp.float32
        )

    def give(weights, right_side):
        return jnp.einsum(
            "bhqk,bqhd->bkhd", weights, right_side, preferred_element_type=jnp.float32
        )

    scores = jnp.where(allowed[:, None], pair(query_low, key_low) * head_scale, -1000000000.0)
    top_score = jnp.max(scores, -1, keepdims=True)
    log_total = top_score + jnp.log(jnp.sum(jnp.exp(scores - top_score), -1, keepdims=True))
    probs = jnp.exp(scores - log_total)
    probs_low = probs.astype(jnp.bfloat16)
    context_low = (
        take(probs_low, value_low).reshape(group_tok, attn_cols).astype(jnp.bfloat16)
    )
    group_context = jnp.concatenate(by_member(gather_columns(context_low), member), 1)
    attn_out = jnp.dot(group_context, full_attn[3], preferred_element_type=jnp.float32)
    out_part = lax.dynamic_update_slice(
        mlp_part,
        columns_of(mlp_part, member, attn_cols, 1) + attn_out,
        (0, member * attn_cols),
    )
    layer_out = (
        streams[3] + scatter_tokens(out_part) + (param_vals[11] + param_vals[12])
    ).astype(jnp.bfloat16)

    cot_cols = columns_of(group_cot, member, attn_cols, 1)
    context_grad_part = product_nt(cot_cols, full_attn[3])
    context_grad = split_heads(
        scatter_columns(
            [columns_of(context_grad_part, member ^ at, attn_cols, 1) for at in range(group)]
        ).astype(jnp.bfloat16)
    )
    prob_grad = pair(context_grad, value_low)
    score_grad = (
        probs * (prob_grad - jnp.sum(probs * prob_grad, -1, keepdims=True))
    ).astype(jnp.bfloat16)
    value_grad = give(probs_low, context_grad).reshape(group_tok, attn_cols).astype(jnp.bfloat16)
    query_grad = take(score_grad, key_low) * head_scale
    key_grad = give(score_grad, query_low) * head_scale
    query_back = (
        rotate(query_grad, cosine, -sine_tab).reshape(group_tok, attn_cols).astype(jnp.bfloat16)
    )
    key_back = (
        rotate(key_grad, cosine, -sine_tab).reshape(group_tok, attn_cols).astype(jnp.bfloat16)
    )
    proj_grads = (query_back, key_back, value_grad)
    for index in range(3):
        in_grads[index] = scatter_tokens(product_nt(proj_grads[index], full_attn[index]))
    lefts = (group_normed[0], group_normed[1], group_normed[2], group_context)
    rights = (query_back, key_back, value_grad, cot_cols)
    attn_grads = [
        scatter_rows(
            product_tn(left_side, right_side)
            .astype(jnp.bfloat16)
            .reshape(members, rows, attn_cols),
            jnp.bfloat16,
        )
        for left_side, right_side in zip(lefts, rights)
    ]

    stream_grads = []
    gain_list = []
    shift_list = []
    for index in range(4):
        grad_stream, gain_part, shift_part = norm_back(
            in_grads[index], norm_keep[index][0], norm_keep[index][1], param_vals[index]
        )
        stream_grads.append(grad_stream)
        gain_list.append(gain_part)
        shift_list.append(shift_part)
    stream_grads[3] = stream_grads[3] + out_cot
    coef_grad = jnp.stack(
        [
            jnp.stack(
                [
                    jnp.sum(history[source].astype(jnp.float32) * stream_grads[index], -1)
                    for source in range(hist_count)
                ],
                -1,
            )
            for index in range(4)
        ],
        1,
    )
    coef_flat = coef_grad.reshape(tok_count, 4 * hist_count)
    mixing_grad = jnp.concatenate(
        [
            jnp.dot(hidden.T, coef_flat, precision=HIGHEST, preferred_element_type=jnp.float32),
            jnp.sum(coef_flat, 0)[None],
        ],
        0,
    )
    hidden_grad = jnp.dot(
        coef_flat, mixing[:MIXW].T, precision=HIGHEST, preferred_element_type=jnp.float32
    )
    inner_grad = gelu_inner(hidden_grad)[0].astype(jnp.bfloat16)
    mix_weight_grad = product_tn(inner_grad, unit_low)
    unit_grad = jnp.dot(inner_grad, mix_weight, preferred_element_type=jnp.float32)
    last_grad = inv_rms * (unit_grad - unit_rms * jnp.mean(unit_grad * unit_rms, -1, keepdims=True))
    hist_parts = []
    for source in range(hist_count):
        running = coeffs[:, 0, source, None] * stream_grads[0]
        for index in range(1, 4):
            running = running + coeffs[:, index, source, None] * stream_grads[index]
        if source == hist_count - 1:
            running = running + last_grad
        hist_parts.append(running.astype(jnp.bfloat16))
    history_grad = jnp.stack(hist_parts)
    out_bias_grad = jnp.sum(cot_low.astype(jnp.float32), 0)

    def placed(values, width, at, total):
        return lax.dynamic_update_slice(
            jnp.zeros((total,), jnp.float32),
            jnp.sum(values.astype(jnp.float32), 0),
            (at * width,),
        )

    param_grad = jnp.concatenate(
        [
            jnp.stack(gain_list),
            jnp.stack(shift_list),
            jnp.stack([placed(part, attn_cols, member, model_width) for part in proj_grads]),
            out_bias_grad[None],
            out_bias_grad[None],
            placed(up_grad, mlp_cols, member, group * mlp_cols).reshape(-1, model_width),
            mix_weight_grad,
        ],
        0,
    )
    param_pieces_grad = jnp.moveaxis(
        param_grad.reshape(params.shape[0], members, rows), 1, 0
    )
    param_part = sum_group(scatter_rows(param_pieces_grad, jnp.float32))
    mixing_grad = sum_all(mixing_grad)

    mlp_grad = jnp.stack([up_weight_grad, down_weight_grad])
    attn_grad = jnp.stack(attn_grads)
    mlp_mom = MOMENTUM * mlp_moment + mlp_grad
    (mlp_cur,) = orthogonal([mlp_mom])
    mlp_new = mlp_master * (1.0 - LR_MUON * DECAY) - LR_MUON * 0.2 * math.sqrt(FF) * mlp_cur
    mlp_copy = jnp.concatenate(
        by_member(gather_group(mlp_new.astype(jnp.bfloat16)), member), 2
    )
    attn_mom = MOMENTUM * attn_moment + attn_grad
    (attn_cur,) = orthogonal([attn_mom])
    attn_new = (
        attn_master * (1.0 - LR_MUON * DECAY) - LR_MUON * 0.2 * math.sqrt(model_width) * attn_cur
    )
    attn_copy = jnp.concatenate(
        by_member(gather_group(attn_new.astype(jnp.bfloat16)), member), 2
    )
    params_m_new, params_v_new, params_new = adamw(params, param_part, params_m, params_v)
    mix_out_m_new, mix_out_v_new, mix_out_new = adamw(mix_out, mixing_grad, mix_out_m, mix_out_v)
    return (
        layer_out,
        history_grad,
        attn_grad,
        attn_mom,
        attn_new,
        attn_copy,
        mlp_grad,
        mlp_mom,
        mlp_new,
        mlp_copy,
        param_part,
        param_part[11:13],
        params_m_new,
        params_v_new,
        params_new,
        mixing_grad,
        mix_out_m_new,
        mix_out_v_new,
        mix_out_new,
    )


def solution(mesh):
    in_specs = (
        P(None, ("dp", "fsdp"), None),
        P(("dp", "fsdp"), None),
        P(("dp", "fsdp"), None),
        P(("dp", "fsdp"), None),
        P(),
        P(None, "fsdp", None),
        P(None, "fsdp", "dp"),
        P(None, "fsdp", "dp"),
        P(None, "fsdp", None),
        P(None, "fsdp", "dp"),
        P(None, "fsdp", "dp"),
        P(None, "fsdp"),
        P(None, "fsdp"),
        P(None, "fsdp"),
        P(),
        P(),
        P(),
    )
    out_specs = (
        P(("dp", "fsdp"), None),
        P(None, ("dp", "fsdp"), None),
        P(None, "fsdp", "dp"),
        P(None, "fsdp", "dp"),
        P(None, "fsdp", "dp"),
        P(None, "fsdp", None),
        P(None, "fsdp", "dp"),
        P(None, "fsdp", "dp"),
        P(None, "fsdp", "dp"),
        P(None, "fsdp", None),
        P(None, "fsdp"),
        P(None, "fsdp"),
        P(None, "fsdp"),
        P(None, "fsdp"),
        P(None, "fsdp"),
        P(),
        P(),
        P(),
        P(),
    )
    return jax.shard_map(body, mesh=mesh, in_specs=in_specs, out_specs=out_specs, check_vma=False)
```

```python
import math

import jax
import jax.numpy as jnp
from jax import lax
from jax.sharding import PartitionSpec as P

HEADS = 16
HEAD = 128
FF = 8192
ROT = 32
MIXW = 36
DOCS = 3
NDOM = 22
STEP = 6


NS_A = 3.4445
NS_B = -4.775
NS_C = 2.0315
ROPE_BASE = 10000.0
LR_MUON = 0.1
LR_ADAM = 0.03
DECAY = 0.01
MOMENTUM = 0.95
BETA_ONE = 0.9
BETA_TWO = 0.95
HIGHEST = lax.Precision.HIGHEST


def exact_gelu(values):
    return jax.nn.gelu(values, approximate=False)


def rope_tables(tok_count):
    half_rot = ROT // 2
    inverse_freq = ROPE_BASE ** (-(2.0 * jnp.arange(half_rot, dtype=jnp.float32)) / ROT)
    angles = jnp.arange(tok_count, dtype=jnp.float32)[:, None] * inverse_freq[None, :]
    return (jnp.cos(angles)[:, None, :], jnp.sin(angles)[:, None, :])


def rotate(values, cosine, sine_tab):
    half_rot = cosine.shape[-1]
    first_half = values[..., :half_rot]
    second_half = values[..., half_rot : 2 * half_rot]
    remain = values[..., 2 * half_rot :]
    return jnp.concatenate(
        [
            first_half * cosine - second_half * sine_tab,
            second_half * cosine + first_half * sine_tab,
            remain,
        ],
        -1,
    )


def layer_norm(values, gain_row, shift_row):
    centred = values - jnp.mean(values, -1, keepdims=True)
    inv_std = lax.rsqrt(jnp.mean(centred * centred, -1, keepdims=True) + 1e-05)
    normed = centred * inv_std
    return (normed * gain_row + shift_row, normed, inv_std)


def norm_back(grad_out, normed, inv_std, gain_row):
    scaled = grad_out * gain_row
    grad_in = inv_std * (
        scaled
        - jnp.mean(scaled, -1, keepdims=True)
        - normed * jnp.mean(scaled * normed, -1, keepdims=True)
    )
    return (grad_in, jnp.sum(grad_out * normed, 0), jnp.sum(grad_out, 0))


def product_nt(left_side, right_side):
    return lax.dot_general(
        left_side, right_side, (((1,), (1,)), ((), ())), preferred_element_type=jnp.float32
    )


def product_tn(left_side, right_side):
    return lax.dot_general(
        left_side, right_side, (((0,), (0,)), ((), ())), preferred_element_type=jnp.float32
    )


def pack_info(lengths, domains, weight_table, tok_count):
    doc_ends = jnp.cumsum(lengths)
    positions = jnp.arange(tok_count, dtype=jnp.int32)
    doc_of = jnp.sum((positions[:, None] >= doc_ends[None, :]).astype(jnp.int32), 1)
    allowed = (doc_of[:, None] == doc_of[None, :]) & (positions[:, None] >= positions[None, :])
    domain = jnp.sum(
        jnp.where(
            doc_of[:, None] == jnp.arange(DOCS, dtype=jnp.int32)[None, :], domains[None, :], 0
        ),
        1,
    )
    weight = jnp.sum(
        jnp.where(
            domain[:, None] == jnp.arange(NDOM, dtype=jnp.int32)[None, :], weight_table[None, :], 0
        ),
        1,
    )
    return (allowed, weight.astype(jnp.float32) / 256.0)


class Lane:
    def __init__(self):
        self.last = None

    def send(self, values, axis, pairs):
        if self.last is not None:
            values, _ = lax.optimization_barrier((values, self.last))
        self.last = lax.ppermute(values, axis, pairs)
        return self.last


class Links:
    def __init__(self):
        self.members = lax.axis_size("fsdp")
        self.depth = self.members // 2
        place = lax.axis_index("fsdp")
        self.z_at = place // 2
        self.x_at = place % 2
        self.member = lax.axis_index("dp")
        self.lanes = {name: Lane() for name in ("x", "up", "down", "y", "core")}

    def swap_core(self, values):
        return self.lanes["core"].send(values, "dp", [(at, at ^ 1) for at in range(4)])

    def swap_y(self, values):
        return self.lanes["y"].send(values, "dp", [(at, at ^ 2) for at in range(4)])

    def swap_x(self, values, low=0, high=None):
        high = self.depth if high is None else high
        pairs = [
            (at, at ^ 1)
            for at in range(self.members)
            if low <= at // 2 < high
        ]
        return self.lanes["x"].send(values, "fsdp", pairs)

    def slots(self):
        return [
            ((self.z_at + self.depth - hops) % self.depth) * 2
            + (self.x_at if side == 0 else 1 - self.x_at)
            for side in range(2)
            for hops in range(self.depth)
        ]

    def slot_of(self, owner):
        hops = (self.z_at + self.depth - owner // 2) % self.depth
        side = (owner % 2) ^ self.x_at
        return side * self.depth + hops

    def to_slots(self, values):
        width = values.shape[-1] // self.members
        return jnp.concatenate(
            [
                lax.dynamic_slice_in_dim(values, owner * width, width, values.ndim - 1)
                for owner in self.slots()
            ],
            -1,
        )

    def from_slots(self, values, first=0, count=None):
        width = values.shape[-1] // self.members
        count = self.members if count is None else count
        return jnp.concatenate(
            [
                lax.dynamic_slice_in_dim(
                    values, self.slot_of(first + at) * width, width, values.ndim - 1
                )
                for at in range(count)
            ],
            -1,
        )

    def gather_rows(self, shard):
        depth = self.depth
        z_at = self.z_at
        near = [shard]
        far = [self.swap_x(shard)]
        rise, fall, rise_far, fall_far = {}, {}, {}, {}
        up_run = down_run = shard
        for hops in range(1, depth):
            up_run = self.lanes["up"].send(
                up_run,
                "fsdp",
                [(at, at + 2) for at in range(2 * hops - 2, self.members - 2)],
            )
            down_run = self.lanes["down"].send(
                down_run,
                "fsdp",
                [(at + 2, at) for at in range(0, self.members - 2 * hops)],
            )
            rise[hops], fall[hops] = up_run, down_run
            if 2 * hops < depth:
                rise_far[hops] = self.swap_x(up_run, hops, depth)
                fall_far[hops] = self.swap_x(down_run, 0, depth - hops)
            else:
                either = jnp.where(z_at >= hops, up_run, down_run)
                pairs = [
                    (at, at ^ 1)
                    for at in range(self.members)
                    if at // 2 >= hops or at // 2 < depth - hops
                ]
                rise_far[hops] = fall_far[hops] = self.lanes["x"].send(either, "fsdp", pairs)
        for hops in range(1, depth):
            near.append(jnp.where(z_at >= hops, rise[hops], fall[depth - hops]))
            far.append(jnp.where(z_at >= hops, rise_far[hops], fall_far[depth - hops]))
        return jnp.concatenate(near + far, 0)

    def scatter_rows(self, left_side, right_side):
        half = left_side.shape[1] // 2
        rows = half // self.depth
        outgoing = product_tn(left_side[:, half:], right_side).astype(jnp.bfloat16)
        arrived = self.swap_x(outgoing).astype(jnp.float32)
        summed = (product_tn(left_side[:, :half], right_side) + arrived).astype(jnp.bfloat16)
        total = summed[:rows].astype(jnp.float32)
        for hops in range(1, self.depth):
            slot = self.depth - hops
            lane = self.lanes["down" if 2 * hops > self.depth else "up"]
            total = total + lane.send(
                summed[slot * rows : (slot + 1) * rows],
                "fsdp",
                [(at, (at + 2 * hops) % self.members) for at in range(self.members)],
            ).astype(jnp.float32)
        return total

    def gather_tokens(self, values):
        pair = jnp.concatenate([values, self.swap_y(values)], 0)
        return jnp.concatenate([pair, self.swap_core(pair)], 0)

    def scatter_tokens(self, values):
        half = values.shape[0] // 2
        quarter = half // 2
        arrived = self.swap_core(values[half:].astype(jnp.bfloat16))
        summed = values[:half] + arrived.astype(jnp.float32)
        return summed[:quarter] + self.swap_y(summed[quarter:].astype(jnp.bfloat16)).astype(
            jnp.float32
        )

    def partner(self, at):
        return self.member ^ ((at % 2) * 2 + at // 2)

    def gather_columns(self, values):
        across = self.swap_y(turn_y(values))
        pair = jnp.concatenate([values, across], 1)
        return jnp.concatenate([pair, self.swap_core(turn_core(pair))], 1)

    def scatter_columns(self, parts):
        sent = turn_core(jnp.concatenate(parts[2:], 1).astype(jnp.bfloat16))
        arrived = self.swap_core(sent)
        width = parts[0].shape[1]
        first = parts[0] + arrived[:, :width].astype(jnp.float32)
        second = parts[1] + arrived[:, width:].astype(jnp.float32)
        return first + self.swap_y(turn_y(second.astype(jnp.bfloat16))).astype(jnp.float32)

    def sum_group(self, values):
        values = values + self.swap_core(values)
        return values + self.swap_y(values)

    def gather_copies(self, values):
        across = self.swap_y(values)
        other, other_across = self.swap_core(jnp.stack([values, across]))
        odd_core = self.member % 2 == 1
        high_y = self.member >= 2
        near = [jnp.where(odd_core, other, values), jnp.where(odd_core, values, other)]
        far = [
            jnp.where(odd_core, other_across, across),
            jnp.where(odd_core, across, other_across),
        ]
        low_pair = [jnp.where(high_y, b, a) for a, b in zip(near, far)]
        high_pair = [jnp.where(high_y, a, b) for a, b in zip(near, far)]
        return jnp.concatenate(low_pair + high_pair, -1)


def turn_y(values):
    count = values.shape[0] // 4
    blocks = [values[at * count : (at + 1) * count] for at in (1, 0, 3, 2)]
    return jnp.concatenate(blocks, 0)


def turn_core(values):
    half = values.shape[0] // 2
    return jnp.concatenate([values[half:], values[:half]], 0)


def high_dot(equation, left_side, right_side):
    return jnp.einsum(
        equation, left_side, right_side, precision=HIGHEST, preferred_element_type=jnp.float32
    )


def orthogonal(links, moments):
    gram = links.sum_group(high_dot("mik,mjk->mij", moments, moments))
    norm = jnp.sqrt(jnp.trace(gram, axis1=1, axis2=2)) + 1e-07
    gram = gram / (norm * norm)[:, None, None]
    eye = jnp.eye(gram.shape[-1], dtype=jnp.float32)[None]
    chain = None
    for turn in range(5):
        square = high_dot("mij,mjk->mik", gram, gram)
        factor = NS_A * eye + NS_B * gram + NS_C * square
        chain = factor if chain is None else high_dot("mij,mjk->mik", factor, chain)
        if turn < 4:
            gram = high_dot("mij,mjk->mik", high_dot("mij,mjk->mik", factor, gram), factor)
    chain = chain / norm[:, None, None]
    return high_dot("mij,mjk->mik", chain, moments)


def adamw(current, grad_in, moment_one, moment_two):
    one_new = BETA_ONE * moment_one + (1.0 - BETA_ONE) * grad_in
    two_new = BETA_TWO * moment_two + (1.0 - BETA_TWO) * grad_in * grad_in
    one_hat = one_new / (1.0 - BETA_ONE**STEP)
    two_hat = two_new / (1.0 - BETA_TWO**STEP)
    updated = current * (1.0 - LR_ADAM * DECAY) - LR_ADAM * one_hat / (jnp.sqrt(two_hat) + 1e-08)
    return (one_new, two_new, updated)


def columns_of(values, member, width, axis):
    return lax.dynamic_slice_in_dim(values, member * width, width, axis)


def body(
    history,
    out_grad,
    doc_lengths,
    doc_domain,
    domain_weight,
    attn_weight,
    attn_master,
    attn_moment,
    mlp_weight,
    mlp_master,
    mlp_moment,
    params,
    params_m,
    params_v,
    mix_out,
    mix_out_m,
    mix_out_v,
):
    hist_count, tok_count, model_width = history.shape
    links = Links()
    members = links.members
    member = links.member
    rows = attn_weight.shape[1]
    group = lax.axis_size("dp")
    attn_cols = attn_weight.shape[2] // group
    mlp_cols = mlp_weight.shape[2] // group
    col_blocks = attn_cols // rows
    heads = HEADS // group
    group_tok = group * tok_count
    param_rows = params.shape[0]
    head_scale = 1.0 / math.sqrt(HEAD)

    param_pieces = lax.all_to_all(
        jnp.broadcast_to(params.astype(jnp.bfloat16)[None], (members, param_rows, rows)),
        "fsdp",
        0,
        0,
        tiled=True,
    )
    param_vals_low = jnp.moveaxis(param_pieces, 0, 1).reshape(param_rows, model_width)
    param_vals = param_vals_low.astype(jnp.float32)
    mix_weight = param_vals_low[17:]

    full_up = links.gather_rows(columns_of(mlp_weight[0], member, mlp_cols, 1))
    full_down = links.gather_rows(columns_of(mlp_weight[1], member, mlp_cols, 1))
    attn_shard = columns_of(attn_weight, member, attn_cols, 2)
    attn_shard = jnp.concatenate([attn_shard[at] for at in range(4)], 1)
    full_attn = links.gather_rows(attn_shard)
    full_attn = [full_attn[:, at * attn_cols : (at + 1) * attn_cols] for at in range(4)]

    mixing = lax.optimization_barrier(mix_out.astype(jnp.bfloat16)).astype(jnp.float32)
    _, tok_weight = pack_info(doc_lengths[0], doc_domain[0], domain_weight, tok_count)
    out_cot = out_grad.astype(jnp.float32) * tok_weight[:, None]
    cot_low = out_cot.astype(jnp.bfloat16)
    group_lengths = links.gather_tokens(doc_lengths)
    allowed = jnp.stack(
        [
            pack_info(group_lengths[at], doc_domain[0], domain_weight, tok_count)[0]
            for at in range(group)
        ]
    )
    group_cot = links.gather_tokens(links.to_slots(cot_low))

    last_hist = history[hist_count - 1].astype(jnp.float32)
    inv_rms = lax.rsqrt(jnp.mean(last_hist * last_hist, -1, keepdims=True) + 1e-06)
    unit_rms = last_hist * inv_rms
    unit_low = unit_rms.astype(jnp.bfloat16)
    inner_pre = product_nt(unit_low, mix_weight)
    hidden, gelu_inner = jax.vjp(exact_gelu, inner_pre)
    coeffs = (
        jnp.dot(hidden, mixing[:MIXW], precision=HIGHEST, preferred_element_type=jnp.float32)
        + mixing[MIXW]
    ).reshape(tok_count, 4, hist_count)
    streams = []
    for index in range(4):
        running = coeffs[:, index, 0, None] * history[0].astype(jnp.float32)
        for source in range(1, hist_count):
            running = running + coeffs[:, index, source, None] * history[source].astype(
                jnp.float32
            )
        streams.append(running)
    norm_keep = [None] * 4
    group_normed = [None] * 4
    for index in (3, 2, 0, 1):
        result, normed, inv_std = layer_norm(
            streams[index], param_vals[index], param_vals[4 + index]
        )
        group_normed[index] = links.gather_tokens(links.to_slots(result.astype(jnp.bfloat16)))
        norm_keep[index] = (normed, inv_std)

    up_bias = lax.dynamic_index_in_dim(param_vals, 13 + member, 0)
    up_pre = jnp.dot(group_normed[3], full_up, preferred_element_type=jnp.float32) + up_bias
    act_val, gelu_up = jax.vjp(exact_gelu, up_pre)
    act_low = act_val.astype(jnp.bfloat16)
    down_weight_grad = links.scatter_rows(group_cot, act_low)
    act_grad = jnp.dot(group_cot, full_down, preferred_element_type=jnp.float32)
    up_grad = gelu_up(act_grad)[0].astype(jnp.bfloat16)
    up_weight_grad = links.scatter_rows(group_normed[3], up_grad)
    mlp_in_grad = product_nt(up_grad, full_up)
    in_grads = [None, None, None, links.from_slots(links.scatter_tokens(mlp_in_grad))]
    mlp_part = product_nt(act_low, full_down)

    cot_cols = links.from_slots(group_cot, member * col_blocks, col_blocks)
    context_grad_part = product_nt(cot_cols, full_attn[3])

    cosine, sine_tab = rope_tables(tok_count)

    def split_heads(values):
        return values.reshape(group, tok_count, heads, HEAD)

    context_grad = split_heads(
        links.scatter_columns(
            [
                links.from_slots(context_grad_part, links.partner(at) * col_blocks, col_blocks)
                for at in range(group)
            ]
        ).astype(jnp.bfloat16)
    )

    def bias_piece(row):
        return lax.dynamic_slice(param_vals, (row, member * attn_cols), (1, attn_cols))

    q_pre = jnp.dot(group_normed[0], full_attn[0], preferred_element_type=jnp.float32) + bias_piece(8)
    k_pre = jnp.dot(group_normed[1], full_attn[1], preferred_element_type=jnp.float32) + bias_piece(9)
    value_low = split_heads(
        (
            jnp.dot(group_normed[2], full_attn[2], preferred_element_type=jnp.float32)
            + bias_piece(10)
        ).astype(jnp.bfloat16)
    )
    query_low = rotate(split_heads(q_pre), cosine, sine_tab).astype(jnp.bfloat16)
    key_low = rotate(split_heads(k_pre), cosine, sine_tab).astype(jnp.bfloat16)

    def pair(left_side, right_side):
        return jnp.einsum(
            "bqhd,bkhd->bhqk", left_side, right_side, preferred_element_type=jnp.float32
        )

    def take(weights, right_side):
        return jnp.einsum(
            "bhqk,bkhd->bqhd", weights, right_side, preferred_element_type=jnp.float32
        )

    def give(weights, right_side):
        return jnp.einsum(
            "bhqk,bqhd->bkhd", weights, right_side, preferred_element_type=jnp.float32
        )

    scores = jnp.where(allowed[:, None], pair(query_low, key_low) * head_scale, -1000000000.0)
    top_score = jnp.max(scores, -1, keepdims=True)
    log_total = top_score + jnp.log(jnp.sum(jnp.exp(scores - top_score), -1, keepdims=True))
    probs = jnp.exp(scores - log_total)
    probs_low = probs.astype(jnp.bfloat16)
    context_low = (
        take(probs_low, value_low).reshape(group_tok, attn_cols).astype(jnp.bfloat16)
    )
    context_all = links.gather_columns(context_low)
    pieces = []
    for owner in links.slots():
        place = (owner // col_blocks) ^ member
        place = (place % 2) * 2 + place // 2
        start = place * attn_cols + (owner % col_blocks) * rows
        pieces.append(lax.dynamic_slice_in_dim(context_all, start, rows, 1))
    group_context = jnp.concatenate(pieces, 1)
    out_weight_grad = links.scatter_rows(group_context, cot_cols)

    prob_grad = pair(context_grad, value_low)
    score_grad = (
        probs * (prob_grad - jnp.sum(probs * prob_grad, -1, keepdims=True))
    ).astype(jnp.bfloat16)
    value_grad = give(probs_low, context_grad).reshape(group_tok, attn_cols).astype(jnp.bfloat16)
    query_grad = take(score_grad, key_low) * head_scale
    key_grad = give(score_grad, query_low) * head_scale
    query_back = (
        rotate(query_grad, cosine, -sine_tab).reshape(group_tok, attn_cols).astype(jnp.bfloat16)
    )
    key_back = (
        rotate(key_grad, cosine, -sine_tab).reshape(group_tok, attn_cols).astype(jnp.bfloat16)
    )
    proj_grads = (query_back, key_back, value_grad)
    attn_grads = [None, None, None, out_weight_grad]
    for index in (2, 0, 1):
        attn_grads[index] = links.scatter_rows(group_normed[index], proj_grads[index])
    for index in (2, 0, 1):
        in_grads[index] = links.from_slots(
            links.scatter_tokens(product_nt(proj_grads[index], full_attn[index]))
        )

    mlp_grad = jnp.stack([up_weight_grad, down_weight_grad])
    mlp_mom = MOMENTUM * mlp_moment + mlp_grad
    mlp_cur = orthogonal(links, mlp_mom)
    mlp_new = mlp_master * (1.0 - LR_MUON * DECAY) - LR_MUON * 0.2 * math.sqrt(FF) * mlp_cur
    mlp_copy = links.gather_copies(mlp_new.astype(jnp.bfloat16))

    attn_out = jnp.dot(group_context, full_attn[3], preferred_element_type=jnp.float32)
    out_part = mlp_part
    for at in range(col_blocks):
        place = links.slot_of(member * col_blocks + at) * rows
        piece = lax.dynamic_slice_in_dim(out_part, place, rows, 1)
        piece = piece + attn_out[:, at * rows : (at + 1) * rows]
        out_part = lax.dynamic_update_slice_in_dim(out_part, piece, place, 1)
    layer_out = (
        streams[3]
        + links.from_slots(links.scatter_tokens(out_part))
        + (param_vals[11] + param_vals[12])
    ).astype(jnp.bfloat16)

    stream_grads = []
    gain_list = []
    shift_list = []
    for index in range(4):
        grad_stream, gain_part, shift_part = norm_back(
            in_grads[index], norm_keep[index][0], norm_keep[index][1], param_vals[index]
        )
        stream_grads.append(grad_stream)
        gain_list.append(gain_part)
        shift_list.append(shift_part)
    stream_grads[3] = stream_grads[3] + out_cot
    coef_grad = jnp.stack(
        [
            jnp.stack(
                [
                    jnp.sum(history[source].astype(jnp.float32) * stream_grads[index], -1)
                    for source in range(hist_count)
                ],
                -1,
            )
            for index in range(4)
        ],
        1,
    )
    coef_flat = coef_grad.reshape(tok_count, 4 * hist_count)
    mixing_grad = jnp.concatenate(
        [
            jnp.dot(hidden.T, coef_flat, precision=HIGHEST, preferred_element_type=jnp.float32),
            jnp.sum(coef_flat, 0)[None],
        ],
        0,
    )
    hidden_grad = jnp.dot(
        coef_flat, mixing[:MIXW].T, precision=HIGHEST, preferred_element_type=jnp.float32
    )
    inner_grad = gelu_inner(hidden_grad)[0].astype(jnp.bfloat16)
    mix_weight_grad = product_tn(inner_grad, unit_low)
    unit_grad = jnp.dot(inner_grad, mix_weight, preferred_element_type=jnp.float32)
    last_grad = inv_rms * (unit_grad - unit_rms * jnp.mean(unit_grad * unit_rms, -1, keepdims=True))
    hist_parts = []
    for source in range(hist_count):
        running = coeffs[:, 0, source, None] * stream_grads[0]
        for index in range(1, 4):
            running = running + coeffs[:, index, source, None] * stream_grads[index]
        if source == hist_count - 1:
            running = running + last_grad
        hist_parts.append(running.astype(jnp.bfloat16))
    history_grad = jnp.stack(hist_parts)
    out_bias_grad = jnp.sum(cot_low.astype(jnp.float32), 0)

    def placed(values, width, total):
        return lax.dynamic_update_slice(
            jnp.zeros((total,), jnp.float32),
            jnp.sum(values.astype(jnp.float32), 0),
            (member * width,),
        )

    param_grad = jnp.concatenate(
        [
            jnp.stack(gain_list),
            jnp.stack(shift_list),
            jnp.stack([placed(part, attn_cols, model_width) for part in proj_grads]),
            out_bias_grad[None],
            out_bias_grad[None],
            placed(up_grad, mlp_cols, group * mlp_cols).reshape(-1, model_width),
            mix_weight_grad,
        ],
        0,
    )
    param_pieces_grad = jnp.moveaxis(param_grad.reshape(param_rows, members, rows), 1, 0)
    mix_size = mixing_grad.size
    mix_rows = -(-mix_size // rows)
    mix_flat = jnp.pad(mixing_grad.reshape(-1), (0, mix_rows * rows - mix_size))
    mix_flat = jnp.broadcast_to(mix_flat.reshape(1, mix_rows, rows), (members, mix_rows, rows))
    small = lax.all_to_all(
        jnp.concatenate([param_pieces_grad, mix_flat], 1), "fsdp", 0, 0, tiled=True
    )
    small = links.sum_group(jnp.sum(small, 0))
    param_part = small[:param_rows]
    mixing_grad = small[param_rows:].reshape(-1)[:mix_size].reshape(mixing_grad.shape)

    attn_grad = jnp.stack(attn_grads)
    attn_mom = MOMENTUM * attn_moment + attn_grad
    attn_cur = orthogonal(links, attn_mom)
    attn_new = (
        attn_master * (1.0 - LR_MUON * DECAY) - LR_MUON * 0.2 * math.sqrt(model_width) * attn_cur
    )
    attn_copy = links.gather_copies(attn_new.astype(jnp.bfloat16))
    params_m_new, params_v_new, params_new = adamw(params, param_part, params_m, params_v)
    mix_out_m_new, mix_out_v_new, mix_out_new = adamw(mix_out, mixing_grad, mix_out_m, mix_out_v)
    return (
        layer_out,
        history_grad,
        attn_grad,
        attn_mom,
        attn_new,
        attn_copy,
        mlp_grad,
        mlp_mom,
        mlp_new,
        mlp_copy,
        param_part,
        param_part[11:13],
        params_m_new,
        params_v_new,
        params_new,
        mixing_grad,
        mix_out_m_new,
        mix_out_v_new,
        mix_out_new,
    )


def solution(mesh):
    in_specs = (
        P(None, ("dp", "fsdp"), None),
        P(("dp", "fsdp"), None),
        P(("dp", "fsdp"), None),
        P(("dp", "fsdp"), None),
        P(),
        P(None, "fsdp", None),
        P(None, "fsdp", "dp"),
        P(None, "fsdp", "dp"),
        P(None, "fsdp", None),
        P(None, "fsdp", "dp"),
        P(None, "fsdp", "dp"),
        P(None, "fsdp"),
        P(None, "fsdp"),
        P(None, "fsdp"),
        P(),
        P(),
        P(),
    )
    out_specs = (
        P(("dp", "fsdp"), None),
        P(None, ("dp", "fsdp"), None),
        P(None, "fsdp", "dp"),
        P(None, "fsdp", "dp"),
        P(None, "fsdp", "dp"),
        P(None, "fsdp", None),
        P(None, "fsdp", "dp"),
        P(None, "fsdp", "dp"),
        P(None, "fsdp", "dp"),
        P(None, "fsdp", None),
        P(None, "fsdp"),
        P(None, "fsdp"),
        P(None, "fsdp"),
        P(None, "fsdp"),
        P(None, "fsdp"),
        P(),
        P(),
        P(),
        P(),
    )
    return jax.shard_map(body, mesh=mesh, in_specs=in_specs, out_specs=out_specs, check_vma=False)
```

```python
import functools
import math

import jax
import jax.numpy as jnp
from jax import lax
from jax.experimental import pallas as pl
from jax.experimental.pallas import tpu as pltpu
from jax.sharding import PartitionSpec as P

HEADS = 16
HEAD = 128
FF = 8192
ROT = 32
MIXW = 36
DOCS = 3
NDOM = 22
STEP = 6


NS_A = 3.4445
NS_B = -4.775
NS_C = 2.0315
ROPE_BASE = 10000.0
LR_MUON = 0.1
LR_ADAM = 0.03
DECAY = 0.01
MOMENTUM = 0.95
BETA_ONE = 0.9
BETA_TWO = 0.95
HIGHEST = lax.Precision.HIGHEST


def rope_rows(tok_count):
    half_rot = ROT // 2
    inverse_freq = ROPE_BASE ** (-(2.0 * jnp.arange(half_rot, dtype=jnp.float32)) / ROT)
    angles = jnp.arange(tok_count, dtype=jnp.float32)[:, None] * inverse_freq[None, :]
    cosine, sine_tab = jnp.cos(angles), jnp.sin(angles)
    zero = jnp.zeros_like(sine_tab)
    rest = jnp.zeros((tok_count, HEAD - ROT), jnp.float32)
    return jnp.stack(
        [
            jnp.concatenate([cosine, cosine, rest + 1.0], 1),
            jnp.concatenate([-sine_tab, zero, rest], 1),
            jnp.concatenate([zero, sine_tab, rest], 1),
        ]
    )


def product_nt(left_side, right_side):
    return lax.dot_general(
        left_side, right_side, (((1,), (1,)), ((), ())), preferred_element_type=jnp.float32
    )


def product_tn(left_side, right_side):
    return lax.dot_general(
        left_side, right_side, (((0,), (0,)), ((), ())), preferred_element_type=jnp.float32
    )


def token_weights(lengths, domains, weight_table, tok_count):
    doc_ends = jnp.cumsum(lengths)
    positions = jnp.arange(tok_count, dtype=jnp.int32)
    doc_of = jnp.sum((positions[:, None] >= doc_ends[None, :]).astype(jnp.int32), 1)
    domain = jnp.sum(
        jnp.where(
            doc_of[:, None] == jnp.arange(DOCS, dtype=jnp.int32)[None, :], domains[None, :], 0
        ),
        1,
    )
    weight = jnp.sum(
        jnp.where(
            domain[:, None] == jnp.arange(NDOM, dtype=jnp.int32)[None, :], weight_table[None, :], 0
        ),
        1,
    )
    return weight.astype(jnp.float32) / 256.0


SMALL_COST = pl.CostEstimate(flops=1, bytes_accessed=1, transcendentals=0)
VMEM_BYTES = 56 * 1024 * 1024


def kernel_params():
    return pltpu.CompilerParams(vmem_limit_bytes=VMEM_BYTES)


def whole_block(shape):
    return pl.BlockSpec(shape, lambda *_: (0,) * len(shape))


def shaped(shape, dtype):
    return jax.ShapeDtypeStruct(shape, dtype)


def gelu_pair(values):
    share = 0.5 * (1.0 + lax.erf(values * math.sqrt(0.5)))
    bell = jnp.exp(-0.5 * values * values) * (1.0 / math.sqrt(2.0 * math.pi))
    return (values * share, share + values * bell)


def dot_nn(left_side, right_side):
    return jnp.dot(left_side, right_side, preferred_element_type=jnp.float32)


def exact_dot(left_side, right_side, dims=((1,), (0,))):
    return lax.dot_general(
        left_side,
        right_side,
        (dims, ((), ())),
        precision=HIGHEST,
        preferred_element_type=jnp.float32,
    )


def copy_kernel(order_ref, *refs, counts):
    sources, targets = refs[: -len(counts)], refs[-len(counts) :]
    at = 0
    for target, count in zip(targets, counts):
        height = target.shape[0] // count
        for place in range(count):
            target[place * height : (place + 1) * height, :] = sources[at][...]
            at += 1


def take_blocks(groups, order, width):
    count = order.shape[0]
    if width % 128:
        return [
            jnp.concatenate(
                [
                    jnp.concatenate(
                        [
                            lax.dynamic_slice_in_dim(values, order[at] * width, width, 1)
                            for at in range(count)
                        ],
                        1,
                    )
                    for values in arrays
                ],
                0,
            )
            for arrays in groups
        ]
    flat = [values for arrays in groups for values in arrays]
    heights = [len(arrays) * arrays[0].shape[0] for arrays in groups]
    return pl.pallas_call(
        functools.partial(copy_kernel, counts=[len(arrays) for arrays in groups]),
        grid_spec=pltpu.PrefetchScalarGridSpec(
            num_scalar_prefetch=1,
            grid=(count,),
            in_specs=[
                pl.BlockSpec((values.shape[0], width), lambda at, order_ref: (0, order_ref[at]))
                for values in flat
            ],
            out_specs=[
                pl.BlockSpec((height, width), lambda at, order_ref: (0, at)) for height in heights
            ],
        ),
        out_shape=[
            shaped((height, count * width), arrays[0].dtype)
            for height, arrays in zip(heights, groups)
        ],
        compiler_params=kernel_params(),
        cost_estimate=SMALL_COST,
        name="take_blocks",
    )(order, *flat)


def rows_kernel(order_ref, left_ref, even_ref, odd_ref, near_ref, far_ref):
    width = even_ref.shape[0]
    half = near_ref.shape[0]
    for at, right_ref in enumerate((even_ref, odd_ref)):
        span = slice(at * width, (at + 1) * width)
        result = product_nt(left_ref[...], right_ref[...])
        near_ref[:, span] = result[:half].astype(near_ref.dtype)
        far_ref[:, span] = result[half:].astype(far_ref.dtype)


def product_rows(left_side, right_side, order, width, far_type):
    tokens, depth = left_side.shape
    half = tokens // 2
    count = order.shape[0]
    if width % 128:
        ((result,),) = [take_blocks([[product_nt(left_side, right_side)]], order, width)]
        return (result[:half], result[half:].astype(far_type))
    out_block = pl.BlockSpec((half, 2 * width), lambda at, order_ref: (0, at))
    return pl.pallas_call(
        rows_kernel,
        grid_spec=pltpu.PrefetchScalarGridSpec(
            num_scalar_prefetch=1,
            grid=(count // 2,),
            in_specs=[
                pl.BlockSpec((tokens, depth), lambda at, order_ref: (0, 0)),
                pl.BlockSpec((width, depth), lambda at, order_ref: (order_ref[2 * at], 0)),
                pl.BlockSpec((width, depth), lambda at, order_ref: (order_ref[2 * at + 1], 0)),
            ],
            out_specs=[out_block, out_block],
        ),
        out_shape=[
            shaped((half, count * width), jnp.float32),
            shaped((half, count * width), far_type),
        ],
        compiler_params=kernel_params(),
        cost_estimate=SMALL_COST,
        name="product_rows",
    )(order, left_side, right_side, right_side)


def grad_kernel(left_refs, right_refs, extra_refs, out_ref):
    start = 0
    for left_ref, right_ref in zip(left_refs, right_refs):
        span = slice(start, start + right_ref.shape[1])
        start = span.stop
        result = product_tn(left_ref[...], right_ref[...])
        if extra_refs:
            result = result + extra_refs[0][:, span].astype(jnp.float32)
        out_ref[:, span] = result.astype(out_ref.dtype)


def half_product(lefts, rights, part, extra=None):
    tokens, width = lefts[0].shape
    columns = rights[0].shape[1]
    tile = 512
    col_tile = columns if len(rights) > 1 else 512
    steps = width // 2 // tile
    out_block = pl.BlockSpec((tile, len(rights) * col_tile), lambda at, to: (at, to))
    extras = [] if extra is None else [extra]
    return pl.pallas_call(
        grad_kernel,
        grid=(steps, columns // col_tile),
        in_specs=[
            [pl.BlockSpec((tokens, tile), lambda at, to: (0, part * steps + at))] * len(lefts),
            [pl.BlockSpec((tokens, col_tile), lambda at, to: (0, to))] * len(rights),
            [out_block] * len(extras),
        ],
        out_specs=out_block,
        out_shape=shaped((width // 2, len(rights) * columns), jnp.bfloat16),
        compiler_params=kernel_params(),
        cost_estimate=SMALL_COST,
        name="half_product",
    )(lefts, rights, extras)


MIX_STEP = 64
MIX_ROWS = 16


def mix_forward_kernel(hist_ref, weight_ref, mixing_ref, norm_ref, *outs):
    normed_refs = outs[:4]
    kept_ref, coef_ref, inner_ref, scale_ref, stream_ref = outs[4:]
    hist_count = hist_ref.shape[0]
    last = hist_ref[hist_count - 1].astype(jnp.float32)
    inv_rms = lax.rsqrt(jnp.mean(last * last, -1, keepdims=True) + 1e-06)
    inner = product_nt((last * inv_rms).astype(jnp.bfloat16), weight_ref[...])
    inner_ref[...] = inner
    hidden, _ = gelu_pair(inner)
    coef_ref[...] = exact_dot(hidden, mixing_ref[:MIXW]) + mixing_ref[MIXW:]

    def rows_step(step, carry):
        rows = pl.ds(pl.multiple_of(step * MIX_ROWS, MIX_ROWS), MIX_ROWS)
        coef = coef_ref[rows, :]
        for index in range(4):
            running = None
            for source in range(hist_count):
                at = index * hist_count + source
                term = coef[:, at : at + 1] * hist_ref[source, rows, :].astype(jnp.float32)
                running = term if running is None else running + term
            if index == 3:
                stream_ref[rows, :] = running
            centred = running - jnp.mean(running, -1, keepdims=True)
            inv_std = lax.rsqrt(jnp.mean(centred * centred, -1, keepdims=True) + 1e-05)
            normed = centred * inv_std
            kept_ref[index, rows, :] = normed
            scale_ref[rows, index : index + 1] = inv_std
            result = normed * norm_ref[index : index + 1] + norm_ref[4 + index : 5 + index]
            normed_refs[index][rows, :] = result.astype(jnp.bfloat16)
        return carry

    lax.fori_loop(0, MIX_STEP // MIX_ROWS, rows_step, 0)


def mix_forward(history, mix_weight, mixing, norm_rows):
    hist_count, tok_count, width = history.shape
    token_block = pl.BlockSpec((MIX_STEP, width), lambda at: (at, 0))
    narrow = pl.BlockSpec((MIX_STEP, MIXW), lambda at: (at, 0))
    return pl.pallas_call(
        mix_forward_kernel,
        grid=(tok_count // MIX_STEP,),
        in_specs=[
            pl.BlockSpec((hist_count, MIX_STEP, width), lambda at: (0, at, 0)),
            whole_block(mix_weight.shape),
            whole_block(mixing.shape),
            whole_block(norm_rows.shape),
        ],
        out_specs=[token_block] * 4
        + [
            pl.BlockSpec((4, MIX_STEP, width), lambda at: (0, at, 0)),
            narrow,
            narrow,
            pl.BlockSpec((MIX_STEP, 4), lambda at: (at, 0)),
            token_block,
        ],
        out_shape=[shaped((tok_count, width), jnp.bfloat16)] * 4
        + [
            shaped((4, tok_count, width), jnp.float32),
            shaped((tok_count, MIXW), jnp.float32),
            shaped((tok_count, MIXW), jnp.float32),
            shaped((tok_count, 4), jnp.float32),
            shaped((tok_count, width), jnp.float32),
        ],
        compiler_params=kernel_params(),
        cost_estimate=SMALL_COST,
        name="mix_forward",
    )(history, mix_weight, mixing, norm_rows)


def mix_backward_kernel(
    hist_ref,
    cot_ref,
    tok_ref,
    back_refs,
    kept_ref,
    coef_ref,
    inner_ref,
    scale_ref,
    weight_ref,
    mixing_ref,
    norm_ref,
    out_ref,
    sums_ref,
    weight_grad_ref,
    mixing_grad_ref,
    stream_ref,
    last_ref,
    coef_grad_ref,
):
    hist_count = hist_ref.shape[0]

    @pl.when(pl.program_id(0) == 0)
    def _():
        sums_ref[...] = jnp.zeros_like(sums_ref)
        weight_grad_ref[...] = jnp.zeros_like(weight_grad_ref)
        mixing_grad_ref[...] = jnp.zeros_like(mixing_grad_ref)

    def rows_step(step, carry):
        rows = pl.ds(pl.multiple_of(step * MIX_ROWS, MIX_ROWS), MIX_ROWS)
        coef = coef_ref[rows, :]
        out_cot = cot_ref[rows, :].astype(jnp.float32) * tok_ref[rows, :]
        cot_low = out_cot.astype(jnp.bfloat16).astype(jnp.float32)
        sums_ref[8:9] += jnp.sum(cot_low, 0, keepdims=True)
        for index in range(4):
            back = back_refs[index][rows, :]
            normed = kept_ref[index, rows, :]
            sums_ref[index : index + 1] += jnp.sum(back * normed, 0, keepdims=True)
            sums_ref[4 + index : 5 + index] += jnp.sum(back, 0, keepdims=True)
            scaled = back * norm_ref[index : index + 1]
            grad = scaled - jnp.mean(scaled, -1, keepdims=True)
            grad = grad - normed * jnp.mean(scaled * normed, -1, keepdims=True)
            grad = grad * scale_ref[rows, index : index + 1]
            if index == 3:
                grad = grad + out_cot
            stream_ref[index] = grad
        for source in range(hist_count):
            values = hist_ref[source, rows, :].astype(jnp.float32)
            running = None
            for index in range(4):
                at = index * hist_count + source
                grad = stream_ref[index]
                coef_grad_ref[rows, at : at + 1] = jnp.sum(values * grad, -1, keepdims=True)
                term = coef[:, at : at + 1] * grad
                running = term if running is None else running + term
            if source == hist_count - 1:
                last_ref[rows, :] = running
            else:
                out_ref[source, rows, :] = running.astype(jnp.bfloat16)
        return carry

    lax.fori_loop(0, MIX_STEP // MIX_ROWS, rows_step, 0)
    coef_grad = coef_grad_ref[...]
    hidden, slope = gelu_pair(inner_ref[...])
    mixing_grad_ref[:MIXW] += exact_dot(hidden, coef_grad, ((0,), (0,)))
    mixing_grad_ref[MIXW:] += jnp.sum(coef_grad, 0, keepdims=True)
    hidden_grad = exact_dot(coef_grad, mixing_ref[:MIXW], ((1,), (1,)))
    inner_grad = (hidden_grad * slope).astype(jnp.bfloat16)
    last = hist_ref[hist_count - 1].astype(jnp.float32)
    inv_rms = lax.rsqrt(jnp.mean(last * last, -1, keepdims=True) + 1e-06)
    unit = last * inv_rms
    weight_grad_ref[...] += product_tn(inner_grad, unit.astype(jnp.bfloat16))
    unit_grad = dot_nn(inner_grad, weight_ref[...])
    last_grad = inv_rms * (unit_grad - unit * jnp.mean(unit_grad * unit, -1, keepdims=True))
    out_ref[hist_count - 1] = (last_ref[...] + last_grad).astype(jnp.bfloat16)


def mix_backward(
    history, cot, tok_weight, backs, kept, coef, inner, scale, mix_weight, mixing, norm_rows
):
    hist_count, tok_count, width = history.shape
    token_block = pl.BlockSpec((MIX_STEP, width), lambda at: (at, 0))
    narrow = pl.BlockSpec((MIX_STEP, MIXW), lambda at: (at, 0))
    hist_block = pl.BlockSpec((hist_count, MIX_STEP, width), lambda at: (0, at, 0))
    return pl.pallas_call(
        mix_backward_kernel,
        grid=(tok_count // MIX_STEP,),
        in_specs=[
            hist_block,
            token_block,
            pl.BlockSpec((MIX_STEP, 1), lambda at: (at, 0)),
            [token_block] * 4,
            pl.BlockSpec((4, MIX_STEP, width), lambda at: (0, at, 0)),
            narrow,
            narrow,
            pl.BlockSpec((MIX_STEP, 4), lambda at: (at, 0)),
            whole_block(mix_weight.shape),
            whole_block(mixing.shape),
            whole_block(norm_rows.shape),
        ],
        out_specs=[
            hist_block,
            whole_block((16, width)),
            whole_block(mix_weight.shape),
            whole_block(mixing.shape),
        ],
        out_shape=[
            shaped(history.shape, jnp.bfloat16),
            shaped((16, width), jnp.float32),
            shaped(mix_weight.shape, jnp.float32),
            shaped(mixing.shape, jnp.float32),
        ],
        scratch_shapes=[
            pltpu.VMEM((4, MIX_ROWS, width), jnp.float32),
            pltpu.VMEM((MIX_STEP, width), jnp.float32),
            pltpu.VMEM((MIX_STEP, MIXW), jnp.float32),
        ],
        compiler_params=kernel_params(),
        cost_estimate=SMALL_COST,
        name="mix_backward",
    )(history, cot, tok_weight, backs, kept, coef, inner, scale, mix_weight, mixing, norm_rows)


def mlp_up_kernel(normed_ref, up_ref, bias_ref, act_ref, slope_ref):
    tokens = normed_ref.shape[0]
    part = tokens // 4
    for at in range(4):
        rows = pl.ds(at * part, part)
        act_val, slope = gelu_pair(dot_nn(normed_ref[rows, :], up_ref[...]) + bias_ref[...])
        act_ref[rows, :] = act_val.astype(jnp.bfloat16)
        slope_ref[rows, :] = slope


def mlp_up(normed, up_weight, bias):
    tokens, width = normed.shape
    hidden = up_weight.shape[1]
    tile = 256
    act_block = pl.BlockSpec((tokens, tile), lambda at: (0, at))
    return pl.pallas_call(
        mlp_up_kernel,
        grid=(hidden // tile,),
        in_specs=[
            whole_block(normed.shape),
            pl.BlockSpec((width, tile), lambda at: (0, at)),
            pl.BlockSpec((1, tile), lambda at: (0, at)),
        ],
        out_specs=[act_block, act_block],
        out_shape=[shaped((tokens, hidden), jnp.bfloat16), shaped((tokens, hidden), jnp.float32)],
        compiler_params=kernel_params(),
        cost_estimate=SMALL_COST,
        name="mlp_up",
    )(normed, up_weight, bias)


def mlp_back_kernel(cot_ref, down_ref, slope_ref, grad_ref, sum_ref):
    tokens = cot_ref.shape[0]
    part = tokens // 4
    total = None
    for at in range(4):
        rows = pl.ds(at * part, part)
        act_grad = dot_nn(cot_ref[rows, :], down_ref[...])
        up_grad = (act_grad * slope_ref[rows, :]).astype(jnp.bfloat16)
        grad_ref[rows, :] = up_grad
        term = jnp.sum(up_grad.astype(jnp.float32), 0, keepdims=True)
        total = term if total is None else total + term
    sum_ref[...] = total


def mlp_back(cot, down_weight, slope):
    tokens, width = cot.shape
    hidden = down_weight.shape[1]
    tile = 256
    act_block = pl.BlockSpec((tokens, tile), lambda at: (0, at))
    row_block = pl.BlockSpec((1, tile), lambda at: (0, at))
    return pl.pallas_call(
        mlp_back_kernel,
        grid=(hidden // tile,),
        in_specs=[
            whole_block(cot.shape),
            pl.BlockSpec((width, tile), lambda at: (0, at)),
            act_block,
        ],
        out_specs=[act_block, row_block],
        out_shape=[shaped((tokens, hidden), jnp.bfloat16), shaped((1, hidden), jnp.float32)],
        compiler_params=kernel_params(),
        cost_estimate=SMALL_COST,
        name="mlp_back",
    )(cot, down_weight, slope)


def attention_kernel(
    ends_ref, normed_refs, weight_refs, bias_ref, rope_ref, cot_ref, ctx_ref, grad_refs, sum_ref
):
    tokens, width = ctx_ref.shape
    at = pl.program_id(0)
    head_scale = 1.0 / math.sqrt(HEAD)
    half_rot = ROT // 2
    cosine, rise, fall = rope_ref[0], rope_ref[1], rope_ref[2]

    def turned(values):
        return pltpu.roll(values, HEAD - half_rot, 1) * rise + pltpu.roll(values, half_rot, 1) * fall

    def doc_of(positions):
        found = jnp.zeros(positions.shape, jnp.int32)
        for doc in range(DOCS):
            found = found + (positions >= ends_ref[at, doc]).astype(jnp.int32)
        return found

    column = lax.broadcasted_iota(jnp.int32, (tokens, tokens), 1)
    row = lax.broadcasted_iota(jnp.int32, (tokens, tokens), 0)
    allowed = (doc_of(row) == doc_of(column)) & (row >= column)
    query_all = dot_nn(normed_refs[0][...], weight_refs[0][...]) + bias_ref[0:1]
    key_all = dot_nn(normed_refs[1][...], weight_refs[1][...]) + bias_ref[1:2]
    value_all = (dot_nn(normed_refs[2][...], weight_refs[2][...]) + bias_ref[2:3]).astype(
        jnp.bfloat16
    )

    @pl.when(at == 0)
    def _():
        sum_ref[...] = jnp.zeros_like(sum_ref)

    for head in range(width // HEAD):
        span = slice(head * HEAD, (head + 1) * HEAD)
        query = query_all[:, span]
        key = key_all[:, span]
        value = value_all[:, span]
        query = (query * cosine + turned(query)).astype(jnp.bfloat16)
        key = (key * cosine + turned(key)).astype(jnp.bfloat16)
        cot = cot_ref[:, span]
        scores = jnp.where(allowed, product_nt(query, key) * head_scale, -1000000000.0)
        weights = jnp.exp(scores - jnp.max(scores, -1, keepdims=True))
        weights = weights / jnp.sum(weights, -1, keepdims=True)
        weights_low = weights.astype(jnp.bfloat16)
        ctx_ref[:, span] = dot_nn(weights_low, value).astype(jnp.bfloat16)
        prob_grad = product_nt(cot, value)
        score_grad = (
            weights * (prob_grad - jnp.sum(weights * prob_grad, -1, keepdims=True))
        ).astype(jnp.bfloat16)
        query_grad = dot_nn(score_grad, key) * head_scale
        key_grad = product_tn(score_grad, query) * head_scale
        value_grad = product_tn(weights_low, cot)
        grads = (
            query_grad * cosine - turned(query_grad),
            key_grad * cosine - turned(key_grad),
            value_grad,
        )
        for index in range(3):
            grad_low = grads[index].astype(jnp.bfloat16)
            grad_refs[index][:, span] = grad_low
            sum_ref[index : index + 1, span] += jnp.sum(
                grad_low.astype(jnp.float32), 0, keepdims=True
            )


def attention_inner(ends, normed, weights, bias, rope, cot):
    group, _ = ends.shape
    tokens = normed[0].shape[0] // group
    model_width, width = weights[0].shape
    normed_block = pl.BlockSpec((tokens, model_width), lambda at: (at, 0))
    head_block = pl.BlockSpec((tokens, width), lambda at: (at, 0))
    out = shaped((group * tokens, width), jnp.bfloat16)
    return pl.pallas_call(
        attention_kernel,
        grid=(group,),
        in_specs=[
            pl.BlockSpec(memory_space=pltpu.SMEM),
            [normed_block] * 3,
            [whole_block(weights[0].shape)] * 3,
            whole_block(bias.shape),
            whole_block(rope.shape),
            head_block,
        ],
        out_specs=[head_block, [head_block] * 3, whole_block((8, width))],
        out_shape=[out, [out] * 3, shaped((8, width), jnp.float32)],
        compiler_params=kernel_params(),
        cost_estimate=SMALL_COST,
        name="attention_inner",
    )(ends, normed, weights, bias, rope, cot)


def finish_kernel(part_refs, moment_ref, grad_ref, mom_ref, gram_ref):
    @pl.when(pl.program_id(0) == 0)
    def _():
        gram_ref[...] = jnp.zeros_like(gram_ref)

    for at, refs in enumerate(part_refs):
        total = refs[0][...].astype(jnp.float32)
        for ref in refs[1:]:
            total = total + ref[...].astype(jnp.float32)
        grad_ref[at] = total
        mom_new = MOMENTUM * moment_ref[at] + total
        mom_ref[at] = mom_new
        gram_ref[at] += exact_dot(mom_new, mom_new, ((1,), (1,)))


def finish_gradient(parts, moment):
    count, rows, width = moment.shape
    tile = 512
    part_block = pl.BlockSpec((rows, tile), lambda at: (0, at))
    stack_block = pl.BlockSpec((count, rows, tile), lambda at: (0, 0, at))
    return pl.pallas_call(
        finish_kernel,
        grid=(width // tile,),
        in_specs=[[[part_block] * len(own) for own in parts], stack_block],
        out_specs=[stack_block, stack_block, whole_block((count, rows, rows))],
        out_shape=[shaped(moment.shape, jnp.float32)] * 2
        + [shaped((count, rows, rows), jnp.float32)],
        compiler_params=kernel_params(),
        cost_estimate=SMALL_COST,
        name="finish_gradient",
    )(parts, moment)


def newton_kernel(gram_ref, mom_ref, master_ref, new_ref, copy_ref, *, rate):
    count, rows, _ = gram_ref.shape
    at_row = lax.broadcasted_iota(jnp.int32, (rows, rows), 0)
    eye = (at_row == lax.broadcasted_iota(jnp.int32, (rows, rows), 1)).astype(jnp.float32)
    chains = [None] * count
    grams = []
    norms = []
    for at in range(count):
        gram = gram_ref[at]
        trace = jnp.sum(jnp.sum(gram * eye, 1, keepdims=True), 0, keepdims=True)
        norm = jnp.sqrt(trace) + 1e-07
        norms.append(norm)
        grams.append(gram / (norm * norm))
    for turn in range(5):
        squares = [exact_dot(gram, gram) for gram in grams]
        factors = [
            NS_A * eye + NS_B * gram + NS_C * square for gram, square in zip(grams, squares)
        ]
        if turn == 0:
            chains = factors
        else:
            chains = [exact_dot(factor, chain) for factor, chain in zip(factors, chains)]
        if turn < 4:
            halves = [exact_dot(factor, gram) for factor, gram in zip(factors, grams)]
            grams = [exact_dot(half, factor) for half, factor in zip(halves, factors)]
    for at in range(count):
        turned = exact_dot(chains[at] / norms[at], mom_ref[at])
        fresh = master_ref[at] * (1.0 - LR_MUON * DECAY) - rate * turned
        new_ref[at] = fresh
        copy_ref[at] = fresh.astype(jnp.bfloat16)


def newton_update(gram, mom, master, rate):
    count, rows, width = mom.shape
    step = 2
    stack_block = pl.BlockSpec((step, rows, width), lambda at: (at, 0, 0))
    return pl.pallas_call(
        functools.partial(newton_kernel, rate=rate),
        grid=(count // step,),
        in_specs=[
            pl.BlockSpec((step, rows, rows), lambda at: (at, 0, 0)),
            stack_block,
            stack_block,
        ],
        out_specs=[stack_block, stack_block],
        out_shape=[shaped(mom.shape, jnp.float32), shaped(mom.shape, jnp.bfloat16)],
        compiler_params=kernel_params(),
        cost_estimate=SMALL_COST,
        name="newton_update",
    )(gram, mom, master)


class Links:
    def __init__(self):
        self.members = lax.axis_size("fsdp")
        self.depth = self.members // 2
        place = lax.axis_index("fsdp")
        self.z_at = place // 2
        self.x_at = place % 2
        self.member = lax.axis_index("dp")

    def swap_core(self, values):
        return lax.ppermute(values, "dp", [(at, at ^ 1) for at in range(4)])

    def swap_y(self, values):
        return lax.ppermute(values, "dp", [(at, at ^ 2) for at in range(4)])

    def swap_x(self, values):
        return lax.ppermute(values, "fsdp", [(at, at ^ 1) for at in range(self.members)])

    def swap_z(self, values, turn):
        pairs = [(at, at ^ (2 * turn)) for at in range(self.members)]
        return lax.ppermute(values, "fsdp", pairs)

    def slots(self):
        return [
            (self.z_at ^ turn) * 2 + (self.x_at ^ side)
            for side in range(2)
            for turn in range(self.depth)
        ]

    def slot_of(self, owner):
        return ((owner % 2) ^ self.x_at) * self.depth + ((owner // 2) ^ self.z_at)

    def slots_of(self, first, count):
        return jnp.stack([self.slot_of(first + at) for at in range(count)]).astype(jnp.int32)

    def hop(self, line):
        rise, fall = line
        hops = len(rise)
        up_pairs = [(at, at + 2) for at in range(2 * hops - 2, self.members - 2)]
        down_pairs = [(at + 2, at) for at in range(0, self.members - 2 * hops)]
        return (
            rise + [lax.ppermute(rise[-1], "fsdp", up_pairs)],
            fall + [lax.ppermute(fall[-1], "fsdp", down_pairs)],
        )

    def near(self, line, turn):
        rise, fall = line
        found = {}
        for place in range(self.depth):
            found.setdefault((place ^ turn) - place, []).append(place)
        result = None
        for distance, places in found.items():
            values = fall[distance] if distance >= 0 else rise[-distance]
            if result is None:
                result = values
                continue
            here = self.z_at == places[0]
            for place in places[1:]:
                here = here | (self.z_at == place)
            result = jnp.where(here, values, result)
        return result

    def partner(self, at):
        return self.member ^ ((at % 2) * 2 + at // 2)

    def sum_group(self, values):
        values = values + self.swap_core(values)
        return values + self.swap_y(values)

    def sum_stack(self, values):
        values = values + self.swap_core(values)
        half = values.shape[0] // 2
        odd_core = self.member % 2
        own = lax.dynamic_slice_in_dim(values, odd_core * half, half, 0)
        own = own + self.swap_y(own)
        other = self.swap_core(own)
        first = jnp.where(odd_core == 1, other, own)
        return jnp.concatenate([first, jnp.where(odd_core == 1, own, other)], 0)

    def gather_copies(self, values, across):
        other = self.swap_core(values)
        other_across = self.swap_core(across)
        odd_core = self.member % 2 == 1
        high_y = self.member >= 2
        near = [jnp.where(odd_core, other, values), jnp.where(odd_core, values, other)]
        far = [
            jnp.where(odd_core, other_across, across),
            jnp.where(odd_core, across, other_across),
        ]
        low_pair = [jnp.where(high_y, b, a) for a, b in zip(near, far)]
        high_pair = [jnp.where(high_y, a, b) for a, b in zip(near, far)]
        return jnp.concatenate(low_pair + high_pair, -1)


def turn_y(values):
    count = values.shape[0] // 4
    blocks = [values[at * count : (at + 1) * count] for at in (1, 0, 3, 2)]
    return jnp.concatenate(blocks, 0)


def turn_core(values):
    half = values.shape[0] // 2
    return jnp.concatenate([values[half:], values[:half]], 0)


def cut(values, counts):
    parts = []
    start = 0
    for count in counts:
        parts.append(values[start : start + count])
        start += count
    return parts


def low(values):
    return values.astype(jnp.bfloat16)


def wide(values):
    return values.astype(jnp.float32)


def adamw(current, grad_in, moment_one, moment_two):
    one_new = BETA_ONE * moment_one + (1.0 - BETA_ONE) * grad_in
    two_new = BETA_TWO * moment_two + (1.0 - BETA_TWO) * grad_in * grad_in
    one_hat = one_new / (1.0 - BETA_ONE**STEP)
    two_hat = two_new / (1.0 - BETA_TWO**STEP)
    updated = current * (1.0 - LR_ADAM * DECAY) - LR_ADAM * one_hat / (jnp.sqrt(two_hat) + 1e-08)
    return (one_new, two_new, updated)


def columns_of(values, member, width, axis):
    return lax.dynamic_slice_in_dim(values, member * width, width, axis)


def fence(*values):
    return lax.optimization_barrier(values)


def body(
    history,
    out_grad,
    doc_lengths,
    doc_domain,
    domain_weight,
    attn_weight,
    attn_master,
    attn_moment,
    mlp_weight,
    mlp_master,
    mlp_moment,
    params,
    params_m,
    params_v,
    mix_out,
    mix_out_m,
    mix_out_v,
):
    hist_count, tok_count, model_width = history.shape
    links = Links()
    members, depth, member = links.members, links.depth, links.member
    rows = attn_weight.shape[1]
    group = lax.axis_size("dp")
    attn_cols = attn_weight.shape[2] // group
    mlp_cols = mlp_weight.shape[2] // group
    col_blocks = attn_cols // rows
    group_tok = group * tok_count
    near_tok = group_tok // 2
    half_width = model_width // 2
    param_rows = params.shape[0]

    slots = jnp.stack(links.slots()).astype(jnp.int32)
    plain = links.slots_of(0, members)

    def scatter_z(summed, turns):
        return [links.swap_z(summed[turn * rows : (turn + 1) * rows], turn) for turn in turns]

    def spread(left_side, right_side):
        return product_rows(left_side, right_side, plain, rows, jnp.bfloat16)

    up_own = columns_of(mlp_weight[0], member, mlp_cols, 1)
    param_pieces = lax.all_to_all(
        jnp.broadcast_to(low(params)[None], (members, param_rows, rows)), "fsdp", 0, 0, tiled=True
    )
    up_line = links.hop(([up_own], [up_own]))
    far_up = links.swap_x(up_own)
    param_low = jnp.moveaxis(param_pieces, 0, 1).reshape(param_rows, model_width)
    tok_weight = token_weights(doc_lengths[0], doc_domain[0], domain_weight, tok_count)
    (cot_own,) = take_blocks([[low(wide(out_grad) * tok_weight[:, None])]], slots, rows)
    near_lengths = jnp.concatenate([doc_lengths, links.swap_y(doc_lengths)], 0)
    group_lengths = jnp.concatenate([near_lengths, links.swap_core(near_lengths)], 0)
    attn_own = columns_of(attn_weight, member, attn_cols, 2)
    attn_own = jnp.concatenate([attn_own[at] for at in range(4)], 1)
    mixing = wide(lax.optimization_barrier(low(mix_out)))
    up_line, far_up, attn_own, param_low, group_lengths, cot_own, mixing = fence(
        up_line, far_up, attn_own, param_low, group_lengths, cot_own, mixing
    )

    for _ in range(2, depth - 1):
        up_line = links.hop(up_line)
    far_attn = links.swap_x(attn_own)
    cot_near = jnp.concatenate([cot_own, links.swap_y(cot_own)], 0)
    *normed_own, kept, coef, inner, scale, stream_three = mix_forward(
        history, param_low[17:], mixing, wide(param_low[:8])
    )
    normed_own = take_blocks(
        [[normed_own[3], normed_own[2]], [normed_own[0], normed_own[1]]], slots, rows
    )
    down_own = columns_of(mlp_weight[1], member, mlp_cols, 1)
    (
        up_line, far_attn, attn_own, param_low, cot_near, normed_own, kept, coef, inner, scale,
        stream_three, down_own,
    ) = fence(
        up_line, far_attn, attn_own, param_low, cot_near, normed_own, kept, coef, inner, scale,
        stream_three, down_own,
    )
    param_vals = wide(param_low)

    up_line = links.hop(up_line)
    down_line = links.hop(([down_own], [down_own]))
    far_second = links.swap_x(jnp.concatenate([down_own, links.near(up_line, 1)], 0))
    first_y = links.swap_y(normed_own[0])
    cot_core = links.swap_core(cot_near)
    up_line, down_line, far_second, first_y, cot_core, cot_near, normed_own = fence(
        up_line, down_line, far_second, first_y, cot_core, cot_near, normed_own
    )
    far_down, far_up_one = cut(far_second, (rows, rows))

    for _ in range(2, depth):
        down_line = links.hop(down_line)
    up_near = [links.near(up_line, turn) for turn in range(depth)]
    far_third = links.swap_x(jnp.concatenate(up_near[2:], 0))
    first_core = links.swap_core(normed_own[0])
    first_far = links.swap_core(first_y)
    last_y = links.swap_y(normed_own[1])
    group_cot = jnp.concatenate([cot_near, cot_core], 0)
    attn_pair = jnp.concatenate([attn_own, far_attn], 0)
    down_line, far_third, first_core, first_far, last_y, attn_pair, up_near, group_cot = fence(
        down_line, far_third, first_core, first_far, last_y, attn_pair, up_near, group_cot
    )

    attn_line = links.hop(([attn_pair], [attn_pair]))
    down_near = [links.near(down_line, turn) for turn in range(depth)]
    far_fourth = links.swap_x(jnp.concatenate(down_near[1 : depth - 1], 0))
    first_parts = (normed_own[0], first_y, first_core, first_far)
    group_normed = [None] * 4
    group_normed[3] = jnp.concatenate([values[:tok_count] for values in first_parts], 0)
    full_up = jnp.concatenate(up_near + [far_up, far_up_one, far_third], 0)
    up_bias = lax.dynamic_index_in_dim(param_vals, 13 + member, 0)
    act_low, slope = mlp_up(group_normed[3], full_up, up_bias)
    down_sent = half_product([group_cot], [act_low], 1)
    attn_line, far_fourth, act_low, slope, down_sent, down_near, full_up = fence(
        attn_line, far_fourth, act_low, slope, down_sent, down_near, full_up
    )

    for _ in range(2, depth - 1):
        attn_line = links.hop(attn_line)
    far_last = links.swap_x(down_near[depth - 1])
    down_first = links.swap_x(down_sent[:rows])
    last_core = links.swap_core(normed_own[1])
    last_far = links.swap_core(last_y)
    group_normed[2] = jnp.concatenate([values[tok_count:] for values in first_parts], 0)
    attn_line, far_last, down_first, down_sent, last_core, last_far, group_normed = fence(
        attn_line, far_last, down_first, down_sent, last_core, last_far, group_normed
    )

    attn_line = links.hop(attn_line)
    down_rest = links.swap_x(down_sent[rows:])
    full_down = jnp.concatenate(down_near + [far_down, far_fourth, far_last], 0)
    up_grad, up_sum = mlp_back(group_cot, full_down, slope)
    up_sent = half_product([group_normed[3]], [up_grad], 1)
    last_parts = (normed_own[1], last_y, last_core, last_far)
    group_normed[0] = jnp.concatenate([values[:tok_count] for values in last_parts], 0)
    group_normed[1] = jnp.concatenate([values[tok_count:] for values in last_parts], 0)
    (cot_cols,) = take_blocks([[group_cot]], links.slots_of(member * col_blocks, col_blocks), rows)
    attn_near = [links.near(attn_line, turn) for turn in range(depth)]
    half_depth = depth // 2
    up_sent = cut(up_sent, (half_depth * rows, half_depth * rows))
    attn_near, down_rest, up_grad, up_sum, up_sent, full_down, cot_cols, group_normed = fence(
        attn_near, down_rest, up_grad, up_sum, up_sent, full_down, cot_cols, group_normed
    )

    up_first = links.swap_x(up_sent[0])
    full_attn = [
        jnp.concatenate(
            [
                values[side * rows : (side + 1) * rows, at * attn_cols : (at + 1) * attn_cols]
                for side in range(2)
                for values in attn_near
            ],
            0,
        )
        for at in range(4)
    ]
    order = [links.slots_of(links.partner(at) * col_blocks, col_blocks) for at in range(group)]
    context_sum = jnp.concatenate(
        product_rows(cot_cols, full_attn[3], jnp.concatenate(order), rows, jnp.float32), 0
    )
    context_sum = [context_sum[:, at * attn_cols : (at + 1) * attn_cols] for at in range(group)]
    sent = low(jnp.concatenate(context_sum[2:], 1))
    arrived = links.swap_core(turn_core(sent))
    context_y = links.swap_y(turn_y(low(context_sum[1] + wide(arrived[:, attn_cols:]))))
    context_grad = low(context_sum[0] + wide(arrived[:, :attn_cols]) + wide(context_y))
    down_summed = half_product(
        [group_cot], [act_low], 0, jnp.concatenate([down_first, down_rest], 0)
    )
    down_parts = scatter_z(down_summed, range(1, depth - 1))
    up_first, down_summed, down_parts, full_attn, context_grad, up_sent = fence(
        up_first, down_summed, down_parts, full_attn, context_grad, up_sent
    )

    up_rest = links.swap_x(up_sent[1])
    down_parts = [down_summed[:rows]] + down_parts + scatter_z(down_summed, [depth - 1])
    attn_bias = lax.dynamic_slice(param_vals, (8, member * attn_cols), (3, attn_cols))
    context_low, proj_grads, proj_sums = attention_inner(
        jnp.cumsum(group_lengths, 1),
        group_normed[:3],
        full_attn[:3],
        attn_bias,
        rope_rows(tok_count),
        context_grad,
    )
    two_sent = half_product(
        [group_normed[2], group_normed[0]], [proj_grads[2], proj_grads[0]], 1
    )
    three_near, three_sent = spread(up_grad, full_up)
    context_turned = turn_y(context_low)
    (
        up_rest, down_parts, context_low, context_turned, proj_grads, proj_sums, two_sent,
        three_near, three_sent,
    ) = fence(
        up_rest, down_parts, context_low, context_turned, proj_grads, proj_sums, two_sent,
        three_near, three_sent,
    )

    two_x = links.swap_x(two_sent)
    up_summed = half_product(
        [group_normed[3]], [up_grad], 0, jnp.concatenate([up_first, up_rest], 0)
    )
    up_parts = scatter_z(up_summed, range(1, depth - 1))
    context_near = jnp.concatenate([context_low, links.swap_y(context_turned)], 1)
    context_far = links.swap_core(turn_core(context_near))
    order = []
    for owner in links.slots():
        place = (owner // col_blocks) ^ member
        place = (place % 2) * 2 + place // 2
        order.append(place * col_blocks + owner % col_blocks)
    (group_context,) = take_blocks(
        [[jnp.concatenate([context_near, context_far], 1)]],
        jnp.stack(order).astype(jnp.int32),
        rows,
    )
    one_sent = half_product([group_normed[1], group_context], [proj_grads[1], cot_cols], 1)
    three_arrived = links.swap_core(three_sent)
    token_parts = [spread(proj_grads[at], full_attn[at]) for at in range(3)]
    two_x, up_summed, up_parts, group_context, one_sent, token_parts, three_arrived = fence(
        two_x, up_summed, up_parts, group_context, one_sent, token_parts, three_arrived
    )

    def across_y(near, arrived):
        summed = near + wide(arrived)
        return summed[:tok_count] + wide(links.swap_y(low(summed[tok_count:])))

    one_x = links.swap_x(one_sent)
    up_parts = [up_summed[:rows]] + up_parts + scatter_z(up_summed, [depth - 1])
    two_summed = half_product(
        [group_normed[2], group_normed[0]], [proj_grads[2], proj_grads[0]], 0, two_x
    )
    two_parts = scatter_z(two_summed, [1])
    back_three = across_y(three_near, three_arrived)
    token_arrived = [links.swap_core(far) for _, far in token_parts]
    back_two = across_y(token_parts[2][0], token_arrived[2])
    one_x, up_parts, two_summed, two_parts, back_three, back_two, token_arrived = fence(
        one_x, up_parts, two_summed, two_parts, back_three, back_two, token_arrived
    )

    two_parts = [two_summed[:rows]] + two_parts + scatter_z(two_summed, range(2, depth))
    mlp_grad, mlp_mom, mlp_gram = finish_gradient([up_parts, down_parts], mlp_moment)
    one_summed = half_product(
        [group_normed[1], group_context], [proj_grads[1], cot_cols], 0, one_x
    )
    one_parts = scatter_z(one_summed, [1])
    mlp_gram = links.sum_stack(mlp_gram)
    back_zero = across_y(token_parts[0][0], token_arrived[0])
    back_one = across_y(token_parts[1][0], token_arrived[1])
    two_parts, one_summed, one_parts, back_zero, back_one, mlp_mom, mlp_gram = fence(
        two_parts, one_summed, one_parts, back_zero, back_one, mlp_mom, mlp_gram
    )

    one_parts = [one_summed[:rows]] + one_parts + scatter_z(one_summed, range(2, depth))
    mlp_new, mlp_low = newton_update(
        mlp_gram, mlp_mom, mlp_master, LR_MUON * 0.2 * math.sqrt(FF)
    )
    mlp_across = links.swap_y(mlp_low)
    history_grad, sums, mix_weight_grad, mixing_grad = mix_backward(
        history,
        out_grad,
        tok_weight[:, None],
        [back_zero, back_one, back_two, back_three],
        kept,
        coef,
        inner,
        scale,
        param_low[17:],
        mixing,
        param_vals[:8],
    )
    one_parts, mlp_low, mlp_across, sums, mix_weight_grad, mixing_grad = fence(
        one_parts, mlp_low, mlp_across, sums, mix_weight_grad, mixing_grad
    )

    attn_parts = [
        [values[:, :attn_cols] for values in two_parts],
        [values[:, attn_cols:] for values in two_parts],
        [values[:, :attn_cols] for values in one_parts],
        [values[:, attn_cols:] for values in one_parts],
    ]
    attn_parts = [attn_parts[1], attn_parts[2], attn_parts[0], attn_parts[3]]
    attn_grad, attn_mom, attn_gram = finish_gradient(attn_parts, attn_moment)
    attn_gram = links.sum_stack(attn_gram)
    mlp_near, mlp_sent = product_rows(act_low, full_down, plain, rows, jnp.float32)
    attn_out = jnp.dot(group_context, full_attn[3], preferred_element_type=jnp.float32)

    def with_attn(part, addend):
        own = columns_of(part, member, attn_cols, 1) + addend
        return lax.dynamic_update_slice_in_dim(part, own, member * attn_cols, 1)

    out_sent = low(with_attn(mlp_sent, attn_out[near_tok:]))
    out_near = with_attn(mlp_near, attn_out[:near_tok])

    def placed(values, total):
        return lax.dynamic_update_slice_in_dim(
            jnp.zeros((values.shape[0], total), jnp.float32), values, member * values.shape[1], 1
        )

    param_grad = jnp.concatenate(
        [
            sums[:8],
            placed(proj_sums[:3], model_width),
            sums[8:9],
            sums[8:9],
            placed(up_sum, group * mlp_cols).reshape(-1, model_width),
            mix_weight_grad,
        ],
        0,
    )
    param_pieces_grad = jnp.moveaxis(param_grad.reshape(param_rows, members, rows), 1, 0)
    mix_size = mixing_grad.size
    mix_rows = -(-mix_size // rows)
    mix_flat = jnp.pad(mixing_grad.reshape(-1), (0, mix_rows * rows - mix_size))
    mix_flat = jnp.broadcast_to(mix_flat.reshape(1, mix_rows, rows), (members, mix_rows, rows))
    small_sent = jnp.concatenate([param_pieces_grad, mix_flat], 1)
    attn_gram, small_sent, attn_mom, out_sent, out_near = fence(
        attn_gram, small_sent, attn_mom, out_sent, out_near
    )

    attn_new, attn_low = newton_update(
        attn_gram, attn_mom, attn_master, LR_MUON * 0.2 * math.sqrt(model_width)
    )
    attn_copy = links.gather_copies(attn_low, links.swap_y(attn_low))
    out_own = across_y(out_near, links.swap_core(out_sent))
    layer_out = low(stream_three + out_own + (param_vals[11] + param_vals[12]))
    mlp_copy = links.gather_copies(mlp_low, mlp_across)
    small = lax.all_to_all(small_sent, "fsdp", 0, 0, tiled=True)
    small = links.sum_group(jnp.sum(small, 0))
    param_part = small[:param_rows]
    mixing_grad = small[param_rows:].reshape(-1)[:mix_size].reshape(mixing_grad.shape)
    params_m_new, params_v_new, params_new = adamw(params, param_part, params_m, params_v)
    mix_out_m_new, mix_out_v_new, mix_out_new = adamw(mix_out, mixing_grad, mix_out_m, mix_out_v)
    return (
        layer_out,
        history_grad,
        attn_grad,
        attn_mom,
        attn_new,
        attn_copy,
        mlp_grad,
        mlp_mom,
        mlp_new,
        mlp_copy,
        param_part,
        param_part[11:13],
        params_m_new,
        params_v_new,
        params_new,
        mixing_grad,
        mix_out_m_new,
        mix_out_v_new,
        mix_out_new,
    )


def solution(mesh):
    in_specs = (
        P(None, ("dp", "fsdp"), None),
        P(("dp", "fsdp"), None),
        P(("dp", "fsdp"), None),
        P(("dp", "fsdp"), None),
        P(),
        P(None, "fsdp", None),
        P(None, "fsdp", "dp"),
        P(None, "fsdp", "dp"),
        P(None, "fsdp", None),
        P(None, "fsdp", "dp"),
        P(None, "fsdp", "dp"),
        P(None, "fsdp"),
        P(None, "fsdp"),
        P(None, "fsdp"),
        P(),
        P(),
        P(),
    )
    out_specs = (
        P(("dp", "fsdp"), None),
        P(None, ("dp", "fsdp"), None),
        P(None, "fsdp", "dp"),
        P(None, "fsdp", "dp"),
        P(None, "fsdp", "dp"),
        P(None, "fsdp", None),
        P(None, "fsdp", "dp"),
        P(None, "fsdp", "dp"),
        P(None, "fsdp", "dp"),
        P(None, "fsdp", None),
        P(None, "fsdp"),
        P(None, "fsdp"),
        P(None, "fsdp"),
        P(None, "fsdp"),
        P(None, "fsdp"),
        P(),
        P(),
        P(),
        P(),
    )
    return jax.shard_map(body, mesh=mesh, in_specs=in_specs, out_specs=out_specs, check_vma=False)
```

```python
import functools
import math

import jax
import jax.numpy as jnp
from jax import lax
from jax.experimental import pallas as pl
from jax.experimental.pallas import tpu as pltpu
from jax.sharding import PartitionSpec as P

HEADS = 16
HEAD = 128
FF = 8192
ROT = 32
MIXW = 36
DOCS = 3
NDOM = 22
STEP = 6


NS_A = 3.4445
NS_B = -4.775
NS_C = 2.0315
ROPE_BASE = 10000.0
LR_MUON = 0.1
LR_ADAM = 0.03
DECAY = 0.01
MOMENTUM = 0.95
BETA_ONE = 0.9
BETA_TWO = 0.95
HIGHEST = lax.Precision.HIGHEST


def rope_rows(tok_count):
    half_rot = ROT // 2
    inverse_freq = ROPE_BASE ** (-(2.0 * jnp.arange(half_rot, dtype=jnp.float32)) / ROT)
    angles = jnp.arange(tok_count, dtype=jnp.float32)[:, None] * inverse_freq[None, :]
    cosine, sine_tab = jnp.cos(angles), jnp.sin(angles)
    zero = jnp.zeros_like(sine_tab)
    rest = jnp.zeros((tok_count, HEAD - ROT), jnp.float32)
    return jnp.stack(
        [
            jnp.concatenate([cosine, cosine, rest + 1.0], 1),
            jnp.concatenate([-sine_tab, zero, rest], 1),
            jnp.concatenate([zero, sine_tab, rest], 1),
        ]
    )


def product_nt(left_side, right_side):
    return lax.dot_general(
        left_side, right_side, (((1,), (1,)), ((), ())), preferred_element_type=jnp.float32
    )


def product_tn(left_side, right_side):
    return lax.dot_general(
        left_side, right_side, (((0,), (0,)), ((), ())), preferred_element_type=jnp.float32
    )


def token_weights(lengths, domains, weight_table, tok_count):
    doc_ends = jnp.cumsum(lengths)
    positions = jnp.arange(tok_count, dtype=jnp.int32)
    doc_of = jnp.sum((positions[:, None] >= doc_ends[None, :]).astype(jnp.int32), 1)
    domain = jnp.sum(
        jnp.where(
            doc_of[:, None] == jnp.arange(DOCS, dtype=jnp.int32)[None, :], domains[None, :], 0
        ),
        1,
    )
    weight = jnp.sum(
        jnp.where(
            domain[:, None] == jnp.arange(NDOM, dtype=jnp.int32)[None, :], weight_table[None, :], 0
        ),
        1,
    )
    return weight.astype(jnp.float32) / 256.0


def cost_of(work):
    return pl.CostEstimate(
        flops=int(work * 1.15e9), bytes_accessed=int(work * 3.69e6), transcendentals=0
    )

VMEM_BYTES = 56 * 1024 * 1024


def kernel_params():
    return pltpu.CompilerParams(vmem_limit_bytes=VMEM_BYTES)


def whole_block(shape):
    return pl.BlockSpec(shape, lambda *_: (0,) * len(shape))


def shaped(shape, dtype):
    return jax.ShapeDtypeStruct(shape, dtype)


def gelu_pair(values):
    share = 0.5 * (1.0 + lax.erf(values * math.sqrt(0.5)))
    bell = jnp.exp(-0.5 * values * values) * (1.0 / math.sqrt(2.0 * math.pi))
    return (values * share, share + values * bell)


def dot_nn(left_side, right_side):
    return jnp.dot(left_side, right_side, preferred_element_type=jnp.float32)


def exact_dot(left_side, right_side, dims=((1,), (0,))):
    return lax.dot_general(
        left_side,
        right_side,
        (dims, ((), ())),
        precision=HIGHEST,
        preferred_element_type=jnp.float32,
    )


def copy_kernel(order_ref, *refs, counts):
    sources, targets = refs[: -len(counts)], refs[-len(counts) :]
    at = 0
    for target, count in zip(targets, counts):
        height = target.shape[0] // count
        for place in range(count):
            target[place * height : (place + 1) * height, :] = sources[at][...]
            at += 1


def take_blocks(groups, order, width):
    count = order.shape[0]
    if width % 128:
        return [
            jnp.concatenate(
                [
                    jnp.concatenate(
                        [
                            lax.dynamic_slice_in_dim(values, order[at] * width, width, 1)
                            for at in range(count)
                        ],
                        1,
                    )
                    for values in arrays
                ],
                0,
            )
            for arrays in groups
        ]
    flat = [values for arrays in groups for values in arrays]
    heights = [len(arrays) * arrays[0].shape[0] for arrays in groups]
    return pl.pallas_call(
        functools.partial(copy_kernel, counts=[len(arrays) for arrays in groups]),
        grid_spec=pltpu.PrefetchScalarGridSpec(
            num_scalar_prefetch=1,
            grid=(count,),
            in_specs=[
                pl.BlockSpec((values.shape[0], width), lambda at, order_ref: (0, order_ref[at]))
                for values in flat
            ],
            out_specs=[
                pl.BlockSpec((height, width), lambda at, order_ref: (0, at)) for height in heights
            ],
        ),
        out_shape=[
            shaped((height, count * width), arrays[0].dtype)
            for height, arrays in zip(heights, groups)
        ],
        compiler_params=kernel_params(),
        cost_estimate=cost_of(0.3),
        name="take_blocks",
    )(order, *flat)


def rows_kernel(order_ref, left_refs, right_refs, near_ref, far_ref):
    half = left_refs[0].shape[0] // 2
    for at, left_ref in enumerate(left_refs):
        rows = slice(at * half, (at + 1) * half)
        for place, right_ref in enumerate(right_refs[at]):
            width = right_ref.shape[0]
            span = slice(place * width, (place + 1) * width)
            result = product_nt(left_ref[...], right_ref[...])
            near_ref[rows, span] = result[:half].astype(near_ref.dtype)
            far_ref[rows, span] = result[half:].astype(far_ref.dtype)


def product_rows(lefts, rights, order, width, far_type, work=0.7):
    tokens, depth = lefts[0].shape
    half = tokens // 2
    count = order.shape[0]
    if width % 128:
        near, far = [], []
        for left_side, right_side in zip(lefts, rights):
            (result,) = take_blocks([[product_nt(left_side, right_side)]], order, width)
            near.append(result[:half])
            far.append(result[half:].astype(far_type))
        return (jnp.concatenate(near, 0), jnp.concatenate(far, 0))
    height = len(lefts) * half
    out_block = pl.BlockSpec((height, 2 * width), lambda at, order_ref: (0, at))
    right_blocks = [
        pl.BlockSpec((width, depth), lambda at, order_ref: (order_ref[2 * at], 0)),
        pl.BlockSpec((width, depth), lambda at, order_ref: (order_ref[2 * at + 1], 0)),
    ]
    return pl.pallas_call(
        rows_kernel,
        grid_spec=pltpu.PrefetchScalarGridSpec(
            num_scalar_prefetch=1,
            grid=(count // 2,),
            in_specs=[
                [pl.BlockSpec((tokens, depth), lambda at, order_ref: (0, 0))] * len(lefts),
                [right_blocks] * len(lefts),
            ],
            out_specs=[out_block, out_block],
        ),
        out_shape=[
            shaped((height, count * width), jnp.float32),
            shaped((height, count * width), far_type),
        ],
        compiler_params=kernel_params(),
        cost_estimate=cost_of(work),
        name="product_rows",
    )(order, lefts, [[right_side, right_side] for right_side in rights])


def grad_kernel(left_refs, right_refs, out_ref):
    start = 0
    for left_ref, right_ref in zip(left_refs, right_refs):
        span = slice(start, start + right_ref.shape[1])
        start = span.stop
        out_ref[:, span] = product_tn(left_ref[...], right_ref[...]).astype(out_ref.dtype)


def half_product(lefts, rights, part):
    tokens, width = lefts[0].shape
    columns = rights[0].shape[1]
    tile = 512
    col_tile = columns if len(rights) > 1 else 512
    steps = width // 2 // tile
    out_type = jnp.bfloat16 if part else jnp.float32
    return pl.pallas_call(
        grad_kernel,
        grid=(steps, columns // col_tile),
        in_specs=[
            [pl.BlockSpec((tokens, tile), lambda at, to: (0, part * steps + at))] * len(lefts),
            [pl.BlockSpec((tokens, col_tile), lambda at, to: (0, to))] * len(rights),
        ],
        out_specs=pl.BlockSpec((tile, len(rights) * col_tile), lambda at, to: (at, to)),
        out_shape=shaped((width // 2, len(rights) * columns), out_type),
        compiler_params=kernel_params(),
        cost_estimate=cost_of(0.55),
        name="half_product",
    )(lefts, rights)


MIX_STEP = 64
MIX_ROWS = 16


def mix_forward_kernel(hist_ref, weight_ref, mixing_ref, norm_ref, *outs):
    normed_refs = outs[:4]
    kept_ref, coef_ref, inner_ref, scale_ref, stream_ref = outs[4:]
    hist_count = hist_ref.shape[0]
    last = hist_ref[hist_count - 1].astype(jnp.float32)
    inv_rms = lax.rsqrt(jnp.mean(last * last, -1, keepdims=True) + 1e-06)
    inner = product_nt((last * inv_rms).astype(jnp.bfloat16), weight_ref[...])
    inner_ref[...] = inner
    hidden, _ = gelu_pair(inner)
    coef_ref[...] = exact_dot(hidden, mixing_ref[:MIXW]) + mixing_ref[MIXW:]

    def rows_step(step, carry):
        rows = pl.ds(pl.multiple_of(step * MIX_ROWS, MIX_ROWS), MIX_ROWS)
        coef = coef_ref[rows, :]
        for index in range(4):
            running = None
            for source in range(hist_count):
                at = index * hist_count + source
                term = coef[:, at : at + 1] * hist_ref[source, rows, :].astype(jnp.float32)
                running = term if running is None else running + term
            if index == 3:
                stream_ref[rows, :] = running
            centred = running - jnp.mean(running, -1, keepdims=True)
            inv_std = lax.rsqrt(jnp.mean(centred * centred, -1, keepdims=True) + 1e-05)
            normed = centred * inv_std
            kept_ref[index, rows, :] = normed
            scale_ref[rows, index : index + 1] = inv_std
            result = normed * norm_ref[index : index + 1] + norm_ref[4 + index : 5 + index]
            normed_refs[index][rows, :] = result.astype(jnp.bfloat16)
        return carry

    lax.fori_loop(0, MIX_STEP // MIX_ROWS, rows_step, 0)


def mix_forward(history, mix_weight, mixing, norm_rows):
    hist_count, tok_count, width = history.shape
    token_block = pl.BlockSpec((MIX_STEP, width), lambda at: (at, 0))
    narrow = pl.BlockSpec((MIX_STEP, MIXW), lambda at: (at, 0))
    return pl.pallas_call(
        mix_forward_kernel,
        grid=(tok_count // MIX_STEP,),
        in_specs=[
            pl.BlockSpec((hist_count, MIX_STEP, width), lambda at: (0, at, 0)),
            whole_block(mix_weight.shape),
            whole_block(mixing.shape),
            whole_block(norm_rows.shape),
        ],
        out_specs=[token_block] * 4
        + [
            pl.BlockSpec((4, MIX_STEP, width), lambda at: (0, at, 0)),
            narrow,
            narrow,
            pl.BlockSpec((MIX_STEP, 4), lambda at: (at, 0)),
            token_block,
        ],
        out_shape=[shaped((tok_count, width), jnp.bfloat16)] * 4
        + [
            shaped((4, tok_count, width), jnp.float32),
            shaped((tok_count, MIXW), jnp.float32),
            shaped((tok_count, MIXW), jnp.float32),
            shaped((tok_count, 4), jnp.float32),
            shaped((tok_count, width), jnp.float32),
        ],
        compiler_params=kernel_params(),
        cost_estimate=cost_of(0.9),
        name="mix_forward",
    )(history, mix_weight, mixing, norm_rows)


def mix_backward_kernel(
    hist_ref,
    cot_ref,
    tok_ref,
    near_refs,
    arrived_refs,
    across_refs,
    kept_ref,
    coef_ref,
    inner_ref,
    scale_ref,
    weight_ref,
    mixing_ref,
    norm_ref,
    out_ref,
    sums_ref,
    weight_grad_ref,
    mixing_grad_ref,
    stream_ref,
    last_ref,
    coef_grad_ref,
):
    hist_count = hist_ref.shape[0]

    @pl.when(pl.program_id(0) == 0)
    def _():
        sums_ref[...] = jnp.zeros_like(sums_ref)
        weight_grad_ref[...] = jnp.zeros_like(weight_grad_ref)
        mixing_grad_ref[...] = jnp.zeros_like(mixing_grad_ref)

    def rows_step(step, carry):
        rows = pl.ds(pl.multiple_of(step * MIX_ROWS, MIX_ROWS), MIX_ROWS)
        coef = coef_ref[rows, :]
        out_cot = cot_ref[rows, :].astype(jnp.float32) * tok_ref[rows, :]
        cot_low = out_cot.astype(jnp.bfloat16).astype(jnp.float32)
        sums_ref[8:9] += jnp.sum(cot_low, 0, keepdims=True)
        for index in range(4):
            back = near_refs[index][rows, :] + arrived_refs[index][rows, :].astype(jnp.float32)
            back = back + across_refs[index][rows, :].astype(jnp.float32)
            normed = kept_ref[index, rows, :]
            sums_ref[index : index + 1] += jnp.sum(back * normed, 0, keepdims=True)
            sums_ref[4 + index : 5 + index] += jnp.sum(back, 0, keepdims=True)
            scaled = back * norm_ref[index : index + 1]
            grad = scaled - jnp.mean(scaled, -1, keepdims=True)
            grad = grad - normed * jnp.mean(scaled * normed, -1, keepdims=True)
            grad = grad * scale_ref[rows, index : index + 1]
            if index == 3:
                grad = grad + out_cot
            stream_ref[index] = grad
        for source in range(hist_count):
            values = hist_ref[source, rows, :].astype(jnp.float32)
            running = None
            for index in range(4):
                at = index * hist_count + source
                grad = stream_ref[index]
                coef_grad_ref[rows, at : at + 1] = jnp.sum(values * grad, -1, keepdims=True)
                term = coef[:, at : at + 1] * grad
                running = term if running is None else running + term
            if source == hist_count - 1:
                last_ref[rows, :] = running
            else:
                out_ref[source, rows, :] = running.astype(jnp.bfloat16)
        return carry

    lax.fori_loop(0, MIX_STEP // MIX_ROWS, rows_step, 0)
    coef_grad = coef_grad_ref[...]
    hidden, slope = gelu_pair(inner_ref[...])
    mixing_grad_ref[:MIXW] += exact_dot(hidden, coef_grad, ((0,), (0,)))
    mixing_grad_ref[MIXW:] += jnp.sum(coef_grad, 0, keepdims=True)
    hidden_grad = exact_dot(coef_grad, mixing_ref[:MIXW], ((1,), (1,)))
    inner_grad = (hidden_grad * slope).astype(jnp.bfloat16)
    last = hist_ref[hist_count - 1].astype(jnp.float32)
    inv_rms = lax.rsqrt(jnp.mean(last * last, -1, keepdims=True) + 1e-06)
    unit = last * inv_rms
    weight_grad_ref[...] += product_tn(inner_grad, unit.astype(jnp.bfloat16))
    unit_grad = dot_nn(inner_grad, weight_ref[...])
    last_grad = inv_rms * (unit_grad - unit * jnp.mean(unit_grad * unit, -1, keepdims=True))
    out_ref[hist_count - 1] = (last_ref[...] + last_grad).astype(jnp.bfloat16)


def mix_backward(
    history, cot, tok_weight, sums, across, kept, coef, inner, scale, mix_weight, mixing, norm_rows
):
    hist_count, tok_count, width = history.shape
    token_block = pl.BlockSpec((MIX_STEP, width), lambda at: (at, 0))
    narrow = pl.BlockSpec((MIX_STEP, MIXW), lambda at: (at, 0))
    hist_block = pl.BlockSpec((hist_count, MIX_STEP, width), lambda at: (0, at, 0))
    pair_steps = 2 * tok_count // MIX_STEP
    pair_blocks = [
        pl.BlockSpec((MIX_STEP, width), lambda at, start=place * pair_steps: (start + at, 0))
        for _, _, place in sums
    ]
    nears = [near for near, _, _ in sums]
    arrived = [values for _, values, _ in sums]
    return pl.pallas_call(
        mix_backward_kernel,
        grid=(tok_count // MIX_STEP,),
        in_specs=[
            hist_block,
            token_block,
            pl.BlockSpec((MIX_STEP, 1), lambda at: (at, 0)),
            pair_blocks,
            pair_blocks,
            [token_block] * 4,
            pl.BlockSpec((4, MIX_STEP, width), lambda at: (0, at, 0)),
            narrow,
            narrow,
            pl.BlockSpec((MIX_STEP, 4), lambda at: (at, 0)),
            whole_block(mix_weight.shape),
            whole_block(mixing.shape),
            whole_block(norm_rows.shape),
        ],
        out_specs=[
            hist_block,
            whole_block((16, width)),
            whole_block(mix_weight.shape),
            whole_block(mixing.shape),
        ],
        out_shape=[
            shaped(history.shape, jnp.bfloat16),
            shaped((16, width), jnp.float32),
            shaped(mix_weight.shape, jnp.float32),
            shaped(mixing.shape, jnp.float32),
        ],
        scratch_shapes=[
            pltpu.VMEM((4, MIX_ROWS, width), jnp.float32),
            pltpu.VMEM((MIX_STEP, width), jnp.float32),
            pltpu.VMEM((MIX_STEP, MIXW), jnp.float32),
        ],
        compiler_params=kernel_params(),
        cost_estimate=cost_of(19),
        name="mix_backward",
    )(history, cot, tok_weight, nears, arrived, across, kept, coef, inner, scale, mix_weight, mixing, norm_rows)


def mlp_up_kernel(normed_ref, up_ref, bias_ref, act_ref, slope_ref):
    tokens = normed_ref.shape[0]
    part = tokens // 4
    for at in range(4):
        rows = pl.ds(at * part, part)
        act_val, slope = gelu_pair(dot_nn(normed_ref[rows, :], up_ref[...]) + bias_ref[...])
        act_ref[rows, :] = act_val.astype(jnp.bfloat16)
        slope_ref[rows, :] = slope


def mlp_up(normed, up_weight, bias):
    tokens, width = normed.shape
    hidden = up_weight.shape[1]
    tile = 256
    act_block = pl.BlockSpec((tokens, tile), lambda at: (0, at))
    return pl.pallas_call(
        mlp_up_kernel,
        grid=(hidden // tile,),
        in_specs=[
            whole_block(normed.shape),
            pl.BlockSpec((width, tile), lambda at: (0, at)),
            pl.BlockSpec((1, tile), lambda at: (0, at)),
        ],
        out_specs=[act_block, act_block],
        out_shape=[shaped((tokens, hidden), jnp.bfloat16), shaped((tokens, hidden), jnp.float32)],
        compiler_params=kernel_params(),
        cost_estimate=cost_of(0.85),
        name="mlp_up",
    )(normed, up_weight, bias)


def mlp_back_kernel(cot_ref, down_ref, slope_ref, grad_ref, sum_ref):
    tokens = cot_ref.shape[0]
    part = tokens // 4
    total = None
    for at in range(4):
        rows = pl.ds(at * part, part)
        act_grad = dot_nn(cot_ref[rows, :], down_ref[...])
        up_grad = (act_grad * slope_ref[rows, :]).astype(jnp.bfloat16)
        grad_ref[rows, :] = up_grad
        term = jnp.sum(up_grad.astype(jnp.float32), 0, keepdims=True)
        total = term if total is None else total + term
    sum_ref[...] = total


def mlp_back(cot, down_weight, slope):
    tokens, width = cot.shape
    hidden = down_weight.shape[1]
    tile = 256
    act_block = pl.BlockSpec((tokens, tile), lambda at: (0, at))
    row_block = pl.BlockSpec((1, tile), lambda at: (0, at))
    return pl.pallas_call(
        mlp_back_kernel,
        grid=(hidden // tile,),
        in_specs=[
            whole_block(cot.shape),
            pl.BlockSpec((width, tile), lambda at: (0, at)),
            act_block,
        ],
        out_specs=[act_block, row_block],
        out_shape=[shaped((tokens, hidden), jnp.bfloat16), shaped((1, hidden), jnp.float32)],
        compiler_params=kernel_params(),
        cost_estimate=cost_of(0.8),
        name="mlp_back",
    )(cot, down_weight, slope)


def attention_kernel(
    ends_ref, normed_refs, weight_refs, bias_ref, rope_ref, cot_ref, ctx_ref, grad_refs, sum_ref
):
    tokens, width = ctx_ref.shape
    at = pl.program_id(0)
    head_scale = 1.0 / math.sqrt(HEAD)
    half_rot = ROT // 2
    cosine, rise, fall = rope_ref[0], rope_ref[1], rope_ref[2]

    def turned(values):
        return pltpu.roll(values, HEAD - half_rot, 1) * rise + pltpu.roll(values, half_rot, 1) * fall

    def doc_of(positions):
        found = jnp.zeros(positions.shape, jnp.int32)
        for doc in range(DOCS):
            found = found + (positions >= ends_ref[at, doc]).astype(jnp.int32)
        return found

    column = lax.broadcasted_iota(jnp.int32, (tokens, tokens), 1)
    row = lax.broadcasted_iota(jnp.int32, (tokens, tokens), 0)
    allowed = (doc_of(row) == doc_of(column)) & (row >= column)
    query_all = dot_nn(normed_refs[0][...], weight_refs[0][...]) + bias_ref[0:1]
    key_all = dot_nn(normed_refs[1][...], weight_refs[1][...]) + bias_ref[1:2]
    value_all = (dot_nn(normed_refs[2][...], weight_refs[2][...]) + bias_ref[2:3]).astype(
        jnp.bfloat16
    )

    @pl.when(at == 0)
    def _():
        sum_ref[...] = jnp.zeros_like(sum_ref)

    for head in range(width // HEAD):
        span = slice(head * HEAD, (head + 1) * HEAD)
        query = query_all[:, span]
        key = key_all[:, span]
        value = value_all[:, span]
        query = (query * cosine + turned(query)).astype(jnp.bfloat16)
        key = (key * cosine + turned(key)).astype(jnp.bfloat16)
        cot = cot_ref[:, span]
        scores = jnp.where(allowed, product_nt(query, key) * head_scale, -1000000000.0)
        weights = jnp.exp(scores - jnp.max(scores, -1, keepdims=True))
        weights = weights / jnp.sum(weights, -1, keepdims=True)
        weights_low = weights.astype(jnp.bfloat16)
        ctx_ref[:, span] = dot_nn(weights_low, value).astype(jnp.bfloat16)
        prob_grad = product_nt(cot, value)
        score_grad = (
            weights * (prob_grad - jnp.sum(weights * prob_grad, -1, keepdims=True))
        ).astype(jnp.bfloat16)
        query_grad = dot_nn(score_grad, key) * head_scale
        key_grad = product_tn(score_grad, query) * head_scale
        value_grad = product_tn(weights_low, cot)
        grads = (
            query_grad * cosine - turned(query_grad),
            key_grad * cosine - turned(key_grad),
            value_grad,
        )
        for index in range(3):
            grad_low = grads[index].astype(jnp.bfloat16)
            grad_refs[index][:, span] = grad_low
            sum_ref[index : index + 1, span] += jnp.sum(
                grad_low.astype(jnp.float32), 0, keepdims=True
            )


def attention_inner(ends, normed, weights, bias, rope, cot):
    group, _ = ends.shape
    tokens = normed[0].shape[0] // group
    model_width, width = weights[0].shape
    normed_block = pl.BlockSpec((tokens, model_width), lambda at: (at, 0))
    head_block = pl.BlockSpec((tokens, width), lambda at: (at, 0))
    out = shaped((group * tokens, width), jnp.bfloat16)
    return pl.pallas_call(
        attention_kernel,
        grid=(group,),
        in_specs=[
            pl.BlockSpec(memory_space=pltpu.SMEM),
            [normed_block] * 3,
            [whole_block(weights[0].shape)] * 3,
            whole_block(bias.shape),
            whole_block(rope.shape),
            head_block,
        ],
        out_specs=[head_block, [head_block] * 3, whole_block((8, width))],
        out_shape=[out, [out] * 3, shaped((8, width), jnp.float32)],
        compiler_params=kernel_params(),
        cost_estimate=cost_of(1.35),
        name="attention_inner",
    )(ends, normed, weights, bias, rope, cot)


def finish_kernel(part_refs, moment_ref, grad_ref, mom_ref, gram_ref):
    @pl.when(pl.program_id(0) == 0)
    def _():
        gram_ref[...] = jnp.zeros_like(gram_ref)

    for at, refs in enumerate(part_refs):
        total = refs[0][...].astype(jnp.float32)
        for ref in refs[1:]:
            total = total + ref[...].astype(jnp.float32)
        grad_ref[at] = total
        mom_new = MOMENTUM * moment_ref[at] + total
        mom_ref[at] = mom_new
        gram_ref[at] += exact_dot(mom_new, mom_new, ((1,), (1,)))


def finish_gradient(parts, moment):
    count, rows, width = moment.shape
    tile = 512
    part_block = pl.BlockSpec((rows, tile), lambda at: (0, at))
    stack_block = pl.BlockSpec((count, rows, tile), lambda at: (0, 0, at))
    return pl.pallas_call(
        finish_kernel,
        grid=(width // tile,),
        in_specs=[[[part_block] * len(own) for own in parts], stack_block],
        out_specs=[stack_block, stack_block, whole_block((count, rows, rows))],
        out_shape=[shaped(moment.shape, jnp.float32)] * 2
        + [shaped((count, rows, rows), jnp.float32)],
        compiler_params=kernel_params(),
        cost_estimate=cost_of(0.5),
        name="finish_gradient",
    )(parts, moment)


def newton_kernel(gram_ref, mom_ref, master_ref, new_ref, copy_ref, *, rate):
    count, rows, _ = gram_ref.shape
    at_row = lax.broadcasted_iota(jnp.int32, (rows, rows), 0)
    eye = (at_row == lax.broadcasted_iota(jnp.int32, (rows, rows), 1)).astype(jnp.float32)
    chains = [None] * count
    grams = []
    norms = []
    for at in range(count):
        gram = gram_ref[at]
        trace = jnp.sum(jnp.sum(gram * eye, 1, keepdims=True), 0, keepdims=True)
        norm = jnp.sqrt(trace) + 1e-07
        norms.append(norm)
        grams.append(gram / (norm * norm))
    for turn in range(5):
        squares = [exact_dot(gram, gram) for gram in grams]
        factors = [
            NS_A * eye + NS_B * gram + NS_C * square for gram, square in zip(grams, squares)
        ]
        if turn == 0:
            chains = factors
        else:
            chains = [exact_dot(factor, chain) for factor, chain in zip(factors, chains)]
        if turn < 4:
            halves = [exact_dot(factor, gram) for factor, gram in zip(factors, grams)]
            grams = [exact_dot(half, factor) for half, factor in zip(halves, factors)]
    for at in range(count):
        turned = exact_dot(chains[at] / norms[at], mom_ref[at])
        fresh = master_ref[at] * (1.0 - LR_MUON * DECAY) - rate * turned
        new_ref[at] = fresh
        copy_ref[at] = fresh.astype(jnp.bfloat16)


def newton_update(gram, mom, master, rate):
    count, rows, width = mom.shape
    step = 2
    stack_block = pl.BlockSpec((step, rows, width), lambda at: (at, 0, 0))
    return pl.pallas_call(
        functools.partial(newton_kernel, rate=rate),
        grid=(count // step,),
        in_specs=[
            pl.BlockSpec((step, rows, rows), lambda at: (at, 0, 0)),
            stack_block,
            stack_block,
        ],
        out_specs=[stack_block, stack_block],
        out_shape=[shaped(mom.shape, jnp.float32), shaped(mom.shape, jnp.bfloat16)],
        compiler_params=kernel_params(),
        cost_estimate=cost_of(12),
        name="newton_update",
    )(gram, mom, master)


class Links:
    def __init__(self):
        self.members = lax.axis_size("fsdp")
        self.depth = self.members // 2
        place = lax.axis_index("fsdp")
        self.z_at = place // 2
        self.x_at = place % 2
        self.member = lax.axis_index("dp")

    def swap_core(self, values):
        return lax.ppermute(values, "dp", [(at, at ^ 1) for at in range(4)])

    def swap_y(self, values):
        return lax.ppermute(values, "dp", [(at, at ^ 2) for at in range(4)])

    def swap_x(self, values):
        return lax.ppermute(values, "fsdp", [(at, at ^ 1) for at in range(self.members)])

    def swap_z(self, values, turn):
        pairs = [(at, at ^ (2 * turn)) for at in range(self.members)]
        return lax.ppermute(values, "fsdp", pairs)

    def slots(self):
        return [
            (self.z_at ^ turn) * 2 + (self.x_at ^ side)
            for side in range(2)
            for turn in range(self.depth)
        ]

    def slot_of(self, owner):
        return ((owner % 2) ^ self.x_at) * self.depth + ((owner // 2) ^ self.z_at)

    def slots_of(self, first, count):
        return jnp.stack([self.slot_of(first + at) for at in range(count)]).astype(jnp.int32)

    def hop(self, line):
        rise, fall = line
        hops = len(rise)
        up_pairs = [(at, at + 2) for at in range(2 * hops - 2, self.members - 2)]
        down_pairs = [(at + 2, at) for at in range(0, self.members - 2 * hops)]
        return (
            rise + [lax.ppermute(rise[-1], "fsdp", up_pairs)],
            fall + [lax.ppermute(fall[-1], "fsdp", down_pairs)],
        )

    def near(self, line, turn):
        rise, fall = line
        found = {}
        for place in range(self.depth):
            found.setdefault((place ^ turn) - place, []).append(place)
        result = None
        for distance, places in found.items():
            values = fall[distance] if distance >= 0 else rise[-distance]
            if result is None:
                result = values
                continue
            here = self.z_at == places[0]
            for place in places[1:]:
                here = here | (self.z_at == place)
            result = jnp.where(here, values, result)
        return result

    def partner(self, at):
        return self.member ^ ((at % 2) * 2 + at // 2)

    def sum_group(self, values):
        values = values + self.swap_core(values)
        return values + self.swap_y(values)

    def sum_stack(self, values):
        values = values + self.swap_core(values)
        half = values.shape[0] // 2
        odd_core = self.member % 2
        own = lax.dynamic_slice_in_dim(values, odd_core * half, half, 0)
        own = own + self.swap_y(own)
        other = self.swap_core(own)
        first = jnp.where(odd_core == 1, other, own)
        return jnp.concatenate([first, jnp.where(odd_core == 1, own, other)], 0)

    def gather_copies(self, values, across, other):
        other_across = self.swap_core(across)
        odd_core = self.member % 2 == 1
        high_y = self.member >= 2
        near = [jnp.where(odd_core, other, values), jnp.where(odd_core, values, other)]
        far = [
            jnp.where(odd_core, other_across, across),
            jnp.where(odd_core, across, other_across),
        ]
        low_pair = [jnp.where(high_y, b, a) for a, b in zip(near, far)]
        high_pair = [jnp.where(high_y, a, b) for a, b in zip(near, far)]
        return jnp.concatenate(low_pair + high_pair, -1)


def turn_y(values):
    count = values.shape[0] // 4
    blocks = [values[at * count : (at + 1) * count] for at in (1, 0, 3, 2)]
    return jnp.concatenate(blocks, 0)


def turn_core(values):
    half = values.shape[0] // 2
    return jnp.concatenate([values[half:], values[:half]], 0)


def cut(values, counts):
    parts = []
    start = 0
    for count in counts:
        parts.append(values[start : start + count])
        start += count
    return parts


def low(values):
    return values.astype(jnp.bfloat16)


def wide(values):
    return values.astype(jnp.float32)


def adamw(current, grad_in, moment_one, moment_two):
    one_new = BETA_ONE * moment_one + (1.0 - BETA_ONE) * grad_in
    two_new = BETA_TWO * moment_two + (1.0 - BETA_TWO) * grad_in * grad_in
    one_hat = one_new / (1.0 - BETA_ONE**STEP)
    two_hat = two_new / (1.0 - BETA_TWO**STEP)
    updated = current * (1.0 - LR_ADAM * DECAY) - LR_ADAM * one_hat / (jnp.sqrt(two_hat) + 1e-08)
    return (one_new, two_new, updated)


def columns_of(values, member, width, axis):
    return lax.dynamic_slice_in_dim(values, member * width, width, axis)


def fence(*values):
    return lax.optimization_barrier(values)


def body(
    history,
    out_grad,
    doc_lengths,
    doc_domain,
    domain_weight,
    attn_weight,
    attn_master,
    attn_moment,
    mlp_weight,
    mlp_master,
    mlp_moment,
    params,
    params_m,
    params_v,
    mix_out,
    mix_out_m,
    mix_out_v,
):
    hist_count, tok_count, model_width = history.shape
    links = Links()
    members, depth, member = links.members, links.depth, links.member
    rows = attn_weight.shape[1]
    group = lax.axis_size("dp")
    attn_cols = attn_weight.shape[2] // group
    mlp_cols = mlp_weight.shape[2] // group
    col_blocks = attn_cols // rows
    group_tok = group * tok_count
    near_tok = group_tok // 2
    half_width = model_width // 2
    param_rows = params.shape[0]

    slots = jnp.stack(links.slots()).astype(jnp.int32)
    plain = links.slots_of(0, members)

    def slot_sums(own, arrived, turns):
        sums = []
        for turn in turns:
            total = own[turn * rows : (turn + 1) * rows] + wide(arrived[turn])
            sums.append(total if turn == 0 else low(total))
        return sums

    def spread(lefts, rights):
        return product_rows(lefts, rights, plain, rows, jnp.bfloat16)

    up_own = columns_of(mlp_weight[0], member, mlp_cols, 1)
    param_pieces = lax.all_to_all(
        jnp.broadcast_to(low(params)[None], (members, param_rows, rows)), "fsdp", 0, 0, tiled=True
    )
    up_line = links.hop(([up_own], [up_own]))
    far_up = links.swap_x(up_own)
    param_low = jnp.moveaxis(param_pieces, 0, 1).reshape(param_rows, model_width)
    tok_weight = token_weights(doc_lengths[0], doc_domain[0], domain_weight, tok_count)
    (cot_own,) = take_blocks([[low(wide(out_grad) * tok_weight[:, None])]], slots, rows)
    near_lengths = jnp.concatenate([doc_lengths, links.swap_y(doc_lengths)], 0)
    group_lengths = jnp.concatenate([near_lengths, links.swap_core(near_lengths)], 0)
    attn_own = columns_of(attn_weight, member, attn_cols, 2)
    attn_own = jnp.concatenate([attn_own[at] for at in range(4)], 1)
    mixing = wide(lax.optimization_barrier(low(mix_out)))
    up_line, far_up, attn_own, param_low, group_lengths, cot_own, mixing = fence(
        up_line, far_up, attn_own, param_low, group_lengths, cot_own, mixing
    )

    for _ in range(2, depth - 1):
        up_line = links.hop(up_line)
    far_attn = links.swap_x(attn_own)
    cot_near = jnp.concatenate([cot_own, links.swap_y(cot_own)], 0)
    *normed_own, kept, coef, inner, scale, stream_three = mix_forward(
        history, param_low[17:], mixing, wide(param_low[:8])
    )
    normed_own = take_blocks(
        [[normed_own[3], normed_own[2]], [normed_own[0], normed_own[1]]], slots, rows
    )
    down_own = columns_of(mlp_weight[1], member, mlp_cols, 1)
    (
        up_line, far_attn, attn_own, param_low, cot_near, normed_own, kept, coef, inner, scale,
        stream_three, down_own,
    ) = fence(
        up_line, far_attn, attn_own, param_low, cot_near, normed_own, kept, coef, inner, scale,
        stream_three, down_own,
    )
    param_vals = wide(param_low)

    up_line = links.hop(up_line)
    down_line = links.hop(([down_own], [down_own]))
    far_second = links.swap_x(jnp.concatenate([down_own, links.near(up_line, 1)], 0))
    first_y = links.swap_y(normed_own[0])
    cot_core = links.swap_core(cot_near)
    up_line, down_line, far_second, first_y, cot_core, cot_near, normed_own = fence(
        up_line, down_line, far_second, first_y, cot_core, cot_near, normed_own
    )
    far_down, far_up_one = cut(far_second, (rows, rows))

    for _ in range(2, depth):
        down_line = links.hop(down_line)
    up_near = [links.near(up_line, turn) for turn in range(depth)]
    far_third = links.swap_x(jnp.concatenate(up_near[2:], 0))
    first_core = links.swap_core(normed_own[0])
    first_far = links.swap_core(first_y)
    last_y = links.swap_y(normed_own[1])
    group_cot = jnp.concatenate([cot_near, cot_core], 0)
    attn_pair = jnp.concatenate([attn_own, far_attn], 0)
    down_line, far_third, first_core, first_far, last_y, attn_pair, up_near, group_cot = fence(
        down_line, far_third, first_core, first_far, last_y, attn_pair, up_near, group_cot
    )

    attn_line = links.hop(([attn_pair], [attn_pair]))
    down_near = [links.near(down_line, turn) for turn in range(depth)]
    far_fourth = links.swap_x(jnp.concatenate(down_near[1 : depth - 1], 0))
    first_parts = (normed_own[0], first_y, first_core, first_far)
    group_normed = [None] * 4
    group_normed[3] = jnp.concatenate([values[:tok_count] for values in first_parts], 0)
    full_up = jnp.concatenate(up_near + [far_up, far_up_one, far_third], 0)
    up_bias = lax.dynamic_index_in_dim(param_vals, 13 + member, 0)
    act_low, slope = mlp_up(group_normed[3], full_up, up_bias)
    attn_line, far_fourth, act_low, slope, down_near, full_up = fence(
        attn_line, far_fourth, act_low, slope, down_near, full_up
    )

    for _ in range(2, depth - 1):
        attn_line = links.hop(attn_line)
    far_last = links.swap_x(down_near[depth - 1])
    down_sent = half_product([group_cot], [act_low], 1)
    down_first = links.swap_x(down_sent[:rows])
    last_core = links.swap_core(normed_own[1])
    last_far = links.swap_core(last_y)
    group_normed[2] = jnp.concatenate([values[tok_count:] for values in first_parts], 0)
    attn_line, far_last, down_first, down_sent, last_core, last_far, group_normed = fence(
        attn_line, far_last, down_first, down_sent, last_core, last_far, group_normed
    )

    attn_line = links.hop(attn_line)
    down_rest = links.swap_x(down_sent[rows:])
    full_down = jnp.concatenate(down_near + [far_down, far_fourth, far_last], 0)
    up_grad, up_sum = mlp_back(group_cot, full_down, slope)
    up_sent = half_product([group_normed[3]], [up_grad], 1)
    down_own_sum = half_product([group_cot], [act_low], 0)
    three_near, three_sent = spread([up_grad], [full_up])
    last_parts = (normed_own[1], last_y, last_core, last_far)
    group_normed[0] = jnp.concatenate([values[:tok_count] for values in last_parts], 0)
    group_normed[1] = jnp.concatenate([values[tok_count:] for values in last_parts], 0)
    (cot_cols,) = take_blocks([[group_cot]], links.slots_of(member * col_blocks, col_blocks), rows)
    attn_near = [links.near(attn_line, turn) for turn in range(depth)]
    half_depth = depth // 2
    up_sent = cut(up_sent, (half_depth * rows, half_depth * rows))
    (
        attn_near, down_rest, up_grad, up_sum, up_sent, full_down, cot_cols, group_normed,
        down_own_sum, three_near, three_sent,
    ) = fence(
        attn_near, down_rest, up_grad, up_sum, up_sent, full_down, cot_cols, group_normed,
        down_own_sum, three_near, three_sent,
    )

    up_last = links.swap_x(up_sent[1])
    down_arrived = [down_first] + cut(down_rest, (rows,) * (depth - 1))
    down_summed = slot_sums(down_own_sum, down_arrived, range(depth))
    down_parts = [links.swap_z(down_summed[turn], turn) for turn in range(1, depth - 1)]
    full_attn = [
        jnp.concatenate(
            [
                values[side * rows : (side + 1) * rows, at * attn_cols : (at + 1) * attn_cols]
                for side in range(2)
                for values in attn_near
            ],
            0,
        )
        for at in range(4)
    ]
    order = [links.slots_of(links.partner(at) * col_blocks, col_blocks) for at in range(group)]
    context_sum = jnp.concatenate(
        product_rows([cot_cols], [full_attn[3]], jnp.concatenate(order), rows, jnp.float32), 0
    )
    context_sum = [context_sum[:, at * attn_cols : (at + 1) * attn_cols] for at in range(group)]
    sent = low(jnp.concatenate(context_sum[2:], 1))
    sent = turn_core(sent)
    context_sent = context_sum[1] + wide(links.swap_core(sent[:, attn_cols:]))
    context_sent = turn_y(low(context_sent))
    context_own = context_sum[0] + wide(links.swap_core(sent[:, :attn_cols]))
    three_arrived = links.swap_core(three_sent)
    up_own_sum = half_product([group_normed[3]], [up_grad], 0)
    (
        up_last, down_summed, down_parts, full_attn, context_sent, context_own, up_sent, up_own_sum,
        three_arrived,
    ) = fence(
        up_last, down_summed, down_parts, full_attn, context_sent, context_own, up_sent, up_own_sum,
        three_arrived,
    )

    def halves(near, arrived):
        summed = near + wide(arrived)
        return (summed[:tok_count], low(summed[tok_count:]))

    up_first = links.swap_x(up_sent[0])
    down_parts = [down_summed[0]] + down_parts + [links.swap_z(down_summed[-1], depth - 1)]
    context_y = links.swap_y(context_sent)
    half_depth = depth // 2
    last_turns = range(half_depth, depth)
    up_arrived = [None] * half_depth + cut(up_last, (rows,) * half_depth)
    up_summed = [None] * half_depth + slot_sums(up_own_sum, up_arrived, last_turns)
    three_sent = low(three_near[tok_count:] + wide(three_arrived[tok_count:]))
    context_grad = low(context_own + wide(context_y))
    (
        up_first, down_parts, context_grad, up_summed, up_own_sum, three_sent,
    ) = fence(
        up_first, down_parts, context_grad, up_summed, up_own_sum, three_sent,
    )

    up_parts = [links.swap_z(up_summed[turn], turn) for turn in list(last_turns)[:-1]]
    three_y = links.swap_y(three_sent)
    attn_bias = lax.dynamic_slice(param_vals, (8, member * attn_cols), (3, attn_cols))
    context_low, proj_grads, proj_sums = attention_inner(
        jnp.cumsum(group_lengths, 1),
        group_normed[:3],
        full_attn[:3],
        attn_bias,
        rope_rows(tok_count),
        context_grad,
    )
    two_sent = half_product(
        [group_normed[2], group_normed[0]], [proj_grads[2], proj_grads[0]], 1
    )
    token_near, token_sent = spread(
        [proj_grads[at] for at in (2, 0, 1)], [full_attn[at] for at in (2, 0, 1)]
    )
    context_turned = turn_y(context_low)
    (
        up_parts, up_summed, context_low, context_turned, proj_grads, proj_sums, two_sent,
        token_near, token_sent, three_y, full_attn, up_first, up_own_sum, act_low, full_down,
    ) = fence(
        up_parts, up_summed, context_low, context_turned, proj_grads, proj_sums, two_sent,
        token_near, token_sent, three_y, full_attn, up_first, up_own_sum, act_low, full_down,
    )

    two_x = links.swap_x(two_sent)
    up_arrived = cut(up_first, (rows,) * half_depth)
    up_summed = slot_sums(up_own_sum, up_arrived, range(half_depth)) + up_summed[half_depth:]
    up_parts = [up_summed[0]] + up_parts
    up_parts += [
        links.swap_z(up_summed[turn], turn) for turn in [depth - 1] + list(range(1, half_depth))
    ]
    token_arrived = links.swap_core(token_sent)
    mlp_near, mlp_sent = product_rows([act_low], [full_down], plain, rows, jnp.float32, 9)
    context_near = jnp.concatenate([context_low, links.swap_y(context_turned)], 1)
    context_sent = turn_core(context_near)
    two_own_sum = half_product(
        [group_normed[2], group_normed[0]], [proj_grads[2], proj_grads[0]], 0
    )
    one_sent = half_product([group_normed[1]], [proj_grads[1]], 1)
    (
        two_x, up_parts, context_near, context_sent, two_own_sum, one_sent, token_near,
        token_arrived, proj_grads, mlp_near, mlp_sent,
    ) = fence(
        two_x, up_parts, context_near, context_sent, two_own_sum, one_sent, token_near,
        token_arrived, proj_grads, mlp_near, mlp_sent,
    )

    one_x = links.swap_x(one_sent)
    two_summed = slot_sums(two_own_sum, cut(two_x, (rows,) * depth), range(depth))
    two_parts = [two_summed[0]]
    two_parts += [
        links.swap_z(two_summed[turn], turn) for turn in list(range(2, depth)) + [1]
    ]
    token_sent = []
    for at in range(3):
        span = slice((2 * at + 1) * tok_count, (2 * at + 2) * tok_count)
        token_sent.append(low(token_near[span] + wide(token_arrived[span])))
    two_y = links.swap_y(token_sent[0])
    zero_y = links.swap_y(token_sent[1])
    context_far = links.swap_core(context_sent)
    order = []
    for owner in links.slots():
        place = (owner // col_blocks) ^ member
        place = (place % 2) * 2 + place // 2
        order.append(place * col_blocks + owner % col_blocks)
    (group_context,) = take_blocks(
        [[jnp.concatenate([context_near, context_far], 1)]],
        jnp.stack(order).astype(jnp.int32),
        rows,
    )
    out_weight_sent = half_product([group_context], [cot_cols], 1)
    one_own_sum = half_product([group_normed[1]], [proj_grads[1]], 0)
    mlp_grad, mlp_mom, mlp_gram = finish_gradient([up_parts, down_parts], mlp_moment)
    (
        one_x, two_parts, zero_y, two_y, group_context, out_weight_sent, one_own_sum, mlp_mom,
        mlp_gram, token_sent,
    ) = fence(
        one_x, two_parts, zero_y, two_y, group_context, out_weight_sent, one_own_sum, mlp_mom,
        mlp_gram, token_sent,
    )

    out_x = links.swap_x(out_weight_sent)
    one_summed = slot_sums(one_own_sum, cut(one_x, (rows,) * depth), range(depth))
    one_parts = [one_summed[0]]
    one_parts += [links.swap_z(one_summed[turn], turn) for turn in range(1, depth)]
    one_y = links.swap_y(token_sent[2])
    mlp_gram = links.sum_stack(mlp_gram)
    out_own_sum = half_product([group_context], [cot_cols], 0)
    attn_out = jnp.dot(group_context, full_attn[3], preferred_element_type=jnp.float32)

    def with_attn(part, addend):
        own = columns_of(part, member, attn_cols, 1) + addend
        return lax.dynamic_update_slice_in_dim(part, own, member * attn_cols, 1)

    out_sent = low(with_attn(mlp_sent, attn_out[near_tok:]))
    out_near = with_attn(mlp_near, attn_out[:near_tok])
    out_own, out_sent = halves(out_near, links.swap_core(out_sent))
    out_x, one_parts, mlp_gram, out_own_sum, out_own, out_sent, zero_y, one_y, two_y, three_y = fence(
        out_x, one_parts, mlp_gram, out_own_sum, out_own, out_sent, zero_y, one_y, two_y, three_y
    )

    out_summed = slot_sums(out_own_sum, cut(out_x, (rows,) * depth), range(depth))
    out_parts = [out_summed[0]]
    out_parts += [links.swap_z(out_summed[turn], turn) for turn in range(1, depth)]
    out_y = links.swap_y(out_sent)
    mlp_new, mlp_low = newton_update(
        mlp_gram, mlp_mom, mlp_master, LR_MUON * 0.2 * math.sqrt(FF)
    )
    out_parts, out_y, mlp_low, zero_y, one_y, two_y, three_y = fence(
        out_parts, out_y, mlp_low, zero_y, one_y, two_y, three_y
    )

    attn_parts = [
        [values[:, attn_cols:] for values in two_parts],
        one_parts,
        [values[:, :attn_cols] for values in two_parts],
        out_parts,
    ]
    attn_grad, attn_mom, attn_gram = finish_gradient(attn_parts, attn_moment)
    attn_gram = links.sum_stack(attn_gram)
    history_grad, sums, mix_weight_grad, mixing_grad = mix_backward(
        history,
        out_grad,
        tok_weight[:, None],
        [(token_near, token_arrived, at) for at in (1, 2, 0)] + [(three_near, three_arrived, 0)],
        [zero_y, one_y, two_y, three_y],
        kept,
        coef,
        inner,
        scale,
        param_low[17:],
        mixing,
        param_vals[:8],
    )
    mlp_across = links.swap_y(mlp_low)
    mlp_other = links.swap_core(mlp_low)
    layer_out = low(stream_three + out_own + wide(out_y) + (param_vals[11] + param_vals[12]))

    def placed(values, total):
        return lax.dynamic_update_slice_in_dim(
            jnp.zeros((values.shape[0], total), jnp.float32), values, member * values.shape[1], 1
        )

    param_grad = jnp.concatenate(
        [
            sums[:8],
            placed(proj_sums[:3], model_width),
            sums[8:9],
            sums[8:9],
            placed(up_sum, group * mlp_cols).reshape(-1, model_width),
            mix_weight_grad,
        ],
        0,
    )
    param_pieces_grad = jnp.moveaxis(param_grad.reshape(param_rows, members, rows), 1, 0)
    mix_size = mixing_grad.size
    mix_rows = -(-mix_size // rows)
    mix_flat = jnp.pad(mixing_grad.reshape(-1), (0, mix_rows * rows - mix_size))
    mix_flat = jnp.broadcast_to(mix_flat.reshape(1, mix_rows, rows), (members, mix_rows, rows))
    small_sent = jnp.concatenate([param_pieces_grad, mix_flat], 1)
    attn_gram, small_sent, attn_mom, mlp_across, mlp_other = fence(
        attn_gram, small_sent, attn_mom, mlp_across, mlp_other
    )

    attn_new, attn_low = newton_update(
        attn_gram, attn_mom, attn_master, LR_MUON * 0.2 * math.sqrt(model_width)
    )
    attn_copy = links.gather_copies(attn_low, links.swap_y(attn_low), links.swap_core(attn_low))
    mlp_copy = links.gather_copies(mlp_low, mlp_across, mlp_other)
    small_sent, attn_low = fence(small_sent, attn_low)
    small = lax.all_to_all(small_sent, "fsdp", 0, 0, tiled=True)
    small = links.sum_group(jnp.sum(small, 0))
    param_part = small[:param_rows]
    mixing_grad = small[param_rows:].reshape(-1)[:mix_size].reshape(mixing_grad.shape)
    params_m_new, params_v_new, params_new = adamw(params, param_part, params_m, params_v)
    mix_out_m_new, mix_out_v_new, mix_out_new = adamw(mix_out, mixing_grad, mix_out_m, mix_out_v)
    return (
        layer_out,
        history_grad,
        attn_grad,
        attn_mom,
        attn_new,
        attn_copy,
        mlp_grad,
        mlp_mom,
        mlp_new,
        mlp_copy,
        param_part,
        param_part[11:13],
        params_m_new,
        params_v_new,
        params_new,
        mixing_grad,
        mix_out_m_new,
        mix_out_v_new,
        mix_out_new,
    )


def solution(mesh):
    in_specs = (
        P(None, ("dp", "fsdp"), None),
        P(("dp", "fsdp"), None),
        P(("dp", "fsdp"), None),
        P(("dp", "fsdp"), None),
        P(),
        P(None, "fsdp", None),
        P(None, "fsdp", "dp"),
        P(None, "fsdp", "dp"),
        P(None, "fsdp", None),
        P(None, "fsdp", "dp"),
        P(None, "fsdp", "dp"),
        P(None, "fsdp"),
        P(None, "fsdp"),
        P(None, "fsdp"),
        P(),
        P(),
        P(),
    )
    out_specs = (
        P(("dp", "fsdp"), None),
        P(None, ("dp", "fsdp"), None),
        P(None, "fsdp", "dp"),
        P(None, "fsdp", "dp"),
        P(None, "fsdp", "dp"),
        P(None, "fsdp", None),
        P(None, "fsdp", "dp"),
        P(None, "fsdp", "dp"),
        P(None, "fsdp", "dp"),
        P(None, "fsdp", None),
        P(None, "fsdp"),
        P(None, "fsdp"),
        P(None, "fsdp"),
        P(None, "fsdp"),
        P(None, "fsdp"),
        P(),
        P(),
        P(),
        P(),
    )
    return jax.shard_map(body, mesh=mesh, in_specs=in_specs, out_specs=out_specs, check_vma=False)
```

```python
import functools
import math

import jax
import jax.numpy as jnp
from jax import lax
from jax.experimental import pallas as pl
from jax.experimental.pallas import tpu as pltpu
from jax.sharding import PartitionSpec as P

HEADS = 16
HEAD = 128
FF = 8192
ROT = 32
MIXW = 36
DOCS = 3
NDOM = 22
STEP = 6


NS_A = 3.4445
NS_B = -4.775
NS_C = 2.0315
ROPE_BASE = 10000.0
LR_MUON = 0.1
LR_ADAM = 0.03
DECAY = 0.01
MOMENTUM = 0.95
BETA_ONE = 0.9
BETA_TWO = 0.95
HIGHEST = lax.Precision.HIGHEST


def rope_rows(tok_count):
    half_rot = ROT // 2
    inverse_freq = ROPE_BASE ** (-(2.0 * jnp.arange(half_rot, dtype=jnp.float32)) / ROT)
    angles = jnp.arange(tok_count, dtype=jnp.float32)[:, None] * inverse_freq[None, :]
    cosine, sine_tab = jnp.cos(angles), jnp.sin(angles)
    zero = jnp.zeros_like(sine_tab)
    rest = jnp.zeros((tok_count, HEAD - ROT), jnp.float32)
    return jnp.stack(
        [
            jnp.concatenate([cosine, cosine, rest + 1.0], 1),
            jnp.concatenate([-sine_tab, zero, rest], 1),
            jnp.concatenate([zero, sine_tab, rest], 1),
        ]
    )


def product_nt(left_side, right_side):
    return lax.dot_general(
        left_side, right_side, (((1,), (1,)), ((), ())), preferred_element_type=jnp.float32
    )


def product_tn(left_side, right_side):
    return lax.dot_general(
        left_side, right_side, (((0,), (0,)), ((), ())), preferred_element_type=jnp.float32
    )


def token_weights(lengths, domains, weight_table, tok_count):
    doc_ends = jnp.cumsum(lengths)
    positions = jnp.arange(tok_count, dtype=jnp.int32)
    doc_of = jnp.sum((positions[:, None] >= doc_ends[None, :]).astype(jnp.int32), 1)
    domain = jnp.sum(
        jnp.where(
            doc_of[:, None] == jnp.arange(DOCS, dtype=jnp.int32)[None, :], domains[None, :], 0
        ),
        1,
    )
    weight = jnp.sum(
        jnp.where(
            domain[:, None] == jnp.arange(NDOM, dtype=jnp.int32)[None, :], weight_table[None, :], 0
        ),
        1,
    )
    return weight.astype(jnp.float32) / 256.0


def cost_of(work):
    return pl.CostEstimate(
        flops=int(work * 1.15e9), bytes_accessed=int(work * 3.69e6), transcendentals=0
    )

VMEM_BYTES = 56 * 1024 * 1024


def kernel_params():
    return pltpu.CompilerParams(vmem_limit_bytes=VMEM_BYTES)


def whole_block(shape):
    return pl.BlockSpec(shape, lambda *_: (0,) * len(shape))


def shaped(shape, dtype):
    return jax.ShapeDtypeStruct(shape, dtype)


def gelu_pair(values):
    share = 0.5 * (1.0 + lax.erf(values * math.sqrt(0.5)))
    bell = jnp.exp(-0.5 * values * values) * (1.0 / math.sqrt(2.0 * math.pi))
    return (values * share, share + values * bell)


def dot_nn(left_side, right_side):
    return jnp.dot(left_side, right_side, preferred_element_type=jnp.float32)


def exact_dot(left_side, right_side, dims=((1,), (0,))):
    return lax.dot_general(
        left_side,
        right_side,
        (dims, ((), ())),
        precision=HIGHEST,
        preferred_element_type=jnp.float32,
    )


def copy_kernel(order_ref, *refs, counts):
    sources, targets = refs[: -len(counts)], refs[-len(counts) :]
    at = 0
    for target, count in zip(targets, counts):
        height = target.shape[0] // count
        for place in range(count):
            target[place * height : (place + 1) * height, :] = sources[at][...]
            at += 1


def take_blocks(groups, order, width):
    count = order.shape[0]
    if width % 128:
        return [
            jnp.concatenate(
                [
                    jnp.concatenate(
                        [
                            lax.dynamic_slice_in_dim(values, order[at] * width, width, 1)
                            for at in range(count)
                        ],
                        1,
                    )
                    for values in arrays
                ],
                0,
            )
            for arrays in groups
        ]
    flat = [values for arrays in groups for values in arrays]
    heights = [len(arrays) * arrays[0].shape[0] for arrays in groups]
    return pl.pallas_call(
        functools.partial(copy_kernel, counts=[len(arrays) for arrays in groups]),
        grid_spec=pltpu.PrefetchScalarGridSpec(
            num_scalar_prefetch=1,
            grid=(count,),
            in_specs=[
                pl.BlockSpec((values.shape[0], width), lambda at, order_ref: (0, order_ref[at]))
                for values in flat
            ],
            out_specs=[
                pl.BlockSpec((height, width), lambda at, order_ref: (0, at)) for height in heights
            ],
        ),
        out_shape=[
            shaped((height, count * width), arrays[0].dtype)
            for height, arrays in zip(heights, groups)
        ],
        compiler_params=kernel_params(),
        cost_estimate=cost_of(0.3),
        name="take_blocks",
    )(order, *flat)


def rows_kernel(order_ref, left_refs, right_refs, near_ref, far_ref):
    half = left_refs[0].shape[0] // 2
    for at, left_ref in enumerate(left_refs):
        rows = slice(at * half, (at + 1) * half)
        for place, right_ref in enumerate(right_refs[at]):
            width = right_ref.shape[0]
            span = slice(place * width, (place + 1) * width)
            result = product_nt(left_ref[...], right_ref[...])
            near_ref[rows, span] = result[:half].astype(near_ref.dtype)
            far_ref[rows, span] = result[half:].astype(far_ref.dtype)


def product_rows(lefts, rights, order, width, far_type, work=0.7):
    tokens, depth = lefts[0].shape
    half = tokens // 2
    count = order.shape[0]
    if width % 128:
        near, far = [], []
        for left_side, right_side in zip(lefts, rights):
            (result,) = take_blocks([[product_nt(left_side, right_side)]], order, width)
            near.append(result[:half])
            far.append(result[half:].astype(far_type))
        return (jnp.concatenate(near, 0), jnp.concatenate(far, 0))
    height = len(lefts) * half
    out_block = pl.BlockSpec((height, 2 * width), lambda at, order_ref: (0, at))
    right_blocks = [
        pl.BlockSpec((width, depth), lambda at, order_ref: (order_ref[2 * at], 0)),
        pl.BlockSpec((width, depth), lambda at, order_ref: (order_ref[2 * at + 1], 0)),
    ]
    return pl.pallas_call(
        rows_kernel,
        grid_spec=pltpu.PrefetchScalarGridSpec(
            num_scalar_prefetch=1,
            grid=(count // 2,),
            in_specs=[
                [pl.BlockSpec((tokens, depth), lambda at, order_ref: (0, 0))] * len(lefts),
                [right_blocks] * len(lefts),
            ],
            out_specs=[out_block, out_block],
        ),
        out_shape=[
            shaped((height, count * width), jnp.float32),
            shaped((height, count * width), far_type),
        ],
        compiler_params=kernel_params(),
        cost_estimate=cost_of(work),
        name="product_rows",
    )(order, lefts, [[right_side, right_side] for right_side in rights])


def grad_kernel(left_refs, right_refs, out_ref):
    start = 0
    for left_ref, right_ref in zip(left_refs, right_refs):
        span = slice(start, start + right_ref.shape[1])
        start = span.stop
        out_ref[:, span] = product_tn(left_ref[...], right_ref[...]).astype(out_ref.dtype)


def half_product(lefts, rights, part):
    tokens, width = lefts[0].shape
    columns = rights[0].shape[1]
    tile = 512
    col_tile = columns if len(rights) > 1 else 512
    steps = width // 2 // tile
    out_type = jnp.bfloat16 if part else jnp.float32
    return pl.pallas_call(
        grad_kernel,
        grid=(steps, columns // col_tile),
        in_specs=[
            [pl.BlockSpec((tokens, tile), lambda at, to: (0, part * steps + at))] * len(lefts),
            [pl.BlockSpec((tokens, col_tile), lambda at, to: (0, to))] * len(rights),
        ],
        out_specs=pl.BlockSpec((tile, len(rights) * col_tile), lambda at, to: (at, to)),
        out_shape=shaped((width // 2, len(rights) * columns), out_type),
        compiler_params=kernel_params(),
        cost_estimate=cost_of(0.55),
        name="half_product",
    )(lefts, rights)


MIX_STEP = 64
MIX_ROWS = 16


def mix_forward_kernel(hist_ref, weight_ref, mixing_ref, norm_ref, *outs):
    normed_refs = outs[:4]
    kept_ref, coef_ref, inner_ref, scale_ref, stream_ref = outs[4:]
    hist_count = hist_ref.shape[0]
    last = hist_ref[hist_count - 1].astype(jnp.float32)
    inv_rms = lax.rsqrt(jnp.mean(last * last, -1, keepdims=True) + 1e-06)
    inner = product_nt((last * inv_rms).astype(jnp.bfloat16), weight_ref[...])
    inner_ref[...] = inner
    hidden, _ = gelu_pair(inner)
    coef_ref[...] = exact_dot(hidden, mixing_ref[:MIXW]) + mixing_ref[MIXW:]

    def rows_step(step, carry):
        rows = pl.ds(pl.multiple_of(step * MIX_ROWS, MIX_ROWS), MIX_ROWS)
        coef = coef_ref[rows, :]
        for index in range(4):
            running = None
            for source in range(hist_count):
                at = index * hist_count + source
                term = coef[:, at : at + 1] * hist_ref[source, rows, :].astype(jnp.float32)
                running = term if running is None else running + term
            if index == 3:
                stream_ref[rows, :] = running
            centred = running - jnp.mean(running, -1, keepdims=True)
            inv_std = lax.rsqrt(jnp.mean(centred * centred, -1, keepdims=True) + 1e-05)
            normed = centred * inv_std
            kept_ref[index, rows, :] = normed
            scale_ref[rows, index : index + 1] = inv_std
            result = normed * norm_ref[index : index + 1] + norm_ref[4 + index : 5 + index]
            normed_refs[index][rows, :] = result.astype(jnp.bfloat16)
        return carry

    lax.fori_loop(0, MIX_STEP // MIX_ROWS, rows_step, 0)


def mix_forward(history, mix_weight, mixing, norm_rows):
    hist_count, tok_count, width = history.shape
    token_block = pl.BlockSpec((MIX_STEP, width), lambda at: (at, 0))
    narrow = pl.BlockSpec((MIX_STEP, MIXW), lambda at: (at, 0))
    return pl.pallas_call(
        mix_forward_kernel,
        grid=(tok_count // MIX_STEP,),
        in_specs=[
            pl.BlockSpec((hist_count, MIX_STEP, width), lambda at: (0, at, 0)),
            whole_block(mix_weight.shape),
            whole_block(mixing.shape),
            whole_block(norm_rows.shape),
        ],
        out_specs=[token_block] * 4
        + [
            pl.BlockSpec((4, MIX_STEP, width), lambda at: (0, at, 0)),
            narrow,
            narrow,
            pl.BlockSpec((MIX_STEP, 4), lambda at: (at, 0)),
            token_block,
        ],
        out_shape=[shaped((tok_count, width), jnp.bfloat16)] * 4
        + [
            shaped((4, tok_count, width), jnp.float32),
            shaped((tok_count, MIXW), jnp.float32),
            shaped((tok_count, MIXW), jnp.float32),
            shaped((tok_count, 4), jnp.float32),
            shaped((tok_count, width), jnp.float32),
        ],
        compiler_params=kernel_params(),
        cost_estimate=cost_of(0.9),
        name="mix_forward",
    )(history, mix_weight, mixing, norm_rows)


def mix_backward_kernel(
    hist_ref,
    cot_ref,
    tok_ref,
    near_refs,
    arrived_refs,
    across_refs,
    kept_ref,
    coef_ref,
    inner_ref,
    scale_ref,
    weight_ref,
    mixing_ref,
    norm_ref,
    out_ref,
    sums_ref,
    weight_grad_ref,
    mixing_grad_ref,
    stream_ref,
    last_ref,
    coef_grad_ref,
):
    hist_count = hist_ref.shape[0]

    @pl.when(pl.program_id(0) == 0)
    def _():
        sums_ref[...] = jnp.zeros_like(sums_ref)
        weight_grad_ref[...] = jnp.zeros_like(weight_grad_ref)
        mixing_grad_ref[...] = jnp.zeros_like(mixing_grad_ref)

    def rows_step(step, carry):
        rows = pl.ds(pl.multiple_of(step * MIX_ROWS, MIX_ROWS), MIX_ROWS)
        coef = coef_ref[rows, :]
        out_cot = cot_ref[rows, :].astype(jnp.float32) * tok_ref[rows, :]
        cot_low = out_cot.astype(jnp.bfloat16).astype(jnp.float32)
        sums_ref[8:9] += jnp.sum(cot_low, 0, keepdims=True)
        for index in range(4):
            back = near_refs[index][rows, :] + arrived_refs[index][rows, :].astype(jnp.float32)
            back = back + across_refs[index][rows, :].astype(jnp.float32)
            normed = kept_ref[index, rows, :]
            sums_ref[index : index + 1] += jnp.sum(back * normed, 0, keepdims=True)
            sums_ref[4 + index : 5 + index] += jnp.sum(back, 0, keepdims=True)
            scaled = back * norm_ref[index : index + 1]
            grad = scaled - jnp.mean(scaled, -1, keepdims=True)
            grad = grad - normed * jnp.mean(scaled * normed, -1, keepdims=True)
            grad = grad * scale_ref[rows, index : index + 1]
            if index == 3:
                grad = grad + out_cot
            stream_ref[index] = grad
        for source in range(hist_count):
            values = hist_ref[source, rows, :].astype(jnp.float32)
            running = None
            for index in range(4):
                at = index * hist_count + source
                grad = stream_ref[index]
                coef_grad_ref[rows, at : at + 1] = jnp.sum(values * grad, -1, keepdims=True)
                term = coef[:, at : at + 1] * grad
                running = term if running is None else running + term
            if source == hist_count - 1:
                last_ref[rows, :] = running
            else:
                out_ref[source, rows, :] = running.astype(jnp.bfloat16)
        return carry

    lax.fori_loop(0, MIX_STEP // MIX_ROWS, rows_step, 0)
    coef_grad = coef_grad_ref[...]
    hidden, slope = gelu_pair(inner_ref[...])
    mixing_grad_ref[:MIXW] += exact_dot(hidden, coef_grad, ((0,), (0,)))
    mixing_grad_ref[MIXW:] += jnp.sum(coef_grad, 0, keepdims=True)
    hidden_grad = exact_dot(coef_grad, mixing_ref[:MIXW], ((1,), (1,)))
    inner_grad = (hidden_grad * slope).astype(jnp.bfloat16)
    last = hist_ref[hist_count - 1].astype(jnp.float32)
    inv_rms = lax.rsqrt(jnp.mean(last * last, -1, keepdims=True) + 1e-06)
    unit = last * inv_rms
    weight_grad_ref[...] += product_tn(inner_grad, unit.astype(jnp.bfloat16))
    unit_grad = dot_nn(inner_grad, weight_ref[...])
    last_grad = inv_rms * (unit_grad - unit * jnp.mean(unit_grad * unit, -1, keepdims=True))
    out_ref[hist_count - 1] = (last_ref[...] + last_grad).astype(jnp.bfloat16)


def mix_backward(
    history, cot, tok_weight, sums, across, kept, coef, inner, scale, mix_weight, mixing, norm_rows
):
    hist_count, tok_count, width = history.shape
    token_block = pl.BlockSpec((MIX_STEP, width), lambda at: (at, 0))
    narrow = pl.BlockSpec((MIX_STEP, MIXW), lambda at: (at, 0))
    hist_block = pl.BlockSpec((hist_count, MIX_STEP, width), lambda at: (0, at, 0))
    pair_steps = 2 * tok_count // MIX_STEP
    pair_blocks = [
        pl.BlockSpec((MIX_STEP, width), lambda at, start=place * pair_steps: (start + at, 0))
        for _, _, place in sums
    ]
    nears = [near for near, _, _ in sums]
    arrived = [values for _, values, _ in sums]
    return pl.pallas_call(
        mix_backward_kernel,
        grid=(tok_count // MIX_STEP,),
        in_specs=[
            hist_block,
            token_block,
            pl.BlockSpec((MIX_STEP, 1), lambda at: (at, 0)),
            pair_blocks,
            pair_blocks,
            [token_block] * 4,
            pl.BlockSpec((4, MIX_STEP, width), lambda at: (0, at, 0)),
            narrow,
            narrow,
            pl.BlockSpec((MIX_STEP, 4), lambda at: (at, 0)),
            whole_block(mix_weight.shape),
            whole_block(mixing.shape),
            whole_block(norm_rows.shape),
        ],
        out_specs=[
            hist_block,
            whole_block((16, width)),
            whole_block(mix_weight.shape),
            whole_block(mixing.shape),
        ],
        out_shape=[
            shaped(history.shape, jnp.bfloat16),
            shaped((16, width), jnp.float32),
            shaped(mix_weight.shape, jnp.float32),
            shaped(mixing.shape, jnp.float32),
        ],
        scratch_shapes=[
            pltpu.VMEM((4, MIX_ROWS, width), jnp.float32),
            pltpu.VMEM((MIX_STEP, width), jnp.float32),
            pltpu.VMEM((MIX_STEP, MIXW), jnp.float32),
        ],
        compiler_params=kernel_params(),
        cost_estimate=cost_of(19),
        name="mix_backward",
    )(history, cot, tok_weight, nears, arrived, across, kept, coef, inner, scale, mix_weight, mixing, norm_rows)


def mlp_up_kernel(normed_ref, up_ref, bias_ref, act_ref, slope_ref):
    tokens = normed_ref.shape[0]
    part = tokens // 4
    for at in range(4):
        rows = pl.ds(at * part, part)
        act_val, slope = gelu_pair(dot_nn(normed_ref[rows, :], up_ref[...]) + bias_ref[...])
        act_ref[rows, :] = act_val.astype(jnp.bfloat16)
        slope_ref[rows, :] = slope


def mlp_up(normed, up_weight, bias):
    tokens, width = normed.shape
    hidden = up_weight.shape[1]
    tile = 256
    act_block = pl.BlockSpec((tokens, tile), lambda at: (0, at))
    return pl.pallas_call(
        mlp_up_kernel,
        grid=(hidden // tile,),
        in_specs=[
            whole_block(normed.shape),
            pl.BlockSpec((width, tile), lambda at: (0, at)),
            pl.BlockSpec((1, tile), lambda at: (0, at)),
        ],
        out_specs=[act_block, act_block],
        out_shape=[shaped((tokens, hidden), jnp.bfloat16), shaped((tokens, hidden), jnp.float32)],
        compiler_params=kernel_params(),
        cost_estimate=cost_of(0.85),
        name="mlp_up",
    )(normed, up_weight, bias)


def mlp_back_kernel(cot_ref, down_ref, slope_ref, grad_ref, sum_ref):
    tokens = cot_ref.shape[0]
    part = tokens // 4
    total = None
    for at in range(4):
        rows = pl.ds(at * part, part)
        act_grad = dot_nn(cot_ref[rows, :], down_ref[...])
        up_grad = (act_grad * slope_ref[rows, :]).astype(jnp.bfloat16)
        grad_ref[rows, :] = up_grad
        term = jnp.sum(up_grad.astype(jnp.float32), 0, keepdims=True)
        total = term if total is None else total + term
    sum_ref[...] = total


def mlp_back(cot, down_weight, slope):
    tokens, width = cot.shape
    hidden = down_weight.shape[1]
    tile = 256
    act_block = pl.BlockSpec((tokens, tile), lambda at: (0, at))
    row_block = pl.BlockSpec((1, tile), lambda at: (0, at))
    return pl.pallas_call(
        mlp_back_kernel,
        grid=(hidden // tile,),
        in_specs=[
            whole_block(cot.shape),
            pl.BlockSpec((width, tile), lambda at: (0, at)),
            act_block,
        ],
        out_specs=[act_block, row_block],
        out_shape=[shaped((tokens, hidden), jnp.bfloat16), shaped((1, hidden), jnp.float32)],
        compiler_params=kernel_params(),
        cost_estimate=cost_of(0.8),
        name="mlp_back",
    )(cot, down_weight, slope)


def attention_kernel(
    ends_ref, normed_refs, weight_refs, bias_ref, rope_ref, cot_ref, ctx_ref, grad_refs, sum_ref
):
    tokens, width = ctx_ref.shape
    at = pl.program_id(0)
    head_scale = 1.0 / math.sqrt(HEAD)
    half_rot = ROT // 2
    cosine, rise, fall = rope_ref[0], rope_ref[1], rope_ref[2]

    def turned(values):
        return pltpu.roll(values, HEAD - half_rot, 1) * rise + pltpu.roll(values, half_rot, 1) * fall

    def doc_of(positions):
        found = jnp.zeros(positions.shape, jnp.int32)
        for doc in range(DOCS):
            found = found + (positions >= ends_ref[at, doc]).astype(jnp.int32)
        return found

    column = lax.broadcasted_iota(jnp.int32, (tokens, tokens), 1)
    row = lax.broadcasted_iota(jnp.int32, (tokens, tokens), 0)
    allowed = (doc_of(row) == doc_of(column)) & (row >= column)
    query_all = dot_nn(normed_refs[0][...], weight_refs[0][...]) + bias_ref[0:1]
    key_all = dot_nn(normed_refs[1][...], weight_refs[1][...]) + bias_ref[1:2]
    value_all = (dot_nn(normed_refs[2][...], weight_refs[2][...]) + bias_ref[2:3]).astype(
        jnp.bfloat16
    )

    @pl.when(at == 0)
    def _():
        sum_ref[...] = jnp.zeros_like(sum_ref)

    for head in range(width // HEAD):
        span = slice(head * HEAD, (head + 1) * HEAD)
        query = query_all[:, span]
        key = key_all[:, span]
        value = value_all[:, span]
        query = (query * cosine + turned(query)).astype(jnp.bfloat16)
        key = (key * cosine + turned(key)).astype(jnp.bfloat16)
        cot = cot_ref[:, span]
        scores = jnp.where(allowed, product_nt(query, key) * head_scale, -1000000000.0)
        weights = jnp.exp(scores - jnp.max(scores, -1, keepdims=True))
        weights = weights / jnp.sum(weights, -1, keepdims=True)
        weights_low = weights.astype(jnp.bfloat16)
        ctx_ref[:, span] = dot_nn(weights_low, value).astype(jnp.bfloat16)
        prob_grad = product_nt(cot, value)
        score_grad = (
            weights * (prob_grad - jnp.sum(weights * prob_grad, -1, keepdims=True))
        ).astype(jnp.bfloat16)
        query_grad = dot_nn(score_grad, key) * head_scale
        key_grad = product_tn(score_grad, query) * head_scale
        value_grad = product_tn(weights_low, cot)
        grads = (
            query_grad * cosine - turned(query_grad),
            key_grad * cosine - turned(key_grad),
            value_grad,
        )
        for index in range(3):
            grad_low = grads[index].astype(jnp.bfloat16)
            grad_refs[index][:, span] = grad_low
            sum_ref[index : index + 1, span] += jnp.sum(
                grad_low.astype(jnp.float32), 0, keepdims=True
            )


def attention_inner(ends, normed, weights, bias, rope, cot):
    group, _ = ends.shape
    tokens = normed[0].shape[0] // group
    model_width, width = weights[0].shape
    normed_block = pl.BlockSpec((tokens, model_width), lambda at: (at, 0))
    head_block = pl.BlockSpec((tokens, width), lambda at: (at, 0))
    out = shaped((group * tokens, width), jnp.bfloat16)
    return pl.pallas_call(
        attention_kernel,
        grid=(group,),
        in_specs=[
            pl.BlockSpec(memory_space=pltpu.SMEM),
            [normed_block] * 3,
            [whole_block(weights[0].shape)] * 3,
            whole_block(bias.shape),
            whole_block(rope.shape),
            head_block,
        ],
        out_specs=[head_block, [head_block] * 3, whole_block((8, width))],
        out_shape=[out, [out] * 3, shaped((8, width), jnp.float32)],
        compiler_params=kernel_params(),
        cost_estimate=cost_of(1.35),
        name="attention_inner",
    )(ends, normed, weights, bias, rope, cot)


def finish_kernel(part_refs, moment_ref, grad_ref, mom_ref, gram_ref):
    @pl.when(pl.program_id(0) == 0)
    def _():
        gram_ref[...] = jnp.zeros_like(gram_ref)

    for at, refs in enumerate(part_refs):
        total = refs[0][...].astype(jnp.float32)
        for ref in refs[1:]:
            total = total + ref[...].astype(jnp.float32)
        grad_ref[at] = total
        mom_new = MOMENTUM * moment_ref[at] + total
        mom_ref[at] = mom_new
        gram_ref[at] += exact_dot(mom_new, mom_new, ((1,), (1,)))


def finish_gradient(parts, moment):
    count, rows, width = moment.shape
    tile = 512
    part_block = pl.BlockSpec((rows, tile), lambda at: (0, at))
    stack_block = pl.BlockSpec((count, rows, tile), lambda at: (0, 0, at))
    return pl.pallas_call(
        finish_kernel,
        grid=(width // tile,),
        in_specs=[[[part_block] * len(own) for own in parts], stack_block],
        out_specs=[stack_block, stack_block, whole_block((count, rows, rows))],
        out_shape=[shaped(moment.shape, jnp.float32)] * 2
        + [shaped((count, rows, rows), jnp.float32)],
        compiler_params=kernel_params(),
        cost_estimate=cost_of(0.5),
        name="finish_gradient",
    )(parts, moment)


def newton_kernel(gram_ref, mom_ref, master_ref, new_ref, copy_ref, *, rate):
    count, rows, _ = gram_ref.shape
    at_row = lax.broadcasted_iota(jnp.int32, (rows, rows), 0)
    eye = (at_row == lax.broadcasted_iota(jnp.int32, (rows, rows), 1)).astype(jnp.float32)
    chains = [None] * count
    grams = []
    norms = []
    for at in range(count):
        gram = gram_ref[at]
        trace = jnp.sum(jnp.sum(gram * eye, 1, keepdims=True), 0, keepdims=True)
        norm = jnp.sqrt(trace) + 1e-07
        norms.append(norm)
        grams.append(gram / (norm * norm))
    for turn in range(5):
        squares = [exact_dot(gram, gram) for gram in grams]
        factors = [
            NS_A * eye + NS_B * gram + NS_C * square for gram, square in zip(grams, squares)
        ]
        if turn == 0:
            chains = factors
        else:
            chains = [exact_dot(factor, chain) for factor, chain in zip(factors, chains)]
        if turn < 4:
            halves = [exact_dot(factor, gram) for factor, gram in zip(factors, grams)]
            grams = [exact_dot(half, factor) for half, factor in zip(halves, factors)]
    for at in range(count):
        turned = exact_dot(chains[at] / norms[at], mom_ref[at])
        fresh = master_ref[at] * (1.0 - LR_MUON * DECAY) - rate * turned
        new_ref[at] = fresh
        copy_ref[at] = fresh.astype(jnp.bfloat16)


def newton_update(gram, mom, master, rate, first=0, pairs=None):
    count, rows, width = mom.shape
    step = 2
    pairs = count // step if pairs is None else pairs
    shape = (pairs * step, rows, width)
    stack_in = pl.BlockSpec((step, rows, width), lambda at: (first + at, 0, 0))
    stack_out = pl.BlockSpec((step, rows, width), lambda at: (at, 0, 0))
    return pl.pallas_call(
        functools.partial(newton_kernel, rate=rate),
        grid=(pairs,),
        in_specs=[
            pl.BlockSpec((step, rows, rows), lambda at: (first + at, 0, 0)),
            stack_in,
            stack_in,
        ],
        out_specs=[stack_out, stack_out],
        out_shape=[shaped(shape, jnp.float32), shaped(shape, jnp.bfloat16)],
        compiler_params=kernel_params(),
        cost_estimate=cost_of(12),
        name="newton_update",
    )(gram, mom, master)


class Links:
    def __init__(self):
        self.members = lax.axis_size("fsdp")
        self.depth = self.members // 2
        place = lax.axis_index("fsdp")
        self.z_at = place // 2
        self.x_at = place % 2
        self.member = lax.axis_index("dp")

    def swap_core(self, values):
        return lax.ppermute(values, "dp", [(at, at ^ 1) for at in range(4)])

    def swap_y(self, values):
        return lax.ppermute(values, "dp", [(at, at ^ 2) for at in range(4)])

    def swap_x(self, values):
        return lax.ppermute(values, "fsdp", [(at, at ^ 1) for at in range(self.members)])

    def swap_z(self, values, turn):
        pairs = [(at, at ^ (2 * turn)) for at in range(self.members)]
        return lax.ppermute(values, "fsdp", pairs)

    def slots(self):
        return [
            (self.z_at ^ turn) * 2 + (self.x_at ^ side)
            for side in range(2)
            for turn in range(self.depth)
        ]

    def slot_of(self, owner):
        return ((owner % 2) ^ self.x_at) * self.depth + ((owner // 2) ^ self.z_at)

    def slots_of(self, first, count):
        return jnp.stack([self.slot_of(first + at) for at in range(count)]).astype(jnp.int32)

    def hop(self, line):
        rise, fall = line
        hops = len(rise)
        up_pairs = [(at, at + 2) for at in range(2 * hops - 2, self.members - 2)]
        down_pairs = [(at + 2, at) for at in range(0, self.members - 2 * hops)]
        return (
            rise + [lax.ppermute(rise[-1], "fsdp", up_pairs)],
            fall + [lax.ppermute(fall[-1], "fsdp", down_pairs)],
        )

    def near(self, line, turn):
        rise, fall = line
        found = {}
        for place in range(self.depth):
            found.setdefault((place ^ turn) - place, []).append(place)
        result = None
        for distance, places in found.items():
            values = fall[distance] if distance >= 0 else rise[-distance]
            if result is None:
                result = values
                continue
            here = self.z_at == places[0]
            for place in places[1:]:
                here = here | (self.z_at == place)
            result = jnp.where(here, values, result)
        return result

    def partner(self, at):
        return self.member ^ ((at % 2) * 2 + at // 2)

    def sum_group(self, values):
        values = values + self.swap_core(values)
        return values + self.swap_y(values)

    def sum_stack(self, values):
        values = values + self.swap_core(values)
        half = values.shape[0] // 2
        odd_core = self.member % 2
        own = lax.dynamic_slice_in_dim(values, odd_core * half, half, 0)
        own = own + self.swap_y(own)
        other = self.swap_core(own)
        first = jnp.where(odd_core == 1, other, own)
        return jnp.concatenate([first, jnp.where(odd_core == 1, own, other)], 0)

    def gather_copies(self, values, across, other):
        other_across = self.swap_core(across)
        odd_core = self.member % 2 == 1
        high_y = self.member >= 2
        near = [jnp.where(odd_core, other, values), jnp.where(odd_core, values, other)]
        far = [
            jnp.where(odd_core, other_across, across),
            jnp.where(odd_core, across, other_across),
        ]
        low_pair = [jnp.where(high_y, b, a) for a, b in zip(near, far)]
        high_pair = [jnp.where(high_y, a, b) for a, b in zip(near, far)]
        return jnp.concatenate(low_pair + high_pair, -1)


def turn_y(values):
    count = values.shape[0] // 4
    blocks = [values[at * count : (at + 1) * count] for at in (1, 0, 3, 2)]
    return jnp.concatenate(blocks, 0)


def turn_core(values):
    half = values.shape[0] // 2
    return jnp.concatenate([values[half:], values[:half]], 0)


def cut(values, counts):
    parts = []
    start = 0
    for count in counts:
        parts.append(values[start : start + count])
        start += count
    return parts


def low(values):
    return values.astype(jnp.bfloat16)


def wide(values):
    return values.astype(jnp.float32)


def adamw(current, grad_in, moment_one, moment_two):
    one_new = BETA_ONE * moment_one + (1.0 - BETA_ONE) * grad_in
    two_new = BETA_TWO * moment_two + (1.0 - BETA_TWO) * grad_in * grad_in
    one_hat = one_new / (1.0 - BETA_ONE**STEP)
    two_hat = two_new / (1.0 - BETA_TWO**STEP)
    updated = current * (1.0 - LR_ADAM * DECAY) - LR_ADAM * one_hat / (jnp.sqrt(two_hat) + 1e-08)
    return (one_new, two_new, updated)


def columns_of(values, member, width, axis):
    return lax.dynamic_slice_in_dim(values, member * width, width, axis)


def fence(*values):
    return lax.optimization_barrier(values)


def body(
    history,
    out_grad,
    doc_lengths,
    doc_domain,
    domain_weight,
    attn_weight,
    attn_master,
    attn_moment,
    mlp_weight,
    mlp_master,
    mlp_moment,
    params,
    params_m,
    params_v,
    mix_out,
    mix_out_m,
    mix_out_v,
):
    hist_count, tok_count, model_width = history.shape
    links = Links()
    members, depth, member = links.members, links.depth, links.member
    rows = attn_weight.shape[1]
    group = lax.axis_size("dp")
    attn_cols = attn_weight.shape[2] // group
    mlp_cols = mlp_weight.shape[2] // group
    col_blocks = attn_cols // rows
    group_tok = group * tok_count
    near_tok = group_tok // 2
    half_width = model_width // 2
    param_rows = params.shape[0]

    slots = jnp.stack(links.slots()).astype(jnp.int32)
    plain = links.slots_of(0, members)

    def slot_sums(own, arrived, turns):
        sums = []
        for turn in turns:
            total = own[turn * rows : (turn + 1) * rows] + wide(arrived[turn])
            sums.append(total if turn == 0 else low(total))
        return sums

    def spread(lefts, rights):
        return product_rows(lefts, rights, plain, rows, jnp.bfloat16)

    up_own = columns_of(mlp_weight[0], member, mlp_cols, 1)
    param_pieces = lax.all_to_all(
        jnp.broadcast_to(low(params)[None], (members, param_rows, rows)), "fsdp", 0, 0, tiled=True
    )
    up_line = links.hop(([up_own], [up_own]))
    far_up = links.swap_x(up_own)
    param_low = jnp.moveaxis(param_pieces, 0, 1).reshape(param_rows, model_width)
    tok_weight = token_weights(doc_lengths[0], doc_domain[0], domain_weight, tok_count)
    (cot_own,) = take_blocks([[low(wide(out_grad) * tok_weight[:, None])]], slots, rows)
    near_lengths = jnp.concatenate([doc_lengths, links.swap_y(doc_lengths)], 0)
    group_lengths = jnp.concatenate([near_lengths, links.swap_core(near_lengths)], 0)
    attn_own = columns_of(attn_weight, member, attn_cols, 2)
    attn_own = jnp.concatenate([attn_own[at] for at in range(4)], 1)
    mixing = wide(lax.optimization_barrier(low(mix_out)))
    up_line, far_up, attn_own, param_low, group_lengths, cot_own, mixing = fence(
        up_line, far_up, attn_own, param_low, group_lengths, cot_own, mixing
    )

    for _ in range(2, depth - 1):
        up_line = links.hop(up_line)
    far_attn = links.swap_x(attn_own)
    cot_near = jnp.concatenate([cot_own, links.swap_y(cot_own)], 0)
    *normed_own, kept, coef, inner, scale, stream_three = mix_forward(
        history, param_low[17:], mixing, wide(param_low[:8])
    )
    normed_own = take_blocks(
        [[normed_own[3], normed_own[2]], [normed_own[0], normed_own[1]]], slots, rows
    )
    down_own = columns_of(mlp_weight[1], member, mlp_cols, 1)
    (
        up_line, far_attn, attn_own, param_low, cot_near, normed_own, kept, coef, inner, scale,
        stream_three, down_own,
    ) = fence(
        up_line, far_attn, attn_own, param_low, cot_near, normed_own, kept, coef, inner, scale,
        stream_three, down_own,
    )
    param_vals = wide(param_low)

    up_line = links.hop(up_line)
    down_line = links.hop(([down_own], [down_own]))
    far_second = links.swap_x(jnp.concatenate([down_own, links.near(up_line, 1)], 0))
    first_y = links.swap_y(normed_own[0])
    cot_core = links.swap_core(cot_near)
    up_line, down_line, far_second, first_y, cot_core, cot_near, normed_own = fence(
        up_line, down_line, far_second, first_y, cot_core, cot_near, normed_own
    )
    far_down, far_up_one = cut(far_second, (rows, rows))

    for _ in range(2, depth):
        down_line = links.hop(down_line)
    up_near = [links.near(up_line, turn) for turn in range(depth)]
    far_third = links.swap_x(jnp.concatenate(up_near[2:], 0))
    first_core = links.swap_core(normed_own[0])
    first_far = links.swap_core(first_y)
    last_y = links.swap_y(normed_own[1])
    group_cot = jnp.concatenate([cot_near, cot_core], 0)
    attn_pair = jnp.concatenate([attn_own, far_attn], 0)
    down_line, far_third, first_core, first_far, last_y, attn_pair, up_near, group_cot = fence(
        down_line, far_third, first_core, first_far, last_y, attn_pair, up_near, group_cot
    )

    attn_line = links.hop(([attn_pair], [attn_pair]))
    down_near = [links.near(down_line, turn) for turn in range(depth)]
    far_fourth = links.swap_x(jnp.concatenate(down_near[1 : depth - 1], 0))
    first_parts = (normed_own[0], first_y, first_core, first_far)
    group_normed = [None] * 4
    group_normed[3] = jnp.concatenate([values[:tok_count] for values in first_parts], 0)
    full_up = jnp.concatenate(up_near + [far_up, far_up_one, far_third], 0)
    up_bias = lax.dynamic_index_in_dim(param_vals, 13 + member, 0)
    act_low, slope = mlp_up(group_normed[3], full_up, up_bias)
    attn_line, far_fourth, act_low, slope, down_near, full_up = fence(
        attn_line, far_fourth, act_low, slope, down_near, full_up
    )

    for _ in range(2, depth - 1):
        attn_line = links.hop(attn_line)
    far_last = links.swap_x(down_near[depth - 1])
    down_sent = half_product([group_cot], [act_low], 1)
    down_first = links.swap_x(down_sent[:rows])
    last_core = links.swap_core(normed_own[1])
    last_far = links.swap_core(last_y)
    group_normed[2] = jnp.concatenate([values[tok_count:] for values in first_parts], 0)
    attn_line, far_last, down_first, down_sent, last_core, last_far, group_normed = fence(
        attn_line, far_last, down_first, down_sent, last_core, last_far, group_normed
    )

    attn_line = links.hop(attn_line)
    down_rest = links.swap_x(down_sent[rows:])
    full_down = jnp.concatenate(down_near + [far_down, far_fourth, far_last], 0)
    up_grad, up_sum = mlp_back(group_cot, full_down, slope)
    up_sent = half_product([group_normed[3]], [up_grad], 1)
    down_own_sum = half_product([group_cot], [act_low], 0)
    three_near, three_sent = spread([up_grad], [full_up])
    last_parts = (normed_own[1], last_y, last_core, last_far)
    group_normed[0] = jnp.concatenate([values[:tok_count] for values in last_parts], 0)
    group_normed[1] = jnp.concatenate([values[tok_count:] for values in last_parts], 0)
    (cot_cols,) = take_blocks([[group_cot]], links.slots_of(member * col_blocks, col_blocks), rows)
    attn_near = [links.near(attn_line, turn) for turn in range(depth)]
    half_depth = depth // 2
    up_sent = cut(up_sent, (half_depth * rows, half_depth * rows))
    (
        attn_near, down_rest, up_grad, up_sum, up_sent, full_down, cot_cols, group_normed,
        down_own_sum, three_near, three_sent,
    ) = fence(
        attn_near, down_rest, up_grad, up_sum, up_sent, full_down, cot_cols, group_normed,
        down_own_sum, three_near, three_sent,
    )

    up_last = links.swap_x(up_sent[1])
    down_arrived = [down_first] + cut(down_rest, (rows,) * (depth - 1))
    down_summed = slot_sums(down_own_sum, down_arrived, range(depth))
    down_parts = [links.swap_z(down_summed[turn], turn) for turn in range(1, depth - 1)]
    full_attn = [
        jnp.concatenate(
            [
                values[side * rows : (side + 1) * rows, at * attn_cols : (at + 1) * attn_cols]
                for side in range(2)
                for values in attn_near
            ],
            0,
        )
        for at in range(4)
    ]
    order = [links.slots_of(links.partner(at) * col_blocks, col_blocks) for at in range(group)]
    context_sum = jnp.concatenate(
        product_rows([cot_cols], [full_attn[3]], jnp.concatenate(order), rows, jnp.float32), 0
    )
    context_sum = [context_sum[:, at * attn_cols : (at + 1) * attn_cols] for at in range(group)]
    sent = low(jnp.concatenate(context_sum[2:], 1))
    sent = turn_core(sent)
    context_sent = context_sum[1] + wide(links.swap_core(sent[:, attn_cols:]))
    context_sent = turn_y(low(context_sent))
    context_own = context_sum[0] + wide(links.swap_core(sent[:, :attn_cols]))
    three_arrived = links.swap_core(three_sent)
    up_own_sum = half_product([group_normed[3]], [up_grad], 0)
    (
        up_last, down_summed, down_parts, full_attn, context_sent, context_own, up_sent, up_own_sum,
        three_arrived,
    ) = fence(
        up_last, down_summed, down_parts, full_attn, context_sent, context_own, up_sent, up_own_sum,
        three_arrived,
    )

    def halves(near, arrived):
        summed = near + wide(arrived)
        return (summed[:tok_count], low(summed[tok_count:]))

    up_first = links.swap_x(up_sent[0])
    down_parts = [down_summed[0]] + down_parts + [links.swap_z(down_summed[-1], depth - 1)]
    context_y = links.swap_y(context_sent)
    half_depth = depth // 2
    last_turns = range(half_depth, depth)
    up_arrived = [None] * half_depth + cut(up_last, (rows,) * half_depth)
    up_summed = [None] * half_depth + slot_sums(up_own_sum, up_arrived, last_turns)
    three_sent = low(three_near[tok_count:] + wide(three_arrived[tok_count:]))
    context_grad = low(context_own + wide(context_y))
    (
        up_first, down_parts, context_grad, up_summed, up_own_sum, three_sent,
    ) = fence(
        up_first, down_parts, context_grad, up_summed, up_own_sum, three_sent,
    )

    up_parts = [links.swap_z(up_summed[turn], turn) for turn in list(last_turns)[:-1]]
    three_y = links.swap_y(three_sent)
    attn_bias = lax.dynamic_slice(param_vals, (8, member * attn_cols), (3, attn_cols))
    context_low, proj_grads, proj_sums = attention_inner(
        jnp.cumsum(group_lengths, 1),
        group_normed[:3],
        full_attn[:3],
        attn_bias,
        rope_rows(tok_count),
        context_grad,
    )
    two_sent = half_product(
        [group_normed[2], group_normed[0]], [proj_grads[2], proj_grads[0]], 1
    )
    token_near, token_sent = spread(
        [proj_grads[at] for at in (2, 0, 1)], [full_attn[at] for at in (2, 0, 1)]
    )
    context_turned = turn_y(context_low)
    (
        up_parts, up_summed, context_low, context_turned, proj_grads, proj_sums, two_sent,
        token_near, token_sent, three_y, full_attn, up_first, up_own_sum, act_low, full_down,
    ) = fence(
        up_parts, up_summed, context_low, context_turned, proj_grads, proj_sums, two_sent,
        token_near, token_sent, three_y, full_attn, up_first, up_own_sum, act_low, full_down,
    )

    two_x = links.swap_x(two_sent)
    up_arrived = cut(up_first, (rows,) * half_depth)
    up_summed = slot_sums(up_own_sum, up_arrived, range(half_depth)) + up_summed[half_depth:]
    up_parts = [up_summed[0]] + up_parts
    up_parts += [
        links.swap_z(up_summed[turn], turn) for turn in [depth - 1] + list(range(1, half_depth))
    ]
    token_arrived = links.swap_core(token_sent)
    mlp_near, mlp_sent = product_rows([act_low], [full_down], plain, rows, jnp.float32, 9)
    context_near = jnp.concatenate([context_low, links.swap_y(context_turned)], 1)
    context_sent = turn_core(context_near)
    two_own_sum = half_product(
        [group_normed[2], group_normed[0]], [proj_grads[2], proj_grads[0]], 0
    )
    one_sent = half_product([group_normed[1]], [proj_grads[1]], 1)
    (
        two_x, up_parts, context_near, context_sent, two_own_sum, one_sent, token_near,
        token_arrived, proj_grads, mlp_near, mlp_sent,
    ) = fence(
        two_x, up_parts, context_near, context_sent, two_own_sum, one_sent, token_near,
        token_arrived, proj_grads, mlp_near, mlp_sent,
    )

    one_x = links.swap_x(one_sent)
    two_summed = slot_sums(two_own_sum, cut(two_x, (rows,) * depth), range(depth))
    two_parts = [two_summed[0]]
    two_parts += [
        links.swap_z(two_summed[turn], turn) for turn in list(range(2, depth)) + [1]
    ]
    token_sent = []
    for at in range(3):
        span = slice((2 * at + 1) * tok_count, (2 * at + 2) * tok_count)
        token_sent.append(low(token_near[span] + wide(token_arrived[span])))
    two_y = links.swap_y(token_sent[0])
    zero_y = links.swap_y(token_sent[1])
    context_far = links.swap_core(context_sent)
    order = []
    for owner in links.slots():
        place = (owner // col_blocks) ^ member
        place = (place % 2) * 2 + place // 2
        order.append(place * col_blocks + owner % col_blocks)
    (group_context,) = take_blocks(
        [[jnp.concatenate([context_near, context_far], 1)]],
        jnp.stack(order).astype(jnp.int32),
        rows,
    )
    out_weight_sent = half_product([group_context], [cot_cols], 1)
    one_own_sum = half_product([group_normed[1]], [proj_grads[1]], 0)
    mlp_grad, mlp_mom, mlp_gram = finish_gradient([up_parts, down_parts], mlp_moment)
    (
        one_x, two_parts, zero_y, two_y, group_context, out_weight_sent, one_own_sum, mlp_mom,
        mlp_gram, token_sent,
    ) = fence(
        one_x, two_parts, zero_y, two_y, group_context, out_weight_sent, one_own_sum, mlp_mom,
        mlp_gram, token_sent,
    )

    out_x = links.swap_x(out_weight_sent)
    one_summed = slot_sums(one_own_sum, cut(one_x, (rows,) * depth), range(depth))
    one_parts = [one_summed[0]]
    one_parts += [links.swap_z(one_summed[turn], turn) for turn in range(1, depth)]
    one_y = links.swap_y(token_sent[2])
    mlp_gram = links.sum_stack(mlp_gram)
    out_own_sum = half_product([group_context], [cot_cols], 0)
    attn_out = jnp.dot(group_context, full_attn[3], preferred_element_type=jnp.float32)

    def with_attn(part, addend):
        own = columns_of(part, member, attn_cols, 1) + addend
        return lax.dynamic_update_slice_in_dim(part, own, member * attn_cols, 1)

    out_sent = low(with_attn(mlp_sent, attn_out[near_tok:]))
    out_near = with_attn(mlp_near, attn_out[:near_tok])
    out_own, out_sent = halves(out_near, links.swap_core(out_sent))
    out_x, one_parts, mlp_gram, out_own_sum, out_own, out_sent, zero_y, one_y, two_y, three_y = fence(
        out_x, one_parts, mlp_gram, out_own_sum, out_own, out_sent, zero_y, one_y, two_y, three_y
    )

    out_summed = slot_sums(out_own_sum, cut(out_x, (rows,) * depth), range(depth))
    out_parts = [out_summed[0]]
    out_parts += [links.swap_z(out_summed[turn], turn) for turn in range(1, depth)]
    out_y = links.swap_y(out_sent)
    mlp_new, mlp_low = newton_update(
        mlp_gram, mlp_mom, mlp_master, LR_MUON * 0.2 * math.sqrt(FF)
    )
    out_parts, out_y, mlp_low, zero_y, one_y, two_y, three_y = fence(
        out_parts, out_y, mlp_low, zero_y, one_y, two_y, three_y
    )

    attn_parts = [
        [values[:, attn_cols:] for values in two_parts],
        one_parts,
        [values[:, :attn_cols] for values in two_parts],
        out_parts,
    ]
    attn_grad, attn_mom, attn_gram = finish_gradient(attn_parts, attn_moment)
    attn_gram = links.sum_stack(attn_gram)
    history_grad, sums, mix_weight_grad, mixing_grad = mix_backward(
        history,
        out_grad,
        tok_weight[:, None],
        [(token_near, token_arrived, at) for at in (1, 2, 0)] + [(three_near, three_arrived, 0)],
        [zero_y, one_y, two_y, three_y],
        kept,
        coef,
        inner,
        scale,
        param_low[17:],
        mixing,
        param_vals[:8],
    )
    mlp_across = links.swap_y(mlp_low)
    mlp_other = links.swap_core(mlp_low)
    layer_out = low(stream_three + out_own + wide(out_y) + (param_vals[11] + param_vals[12]))

    def placed(values, total):
        return lax.dynamic_update_slice_in_dim(
            jnp.zeros((values.shape[0], total), jnp.float32), values, member * values.shape[1], 1
        )

    param_grad = jnp.concatenate(
        [
            sums[:8],
            placed(proj_sums[:3], model_width),
            sums[8:9],
            sums[8:9],
            placed(up_sum, group * mlp_cols).reshape(-1, model_width),
            mix_weight_grad,
        ],
        0,
    )
    param_pieces_grad = jnp.moveaxis(param_grad.reshape(param_rows, members, rows), 1, 0)
    mix_size = mixing_grad.size
    mix_rows = -(-mix_size // rows)
    mix_flat = jnp.pad(mixing_grad.reshape(-1), (0, mix_rows * rows - mix_size))
    mix_flat = jnp.broadcast_to(mix_flat.reshape(1, mix_rows, rows), (members, mix_rows, rows))
    small_sent = jnp.concatenate([param_pieces_grad, mix_flat], 1)
    attn_gram, small_sent, attn_mom, mlp_across, mlp_other = fence(
        attn_gram, small_sent, attn_mom, mlp_across, mlp_other
    )

    attn_new, attn_copy = [], []
    for pair in range(2):
        fresh, attn_low = newton_update(
            attn_gram, attn_mom, attn_master, LR_MUON * 0.2 * math.sqrt(model_width), pair, 1
        )
        attn_new.append(fresh)
        attn_copy.append(
            links.gather_copies(attn_low, links.swap_y(attn_low), links.swap_core(attn_low))
        )
    attn_new = jnp.concatenate(attn_new, 0)
    attn_copy = jnp.concatenate(attn_copy, 0)
    mlp_copy = links.gather_copies(mlp_low, mlp_across, mlp_other)
    small_sent, attn_low = fence(small_sent, attn_low)
    small = lax.all_to_all(small_sent, "fsdp", 0, 0, tiled=True)
    small = links.sum_group(jnp.sum(small, 0))
    param_part = small[:param_rows]
    mixing_grad = small[param_rows:].reshape(-1)[:mix_size].reshape(mixing_grad.shape)
    params_m_new, params_v_new, params_new = adamw(params, param_part, params_m, params_v)
    mix_out_m_new, mix_out_v_new, mix_out_new = adamw(mix_out, mixing_grad, mix_out_m, mix_out_v)
    return (
        layer_out,
        history_grad,
        attn_grad,
        attn_mom,
        attn_new,
        attn_copy,
        mlp_grad,
        mlp_mom,
        mlp_new,
        mlp_copy,
        param_part,
        param_part[11:13],
        params_m_new,
        params_v_new,
        params_new,
        mixing_grad,
        mix_out_m_new,
        mix_out_v_new,
        mix_out_new,
    )


def solution(mesh):
    in_specs = (
        P(None, ("dp", "fsdp"), None),
        P(("dp", "fsdp"), None),
        P(("dp", "fsdp"), None),
        P(("dp", "fsdp"), None),
        P(),
        P(None, "fsdp", None),
        P(None, "fsdp", "dp"),
        P(None, "fsdp", "dp"),
        P(None, "fsdp", None),
        P(None, "fsdp", "dp"),
        P(None, "fsdp", "dp"),
        P(None, "fsdp"),
        P(None, "fsdp"),
        P(None, "fsdp"),
        P(),
        P(),
        P(),
    )
    out_specs = (
        P(("dp", "fsdp"), None),
        P(None, ("dp", "fsdp"), None),
        P(None, "fsdp", "dp"),
        P(None, "fsdp", "dp"),
        P(None, "fsdp", "dp"),
        P(None, "fsdp", None),
        P(None, "fsdp", "dp"),
        P(None, "fsdp", "dp"),
        P(None, "fsdp", "dp"),
        P(None, "fsdp", None),
        P(None, "fsdp"),
        P(None, "fsdp"),
        P(None, "fsdp"),
        P(None, "fsdp"),
        P(None, "fsdp"),
        P(),
        P(),
        P(),
        P(),
    )
    return jax.shard_map(body, mesh=mesh, in_specs=in_specs, out_specs=out_specs, check_vma=False)
```

```python
import functools
import math

import jax
import jax.numpy as jnp
from jax import lax
from jax.experimental import pallas as pl
from jax.experimental.pallas import tpu as pltpu
from jax.sharding import PartitionSpec as P

HEADS = 16
HEAD = 128
FF = 8192
ROT = 32
MIXW = 36
DOCS = 3
NDOM = 22
STEP = 6


NS_A = 3.4445
NS_B = -4.775
NS_C = 2.0315
ROPE_BASE = 10000.0
LR_MUON = 0.1
LR_ADAM = 0.03
DECAY = 0.01
MOMENTUM = 0.95
BETA_ONE = 0.9
BETA_TWO = 0.95
HIGHEST = lax.Precision.HIGHEST


def rope_rows(tok_count):
    half_rot = ROT // 2
    inverse_freq = ROPE_BASE ** (-(2.0 * jnp.arange(half_rot, dtype=jnp.float32)) / ROT)
    angles = jnp.arange(tok_count, dtype=jnp.float32)[:, None] * inverse_freq[None, :]
    cosine, sine_tab = jnp.cos(angles), jnp.sin(angles)
    zero = jnp.zeros_like(sine_tab)
    rest = jnp.zeros((tok_count, HEAD - ROT), jnp.float32)
    return jnp.stack(
        [
            jnp.concatenate([cosine, cosine, rest + 1.0], 1),
            jnp.concatenate([-sine_tab, zero, rest], 1),
            jnp.concatenate([zero, sine_tab, rest], 1),
        ]
    )


def product_nt(left_side, right_side):
    return lax.dot_general(
        left_side, right_side, (((1,), (1,)), ((), ())), preferred_element_type=jnp.float32
    )


def product_tn(left_side, right_side):
    return lax.dot_general(
        left_side, right_side, (((0,), (0,)), ((), ())), preferred_element_type=jnp.float32
    )


def token_weights(lengths, domains, weight_table, tok_count):
    doc_ends = jnp.cumsum(lengths)
    positions = jnp.arange(tok_count, dtype=jnp.int32)
    doc_of = jnp.sum((positions[:, None] >= doc_ends[None, :]).astype(jnp.int32), 1)
    domain = jnp.sum(
        jnp.where(
            doc_of[:, None] == jnp.arange(DOCS, dtype=jnp.int32)[None, :], domains[None, :], 0
        ),
        1,
    )
    weight = jnp.sum(
        jnp.where(
            domain[:, None] == jnp.arange(NDOM, dtype=jnp.int32)[None, :], weight_table[None, :], 0
        ),
        1,
    )
    return weight.astype(jnp.float32) / 256.0


def cost_of(work):
    return pl.CostEstimate(
        flops=int(work * 1.15e9), bytes_accessed=int(work * 3.69e6), transcendentals=0
    )

VMEM_BYTES = 56 * 1024 * 1024


def kernel_params():
    return pltpu.CompilerParams(vmem_limit_bytes=VMEM_BYTES)


def whole_block(shape):
    return pl.BlockSpec(shape, lambda *_: (0,) * len(shape))


def shaped(shape, dtype):
    return jax.ShapeDtypeStruct(shape, dtype)


def gelu_pair(values):
    share = 0.5 * (1.0 + lax.erf(values * math.sqrt(0.5)))
    bell = jnp.exp(-0.5 * values * values) * (1.0 / math.sqrt(2.0 * math.pi))
    return (values * share, share + values * bell)


def dot_nn(left_side, right_side):
    return jnp.dot(left_side, right_side, preferred_element_type=jnp.float32)


def exact_dot(left_side, right_side, dims=((1,), (0,))):
    return lax.dot_general(
        left_side,
        right_side,
        (dims, ((), ())),
        precision=HIGHEST,
        preferred_element_type=jnp.float32,
    )


def copy_kernel(order_ref, *refs, counts):
    sources, targets = refs[: -len(counts)], refs[-len(counts) :]
    at = 0
    for target, count in zip(targets, counts):
        height = target.shape[0] // count
        for place in range(count):
            target[place * height : (place + 1) * height, :] = sources[at][...]
            at += 1


def take_blocks(groups, order, width):
    count = order.shape[0]
    if width % 128:
        return [
            jnp.concatenate(
                [
                    jnp.concatenate(
                        [
                            lax.dynamic_slice_in_dim(values, order[at] * width, width, 1)
                            for at in range(count)
                        ],
                        1,
                    )
                    for values in arrays
                ],
                0,
            )
            for arrays in groups
        ]
    flat = [values for arrays in groups for values in arrays]
    heights = [len(arrays) * arrays[0].shape[0] for arrays in groups]
    return pl.pallas_call(
        functools.partial(copy_kernel, counts=[len(arrays) for arrays in groups]),
        grid_spec=pltpu.PrefetchScalarGridSpec(
            num_scalar_prefetch=1,
            grid=(count,),
            in_specs=[
                pl.BlockSpec((values.shape[0], width), lambda at, order_ref: (0, order_ref[at]))
                for values in flat
            ],
            out_specs=[
                pl.BlockSpec((height, width), lambda at, order_ref: (0, at)) for height in heights
            ],
        ),
        out_shape=[
            shaped((height, count * width), arrays[0].dtype)
            for height, arrays in zip(heights, groups)
        ],
        compiler_params=kernel_params(),
        cost_estimate=cost_of(0.3),
        name="take_blocks",
    )(order, *flat)


def rows_kernel(order_ref, left_refs, right_refs, near_ref, far_ref):
    half = left_refs[0].shape[0] // 2
    for at, left_ref in enumerate(left_refs):
        rows = slice(at * half, (at + 1) * half)
        for place, right_ref in enumerate(right_refs[at]):
            width = right_ref.shape[0]
            span = slice(place * width, (place + 1) * width)
            result = product_nt(left_ref[...], right_ref[...])
            near_ref[rows, span] = result[:half].astype(near_ref.dtype)
            far_ref[rows, span] = result[half:].astype(far_ref.dtype)


def product_rows(lefts, rights, order, width, far_type, work=0.7):
    tokens, depth = lefts[0].shape
    half = tokens // 2
    count = order.shape[0]
    if width % 128:
        near, far = [], []
        for left_side, right_side in zip(lefts, rights):
            (result,) = take_blocks([[product_nt(left_side, right_side)]], order, width)
            near.append(result[:half])
            far.append(result[half:].astype(far_type))
        return (jnp.concatenate(near, 0), jnp.concatenate(far, 0))
    height = len(lefts) * half
    out_block = pl.BlockSpec((height, 2 * width), lambda at, order_ref: (0, at))
    right_blocks = [
        pl.BlockSpec((width, depth), lambda at, order_ref: (order_ref[2 * at], 0)),
        pl.BlockSpec((width, depth), lambda at, order_ref: (order_ref[2 * at + 1], 0)),
    ]
    return pl.pallas_call(
        rows_kernel,
        grid_spec=pltpu.PrefetchScalarGridSpec(
            num_scalar_prefetch=1,
            grid=(count // 2,),
            in_specs=[
                [pl.BlockSpec((tokens, depth), lambda at, order_ref: (0, 0))] * len(lefts),
                [right_blocks] * len(lefts),
            ],
            out_specs=[out_block, out_block],
        ),
        out_shape=[
            shaped((height, count * width), jnp.float32),
            shaped((height, count * width), far_type),
        ],
        compiler_params=kernel_params(),
        cost_estimate=cost_of(work),
        name="product_rows",
    )(order, lefts, [[right_side, right_side] for right_side in rights])


def grad_kernel(left_refs, right_refs, out_ref):
    start = 0
    for left_ref, right_ref in zip(left_refs, right_refs):
        span = slice(start, start + right_ref.shape[1])
        start = span.stop
        out_ref[:, span] = product_tn(left_ref[...], right_ref[...]).astype(out_ref.dtype)


def half_product(lefts, rights, part):
    tokens, width = lefts[0].shape
    columns = rights[0].shape[1]
    tile = 512
    col_tile = columns if len(rights) > 1 else 512
    steps = width // 2 // tile
    out_type = jnp.bfloat16 if part else jnp.float32
    return pl.pallas_call(
        grad_kernel,
        grid=(steps, columns // col_tile),
        in_specs=[
            [pl.BlockSpec((tokens, tile), lambda at, to: (0, part * steps + at))] * len(lefts),
            [pl.BlockSpec((tokens, col_tile), lambda at, to: (0, to))] * len(rights),
        ],
        out_specs=pl.BlockSpec((tile, len(rights) * col_tile), lambda at, to: (at, to)),
        out_shape=shaped((width // 2, len(rights) * columns), out_type),
        compiler_params=kernel_params(),
        cost_estimate=cost_of(0.55),
        name="half_product",
    )(lefts, rights)


MIX_STEP = 64
MIX_ROWS = 16


def mix_forward_kernel(hist_ref, weight_ref, mixing_ref, norm_ref, *outs):
    normed_refs = outs[:4]
    kept_ref, coef_ref, inner_ref, scale_ref, stream_ref = outs[4:]
    hist_count = hist_ref.shape[0]
    last = hist_ref[hist_count - 1].astype(jnp.float32)
    inv_rms = lax.rsqrt(jnp.mean(last * last, -1, keepdims=True) + 1e-06)
    inner = product_nt((last * inv_rms).astype(jnp.bfloat16), weight_ref[...])
    inner_ref[...] = inner
    hidden, _ = gelu_pair(inner)
    coef_ref[...] = exact_dot(hidden, mixing_ref[:MIXW]) + mixing_ref[MIXW:]

    def rows_step(step, carry):
        rows = pl.ds(pl.multiple_of(step * MIX_ROWS, MIX_ROWS), MIX_ROWS)
        coef = coef_ref[rows, :]
        for index in range(4):
            running = None
            for source in range(hist_count):
                at = index * hist_count + source
                term = coef[:, at : at + 1] * hist_ref[source, rows, :].astype(jnp.float32)
                running = term if running is None else running + term
            if index == 3:
                stream_ref[rows, :] = running
            centred = running - jnp.mean(running, -1, keepdims=True)
            inv_std = lax.rsqrt(jnp.mean(centred * centred, -1, keepdims=True) + 1e-05)
            normed = centred * inv_std
            kept_ref[index, rows, :] = normed
            scale_ref[rows, index : index + 1] = inv_std
            result = normed * norm_ref[index : index + 1] + norm_ref[4 + index : 5 + index]
            normed_refs[index][rows, :] = result.astype(jnp.bfloat16)
        return carry

    lax.fori_loop(0, MIX_STEP // MIX_ROWS, rows_step, 0)


def mix_forward(history, mix_weight, mixing, norm_rows):
    hist_count, tok_count, width = history.shape
    token_block = pl.BlockSpec((MIX_STEP, width), lambda at: (at, 0))
    narrow = pl.BlockSpec((MIX_STEP, MIXW), lambda at: (at, 0))
    return pl.pallas_call(
        mix_forward_kernel,
        grid=(tok_count // MIX_STEP,),
        in_specs=[
            pl.BlockSpec((hist_count, MIX_STEP, width), lambda at: (0, at, 0)),
            whole_block(mix_weight.shape),
            whole_block(mixing.shape),
            whole_block(norm_rows.shape),
        ],
        out_specs=[token_block] * 4
        + [
            pl.BlockSpec((4, MIX_STEP, width), lambda at: (0, at, 0)),
            narrow,
            narrow,
            pl.BlockSpec((MIX_STEP, 4), lambda at: (at, 0)),
            token_block,
        ],
        out_shape=[shaped((tok_count, width), jnp.bfloat16)] * 4
        + [
            shaped((4, tok_count, width), jnp.float32),
            shaped((tok_count, MIXW), jnp.float32),
            shaped((tok_count, MIXW), jnp.float32),
            shaped((tok_count, 4), jnp.float32),
            shaped((tok_count, width), jnp.float32),
        ],
        compiler_params=kernel_params(),
        cost_estimate=cost_of(0.9),
        name="mix_forward",
    )(history, mix_weight, mixing, norm_rows)


def mix_backward_kernel(
    hist_ref,
    cot_ref,
    tok_ref,
    near_refs,
    arrived_refs,
    across_refs,
    kept_ref,
    coef_ref,
    inner_ref,
    scale_ref,
    weight_ref,
    mixing_ref,
    norm_ref,
    out_ref,
    sums_ref,
    weight_grad_ref,
    mixing_grad_ref,
    stream_ref,
    last_ref,
    coef_grad_ref,
):
    hist_count = hist_ref.shape[0]

    @pl.when(pl.program_id(0) == 0)
    def _():
        sums_ref[...] = jnp.zeros_like(sums_ref)
        weight_grad_ref[...] = jnp.zeros_like(weight_grad_ref)
        mixing_grad_ref[...] = jnp.zeros_like(mixing_grad_ref)

    def rows_step(step, carry):
        rows = pl.ds(pl.multiple_of(step * MIX_ROWS, MIX_ROWS), MIX_ROWS)
        coef = coef_ref[rows, :]
        out_cot = cot_ref[rows, :].astype(jnp.float32) * tok_ref[rows, :]
        cot_low = out_cot.astype(jnp.bfloat16).astype(jnp.float32)
        sums_ref[8:9] += jnp.sum(cot_low, 0, keepdims=True)
        for index in range(4):
            back = near_refs[index][rows, :] + arrived_refs[index][rows, :].astype(jnp.float32)
            back = back + across_refs[index][rows, :].astype(jnp.float32)
            normed = kept_ref[index, rows, :]
            sums_ref[index : index + 1] += jnp.sum(back * normed, 0, keepdims=True)
            sums_ref[4 + index : 5 + index] += jnp.sum(back, 0, keepdims=True)
            scaled = back * norm_ref[index : index + 1]
            grad = scaled - jnp.mean(scaled, -1, keepdims=True)
            grad = grad - normed * jnp.mean(scaled * normed, -1, keepdims=True)
            grad = grad * scale_ref[rows, index : index + 1]
            if index == 3:
                grad = grad + out_cot
            stream_ref[index] = grad
        for source in range(hist_count):
            values = hist_ref[source, rows, :].astype(jnp.float32)
            running = None
            for index in range(4):
                at = index * hist_count + source
                grad = stream_ref[index]
                coef_grad_ref[rows, at : at + 1] = jnp.sum(values * grad, -1, keepdims=True)
                term = coef[:, at : at + 1] * grad
                running = term if running is None else running + term
            if source == hist_count - 1:
                last_ref[rows, :] = running
            else:
                out_ref[source, rows, :] = running.astype(jnp.bfloat16)
        return carry

    lax.fori_loop(0, MIX_STEP // MIX_ROWS, rows_step, 0)
    coef_grad = coef_grad_ref[...]
    hidden, slope = gelu_pair(inner_ref[...])
    mixing_grad_ref[:MIXW] += exact_dot(hidden, coef_grad, ((0,), (0,)))
    mixing_grad_ref[MIXW:] += jnp.sum(coef_grad, 0, keepdims=True)
    hidden_grad = exact_dot(coef_grad, mixing_ref[:MIXW], ((1,), (1,)))
    inner_grad = (hidden_grad * slope).astype(jnp.bfloat16)
    last = hist_ref[hist_count - 1].astype(jnp.float32)
    inv_rms = lax.rsqrt(jnp.mean(last * last, -1, keepdims=True) + 1e-06)
    unit = last * inv_rms
    weight_grad_ref[...] += product_tn(inner_grad, unit.astype(jnp.bfloat16))
    unit_grad = dot_nn(inner_grad, weight_ref[...])
    last_grad = inv_rms * (unit_grad - unit * jnp.mean(unit_grad * unit, -1, keepdims=True))
    out_ref[hist_count - 1] = (last_ref[...] + last_grad).astype(jnp.bfloat16)


def mix_backward(
    history, cot, tok_weight, sums, across, kept, coef, inner, scale, mix_weight, mixing, norm_rows
):
    hist_count, tok_count, width = history.shape
    token_block = pl.BlockSpec((MIX_STEP, width), lambda at: (at, 0))
    narrow = pl.BlockSpec((MIX_STEP, MIXW), lambda at: (at, 0))
    hist_block = pl.BlockSpec((hist_count, MIX_STEP, width), lambda at: (0, at, 0))
    pair_steps = 2 * tok_count // MIX_STEP
    pair_blocks = [
        pl.BlockSpec((MIX_STEP, width), lambda at, start=place * pair_steps: (start + at, 0))
        for _, _, place in sums
    ]
    nears = [near for near, _, _ in sums]
    arrived = [values for _, values, _ in sums]
    return pl.pallas_call(
        mix_backward_kernel,
        grid=(tok_count // MIX_STEP,),
        in_specs=[
            hist_block,
            token_block,
            pl.BlockSpec((MIX_STEP, 1), lambda at: (at, 0)),
            pair_blocks,
            pair_blocks,
            [token_block] * 4,
            pl.BlockSpec((4, MIX_STEP, width), lambda at: (0, at, 0)),
            narrow,
            narrow,
            pl.BlockSpec((MIX_STEP, 4), lambda at: (at, 0)),
            whole_block(mix_weight.shape),
            whole_block(mixing.shape),
            whole_block(norm_rows.shape),
        ],
        out_specs=[
            hist_block,
            whole_block((16, width)),
            whole_block(mix_weight.shape),
            whole_block(mixing.shape),
        ],
        out_shape=[
            shaped(history.shape, jnp.bfloat16),
            shaped((16, width), jnp.float32),
            shaped(mix_weight.shape, jnp.float32),
            shaped(mixing.shape, jnp.float32),
        ],
        scratch_shapes=[
            pltpu.VMEM((4, MIX_ROWS, width), jnp.float32),
            pltpu.VMEM((MIX_STEP, width), jnp.float32),
            pltpu.VMEM((MIX_STEP, MIXW), jnp.float32),
        ],
        compiler_params=kernel_params(),
        cost_estimate=cost_of(19),
        name="mix_backward",
    )(history, cot, tok_weight, nears, arrived, across, kept, coef, inner, scale, mix_weight, mixing, norm_rows)


def mlp_up_kernel(normed_ref, up_ref, bias_ref, act_ref, slope_ref):
    tokens = normed_ref.shape[0]
    part = tokens // 4
    for at in range(4):
        rows = pl.ds(at * part, part)
        act_val, slope = gelu_pair(dot_nn(normed_ref[rows, :], up_ref[...]) + bias_ref[...])
        act_ref[rows, :] = act_val.astype(jnp.bfloat16)
        slope_ref[rows, :] = slope


def mlp_up(normed, up_weight, bias):
    tokens, width = normed.shape
    hidden = up_weight.shape[1]
    tile = 256
    act_block = pl.BlockSpec((tokens, tile), lambda at: (0, at))
    return pl.pallas_call(
        mlp_up_kernel,
        grid=(hidden // tile,),
        in_specs=[
            whole_block(normed.shape),
            pl.BlockSpec((width, tile), lambda at: (0, at)),
            pl.BlockSpec((1, tile), lambda at: (0, at)),
        ],
        out_specs=[act_block, act_block],
        out_shape=[shaped((tokens, hidden), jnp.bfloat16), shaped((tokens, hidden), jnp.float32)],
        compiler_params=kernel_params(),
        cost_estimate=cost_of(0.85),
        name="mlp_up",
    )(normed, up_weight, bias)


def mlp_back_kernel(cot_ref, down_ref, slope_ref, grad_ref, sum_ref):
    tokens = cot_ref.shape[0]
    part = tokens // 4
    total = None
    for at in range(4):
        rows = pl.ds(at * part, part)
        act_grad = dot_nn(cot_ref[rows, :], down_ref[...])
        up_grad = (act_grad * slope_ref[rows, :]).astype(jnp.bfloat16)
        grad_ref[rows, :] = up_grad
        term = jnp.sum(up_grad.astype(jnp.float32), 0, keepdims=True)
        total = term if total is None else total + term
    sum_ref[...] = total


def mlp_back(cot, down_weight, slope):
    tokens, width = cot.shape
    hidden = down_weight.shape[1]
    tile = 256
    act_block = pl.BlockSpec((tokens, tile), lambda at: (0, at))
    row_block = pl.BlockSpec((1, tile), lambda at: (0, at))
    return pl.pallas_call(
        mlp_back_kernel,
        grid=(hidden // tile,),
        in_specs=[
            whole_block(cot.shape),
            pl.BlockSpec((width, tile), lambda at: (0, at)),
            act_block,
        ],
        out_specs=[act_block, row_block],
        out_shape=[shaped((tokens, hidden), jnp.bfloat16), shaped((1, hidden), jnp.float32)],
        compiler_params=kernel_params(),
        cost_estimate=cost_of(0.8),
        name="mlp_back",
    )(cot, down_weight, slope)


def attention_kernel(
    ends_ref, normed_refs, weight_refs, bias_ref, rope_ref, cot_ref, ctx_ref, grad_refs, sum_ref
):
    tokens, width = ctx_ref.shape
    at = pl.program_id(0)
    head_scale = 1.0 / math.sqrt(HEAD)
    half_rot = ROT // 2
    cosine, rise, fall = rope_ref[0], rope_ref[1], rope_ref[2]

    def turned(values):
        return pltpu.roll(values, HEAD - half_rot, 1) * rise + pltpu.roll(values, half_rot, 1) * fall

    def doc_of(positions):
        found = jnp.zeros(positions.shape, jnp.int32)
        for doc in range(DOCS):
            found = found + (positions >= ends_ref[at, doc]).astype(jnp.int32)
        return found

    column = lax.broadcasted_iota(jnp.int32, (tokens, tokens), 1)
    row = lax.broadcasted_iota(jnp.int32, (tokens, tokens), 0)
    allowed = (doc_of(row) == doc_of(column)) & (row >= column)
    query_all = dot_nn(normed_refs[0][...], weight_refs[0][...]) + bias_ref[0:1]
    key_all = dot_nn(normed_refs[1][...], weight_refs[1][...]) + bias_ref[1:2]
    value_all = (dot_nn(normed_refs[2][...], weight_refs[2][...]) + bias_ref[2:3]).astype(
        jnp.bfloat16
    )

    @pl.when(at == 0)
    def _():
        sum_ref[...] = jnp.zeros_like(sum_ref)

    for head in range(width // HEAD):
        span = slice(head * HEAD, (head + 1) * HEAD)
        query = query_all[:, span]
        key = key_all[:, span]
        value = value_all[:, span]
        query = (query * cosine + turned(query)).astype(jnp.bfloat16)
        key = (key * cosine + turned(key)).astype(jnp.bfloat16)
        cot = cot_ref[:, span]
        scores = jnp.where(allowed, product_nt(query, key) * head_scale, -1000000000.0)
        weights = jnp.exp(scores - jnp.max(scores, -1, keepdims=True))
        weights = weights / jnp.sum(weights, -1, keepdims=True)
        weights_low = weights.astype(jnp.bfloat16)
        ctx_ref[:, span] = dot_nn(weights_low, value).astype(jnp.bfloat16)
        prob_grad = product_nt(cot, value)
        score_grad = (
            weights * (prob_grad - jnp.sum(weights * prob_grad, -1, keepdims=True))
        ).astype(jnp.bfloat16)
        query_grad = dot_nn(score_grad, key) * head_scale
        key_grad = product_tn(score_grad, query) * head_scale
        value_grad = product_tn(weights_low, cot)
        grads = (
            query_grad * cosine - turned(query_grad),
            key_grad * cosine - turned(key_grad),
            value_grad,
        )
        for index in range(3):
            grad_low = grads[index].astype(jnp.bfloat16)
            grad_refs[index][:, span] = grad_low
            sum_ref[index : index + 1, span] += jnp.sum(
                grad_low.astype(jnp.float32), 0, keepdims=True
            )


def attention_inner(ends, normed, weights, bias, rope, cot):
    group, _ = ends.shape
    tokens = normed[0].shape[0] // group
    model_width, width = weights[0].shape
    normed_block = pl.BlockSpec((tokens, model_width), lambda at: (at, 0))
    head_block = pl.BlockSpec((tokens, width), lambda at: (at, 0))
    out = shaped((group * tokens, width), jnp.bfloat16)
    return pl.pallas_call(
        attention_kernel,
        grid=(group,),
        in_specs=[
            pl.BlockSpec(memory_space=pltpu.SMEM),
            [normed_block] * 3,
            [whole_block(weights[0].shape)] * 3,
            whole_block(bias.shape),
            whole_block(rope.shape),
            head_block,
        ],
        out_specs=[head_block, [head_block] * 3, whole_block((8, width))],
        out_shape=[out, [out] * 3, shaped((8, width), jnp.float32)],
        compiler_params=kernel_params(),
        cost_estimate=cost_of(1.35),
        name="attention_inner",
    )(ends, normed, weights, bias, rope, cot)


def finish_kernel(part_refs, moment_ref, grad_ref, mom_ref, gram_ref):
    @pl.when(pl.program_id(0) == 0)
    def _():
        gram_ref[...] = jnp.zeros_like(gram_ref)

    for at, refs in enumerate(part_refs):
        total = refs[0][...].astype(jnp.float32)
        for ref in refs[1:]:
            total = total + ref[...].astype(jnp.float32)
        grad_ref[at] = total
        mom_new = MOMENTUM * moment_ref[at] + total
        mom_ref[at] = mom_new
        gram_ref[at] += exact_dot(mom_new, mom_new, ((1,), (1,)))


def finish_gradient(parts, moment):
    count, rows, width = moment.shape
    tile = 512
    part_block = pl.BlockSpec((rows, tile), lambda at: (0, at))
    stack_block = pl.BlockSpec((count, rows, tile), lambda at: (0, 0, at))
    return pl.pallas_call(
        finish_kernel,
        grid=(width // tile,),
        in_specs=[[[part_block] * len(own) for own in parts], stack_block],
        out_specs=[stack_block, stack_block, whole_block((count, rows, rows))],
        out_shape=[shaped(moment.shape, jnp.float32)] * 2
        + [shaped((count, rows, rows), jnp.float32)],
        compiler_params=kernel_params(),
        cost_estimate=cost_of(0.5),
        name="finish_gradient",
    )(parts, moment)


def newton_kernel(gram_ref, mom_ref, master_ref, new_ref, copy_ref, *, rate):
    count, rows, _ = gram_ref.shape
    at_row = lax.broadcasted_iota(jnp.int32, (rows, rows), 0)
    eye = (at_row == lax.broadcasted_iota(jnp.int32, (rows, rows), 1)).astype(jnp.float32)
    chains = [None] * count
    grams = []
    norms = []
    for at in range(count):
        gram = gram_ref[at]
        trace = jnp.sum(jnp.sum(gram * eye, 1, keepdims=True), 0, keepdims=True)
        norm = jnp.sqrt(trace) + 1e-07
        norms.append(norm)
        grams.append(gram / (norm * norm))
    for turn in range(5):
        squares = [exact_dot(gram, gram) for gram in grams]
        factors = [
            NS_A * eye + NS_B * gram + NS_C * square for gram, square in zip(grams, squares)
        ]
        if turn == 0:
            chains = factors
        else:
            chains = [exact_dot(factor, chain) for factor, chain in zip(factors, chains)]
        if turn < 4:
            halves = [exact_dot(factor, gram) for factor, gram in zip(factors, grams)]
            grams = [exact_dot(half, factor) for half, factor in zip(halves, factors)]
    for at in range(count):
        turned = exact_dot(chains[at] / norms[at], mom_ref[at])
        fresh = master_ref[at] * (1.0 - LR_MUON * DECAY) - rate * turned
        new_ref[at] = fresh
        copy_ref[at] = fresh.astype(jnp.bfloat16)


def newton_update(gram, mom, master, rate, first=0, pairs=None):
    count, rows, width = mom.shape
    step = 2
    pairs = count // step if pairs is None else pairs
    shape = (pairs * step, rows, width)
    stack_in = pl.BlockSpec((step, rows, width), lambda at: (first + at, 0, 0))
    stack_out = pl.BlockSpec((step, rows, width), lambda at: (at, 0, 0))
    return pl.pallas_call(
        functools.partial(newton_kernel, rate=rate),
        grid=(pairs,),
        in_specs=[
            pl.BlockSpec((step, rows, rows), lambda at: (first + at, 0, 0)),
            stack_in,
            stack_in,
        ],
        out_specs=[stack_out, stack_out],
        out_shape=[shaped(shape, jnp.float32), shaped(shape, jnp.bfloat16)],
        compiler_params=kernel_params(),
        cost_estimate=cost_of(12),
        name="newton_update",
    )(gram, mom, master)


class Links:
    def __init__(self):
        self.members = lax.axis_size("fsdp")
        self.depth = self.members // 2
        place = lax.axis_index("fsdp")
        self.z_at = place // 2
        self.x_at = place % 2
        self.member = lax.axis_index("dp")

    def swap_core(self, values):
        return lax.ppermute(values, "dp", [(at, at ^ 1) for at in range(4)])

    def swap_y(self, values):
        return lax.ppermute(values, "dp", [(at, at ^ 2) for at in range(4)])

    def swap_x(self, values):
        return lax.ppermute(values, "fsdp", [(at, at ^ 1) for at in range(self.members)])

    def swap_z(self, values, turn):
        pairs = [(at, at ^ (2 * turn)) for at in range(self.members)]
        return lax.ppermute(values, "fsdp", pairs)

    def slots(self):
        return [
            (self.z_at ^ turn) * 2 + (self.x_at ^ side)
            for side in range(2)
            for turn in range(self.depth)
        ]

    def slot_of(self, owner):
        return ((owner % 2) ^ self.x_at) * self.depth + ((owner // 2) ^ self.z_at)

    def slots_of(self, first, count):
        return jnp.stack([self.slot_of(first + at) for at in range(count)]).astype(jnp.int32)

    def hop(self, line):
        rise, fall = line
        hops = len(rise)
        up_pairs = [(at, at + 2) for at in range(2 * hops - 2, self.members - 2)]
        down_pairs = [(at + 2, at) for at in range(0, self.members - 2 * hops)]
        return (
            rise + [lax.ppermute(rise[-1], "fsdp", up_pairs)],
            fall + [lax.ppermute(fall[-1], "fsdp", down_pairs)],
        )

    def near(self, line, turn):
        rise, fall = line
        found = {}
        for place in range(self.depth):
            found.setdefault((place ^ turn) - place, []).append(place)
        result = None
        for distance, places in found.items():
            values = fall[distance] if distance >= 0 else rise[-distance]
            if result is None:
                result = values
                continue
            here = self.z_at == places[0]
            for place in places[1:]:
                here = here | (self.z_at == place)
            result = jnp.where(here, values, result)
        return result

    def partner(self, at):
        return self.member ^ ((at % 2) * 2 + at // 2)

    def sum_group(self, values):
        values = values + self.swap_core(values)
        return values + self.swap_y(values)

    def sum_stack(self, values):
        values = values + self.swap_core(values)
        half = values.shape[0] // 2
        odd_core = self.member % 2
        own = lax.dynamic_slice_in_dim(values, odd_core * half, half, 0)
        own = own + self.swap_y(own)
        other = self.swap_core(own)
        first = jnp.where(odd_core == 1, other, own)
        return jnp.concatenate([first, jnp.where(odd_core == 1, own, other)], 0)

    def gather_copies(self, values, across, other):
        other_across = self.swap_core(across)
        odd_core = self.member % 2 == 1
        high_y = self.member >= 2
        near = [jnp.where(odd_core, other, values), jnp.where(odd_core, values, other)]
        far = [
            jnp.where(odd_core, other_across, across),
            jnp.where(odd_core, across, other_across),
        ]
        low_pair = [jnp.where(high_y, b, a) for a, b in zip(near, far)]
        high_pair = [jnp.where(high_y, a, b) for a, b in zip(near, far)]
        return jnp.concatenate(low_pair + high_pair, -1)


def turn_y(values):
    count = values.shape[0] // 4
    blocks = [values[at * count : (at + 1) * count] for at in (1, 0, 3, 2)]
    return jnp.concatenate(blocks, 0)


def turn_core(values):
    half = values.shape[0] // 2
    return jnp.concatenate([values[half:], values[:half]], 0)


def cut(values, counts):
    parts = []
    start = 0
    for count in counts:
        parts.append(values[start : start + count])
        start += count
    return parts


def low(values):
    return values.astype(jnp.bfloat16)


def wide(values):
    return values.astype(jnp.float32)


def adamw(current, grad_in, moment_one, moment_two):
    one_new = BETA_ONE * moment_one + (1.0 - BETA_ONE) * grad_in
    two_new = BETA_TWO * moment_two + (1.0 - BETA_TWO) * grad_in * grad_in
    one_hat = one_new / (1.0 - BETA_ONE**STEP)
    two_hat = two_new / (1.0 - BETA_TWO**STEP)
    updated = current * (1.0 - LR_ADAM * DECAY) - LR_ADAM * one_hat / (jnp.sqrt(two_hat) + 1e-08)
    return (one_new, two_new, updated)


def columns_of(values, member, width, axis):
    return lax.dynamic_slice_in_dim(values, member * width, width, axis)


def fence(*values):
    return lax.optimization_barrier(values)


def body(
    history,
    out_grad,
    doc_lengths,
    doc_domain,
    domain_weight,
    attn_weight,
    attn_master,
    attn_moment,
    mlp_weight,
    mlp_master,
    mlp_moment,
    params,
    params_m,
    params_v,
    mix_out,
    mix_out_m,
    mix_out_v,
):
    hist_count, tok_count, model_width = history.shape
    links = Links()
    members, depth, member = links.members, links.depth, links.member
    rows = attn_weight.shape[1]
    group = lax.axis_size("dp")
    attn_cols = attn_weight.shape[2] // group
    mlp_cols = mlp_weight.shape[2] // group
    col_blocks = attn_cols // rows
    group_tok = group * tok_count
    near_tok = group_tok // 2
    half_width = model_width // 2
    param_rows = params.shape[0]

    slots = jnp.stack(links.slots()).astype(jnp.int32)
    plain = links.slots_of(0, members)

    def slot_sums(own, arrived, turns):
        sums = []
        for turn in turns:
            total = own[turn * rows : (turn + 1) * rows] + wide(arrived[turn])
            sums.append(total if turn == 0 else low(total))
        return sums

    def spread(lefts, rights):
        return product_rows(lefts, rights, plain, rows, jnp.bfloat16)

    up_own = columns_of(mlp_weight[0], member, mlp_cols, 1)
    param_pieces = lax.all_to_all(
        jnp.broadcast_to(low(params)[None], (members, param_rows, rows)), "fsdp", 0, 0, tiled=True
    )
    up_line = links.hop(([up_own], [up_own]))
    far_up = links.swap_x(up_own)
    param_low = jnp.moveaxis(param_pieces, 0, 1).reshape(param_rows, model_width)
    tok_weight = token_weights(doc_lengths[0], doc_domain[0], domain_weight, tok_count)
    (cot_own,) = take_blocks([[low(wide(out_grad) * tok_weight[:, None])]], slots, rows)
    near_lengths = jnp.concatenate([doc_lengths, links.swap_y(doc_lengths)], 0)
    group_lengths = jnp.concatenate([near_lengths, links.swap_core(near_lengths)], 0)
    attn_own = columns_of(attn_weight, member, attn_cols, 2)
    attn_own = jnp.concatenate([attn_own[at] for at in range(4)], 1)
    mixing = wide(lax.optimization_barrier(low(mix_out)))
    up_line, far_up, attn_own, param_low, group_lengths, cot_own, mixing = fence(
        up_line, far_up, attn_own, param_low, group_lengths, cot_own, mixing
    )

    for _ in range(2, depth - 1):
        up_line = links.hop(up_line)
    far_attn = links.swap_x(attn_own)
    cot_near = jnp.concatenate([cot_own, links.swap_y(cot_own)], 0)
    *normed_own, kept, coef, inner, scale, stream_three = mix_forward(
        history, param_low[17:], mixing, wide(param_low[:8])
    )
    normed_own = take_blocks(
        [[normed_own[3], normed_own[2]], [normed_own[0], normed_own[1]]], slots, rows
    )
    down_own = columns_of(mlp_weight[1], member, mlp_cols, 1)
    (
        up_line, far_attn, attn_own, param_low, cot_near, normed_own, kept, coef, inner, scale,
        stream_three, down_own,
    ) = fence(
        up_line, far_attn, attn_own, param_low, cot_near, normed_own, kept, coef, inner, scale,
        stream_three, down_own,
    )
    param_vals = wide(param_low)

    up_line = links.hop(up_line)
    down_line = links.hop(([down_own], [down_own]))
    far_second = links.swap_x(jnp.concatenate([down_own, links.near(up_line, 1)], 0))
    first_y = links.swap_y(normed_own[0])
    cot_core = links.swap_core(cot_near)
    up_line, down_line, far_second, first_y, cot_core, cot_near, normed_own = fence(
        up_line, down_line, far_second, first_y, cot_core, cot_near, normed_own
    )
    far_down, far_up_one = cut(far_second, (rows, rows))

    for _ in range(2, depth):
        down_line = links.hop(down_line)
    up_near = [links.near(up_line, turn) for turn in range(depth)]
    far_third = links.swap_x(jnp.concatenate(up_near[2:], 0))
    first_core = links.swap_core(normed_own[0])
    first_far = links.swap_core(first_y)
    last_y = links.swap_y(normed_own[1])
    group_cot = jnp.concatenate([cot_near, cot_core], 0)
    attn_pair = jnp.concatenate([attn_own, far_attn], 0)
    down_line, far_third, first_core, first_far, last_y, attn_pair, up_near, group_cot = fence(
        down_line, far_third, first_core, first_far, last_y, attn_pair, up_near, group_cot
    )

    attn_line = links.hop(([attn_pair], [attn_pair]))
    down_near = [links.near(down_line, turn) for turn in range(depth)]
    far_fourth = links.swap_x(jnp.concatenate(down_near[1 : depth - 1], 0))
    first_parts = (normed_own[0], first_y, first_core, first_far)
    group_normed = [None] * 4
    group_normed[3] = jnp.concatenate([values[:tok_count] for values in first_parts], 0)
    full_up = jnp.concatenate(up_near + [far_up, far_up_one, far_third], 0)
    up_bias = lax.dynamic_index_in_dim(param_vals, 13 + member, 0)
    act_low, slope = mlp_up(group_normed[3], full_up, up_bias)
    attn_line, far_fourth, act_low, slope, down_near, full_up = fence(
        attn_line, far_fourth, act_low, slope, down_near, full_up
    )

    for _ in range(2, depth - 1):
        attn_line = links.hop(attn_line)
    far_last = links.swap_x(down_near[depth - 1])
    down_sent = half_product([group_cot], [act_low], 1)
    down_first = links.swap_x(down_sent[:rows])
    last_core = links.swap_core(normed_own[1])
    last_far = links.swap_core(last_y)
    group_normed[2] = jnp.concatenate([values[tok_count:] for values in first_parts], 0)
    attn_line, far_last, down_first, down_sent, last_core, last_far, group_normed = fence(
        attn_line, far_last, down_first, down_sent, last_core, last_far, group_normed
    )

    attn_line = links.hop(attn_line)
    down_rest = links.swap_x(down_sent[rows:])
    full_down = jnp.concatenate(down_near + [far_down, far_fourth, far_last], 0)
    up_grad, up_sum = mlp_back(group_cot, full_down, slope)
    up_sent = half_product([group_normed[3]], [up_grad], 1)
    down_own_sum = half_product([group_cot], [act_low], 0)
    three_near, three_sent = spread([up_grad], [full_up])
    last_parts = (normed_own[1], last_y, last_core, last_far)
    group_normed[0] = jnp.concatenate([values[:tok_count] for values in last_parts], 0)
    group_normed[1] = jnp.concatenate([values[tok_count:] for values in last_parts], 0)
    (cot_cols,) = take_blocks([[group_cot]], links.slots_of(member * col_blocks, col_blocks), rows)
    attn_near = [links.near(attn_line, turn) for turn in range(depth)]
    half_depth = depth // 2
    up_sent = cut(up_sent, (half_depth * rows, half_depth * rows))
    (
        attn_near, down_rest, up_grad, up_sum, up_sent, full_down, cot_cols, group_normed,
        down_own_sum, three_near, three_sent,
    ) = fence(
        attn_near, down_rest, up_grad, up_sum, up_sent, full_down, cot_cols, group_normed,
        down_own_sum, three_near, three_sent,
    )

    up_last = links.swap_x(up_sent[1])
    down_arrived = [down_first] + cut(down_rest, (rows,) * (depth - 1))
    down_summed = slot_sums(down_own_sum, down_arrived, range(depth))
    down_parts = [links.swap_z(down_summed[turn], turn) for turn in range(1, depth - 1)]
    full_attn = [
        jnp.concatenate(
            [
                values[side * rows : (side + 1) * rows, at * attn_cols : (at + 1) * attn_cols]
                for side in range(2)
                for values in attn_near
            ],
            0,
        )
        for at in range(4)
    ]
    order = [links.slots_of(links.partner(at) * col_blocks, col_blocks) for at in range(group)]
    context_sum = jnp.concatenate(
        product_rows([cot_cols], [full_attn[3]], jnp.concatenate(order), rows, jnp.float32), 0
    )
    context_sum = [context_sum[:, at * attn_cols : (at + 1) * attn_cols] for at in range(group)]
    sent = low(jnp.concatenate(context_sum[2:], 1))
    sent = turn_core(sent)
    context_sent = context_sum[1] + wide(links.swap_core(sent[:, attn_cols:]))
    context_sent = turn_y(low(context_sent))
    context_own = context_sum[0] + wide(links.swap_core(sent[:, :attn_cols]))
    up_own_sum = half_product([group_normed[3]], [up_grad], 0)
    (
        up_last, down_summed, down_parts, full_attn, context_sent, context_own, up_sent, up_own_sum,
    ) = fence(
        up_last, down_summed, down_parts, full_attn, context_sent, context_own, up_sent, up_own_sum,
    )

    def halves(near, arrived):
        summed = near + wide(arrived)
        return (summed[:tok_count], low(summed[tok_count:]))

    up_first = links.swap_x(up_sent[0])
    down_parts = [down_summed[0]] + down_parts + [links.swap_z(down_summed[-1], depth - 1)]
    context_y = links.swap_y(context_sent)
    half_depth = depth // 2
    last_turns = range(half_depth, depth)
    up_arrived = [None] * half_depth + cut(up_last, (rows,) * half_depth)
    up_summed = [None] * half_depth + slot_sums(up_own_sum, up_arrived, last_turns)
    three_arrived = links.swap_core(three_sent)
    context_grad = low(context_own + wide(context_y))
    (
        up_first, down_parts, context_grad, up_summed, up_own_sum, three_arrived,
    ) = fence(
        up_first, down_parts, context_grad, up_summed, up_own_sum, three_arrived,
    )

    up_parts = [links.swap_z(up_summed[turn], turn) for turn in list(last_turns)[:-1]]
    three_y = low(three_near[tok_count:] + wide(three_arrived[tok_count:]))
    three_y = links.swap_y(three_y)
    attn_bias = lax.dynamic_slice(param_vals, (8, member * attn_cols), (3, attn_cols))
    context_low, proj_grads, proj_sums = attention_inner(
        jnp.cumsum(group_lengths, 1),
        group_normed[:3],
        full_attn[:3],
        attn_bias,
        rope_rows(tok_count),
        context_grad,
    )
    two_sent = half_product(
        [group_normed[2], group_normed[0]], [proj_grads[2], proj_grads[0]], 1
    )
    token_near, token_sent = spread(
        [proj_grads[at] for at in (2, 0, 1)], [full_attn[at] for at in (2, 0, 1)]
    )
    context_turned = turn_y(context_low)
    (
        up_parts, up_summed, context_low, context_turned, proj_grads, proj_sums, two_sent,
        token_near, token_sent, three_y, full_attn, up_first, up_own_sum, act_low, full_down,
    ) = fence(
        up_parts, up_summed, context_low, context_turned, proj_grads, proj_sums, two_sent,
        token_near, token_sent, three_y, full_attn, up_first, up_own_sum, act_low, full_down,
    )

    two_x = links.swap_x(two_sent)
    up_arrived = cut(up_first, (rows,) * half_depth)
    up_summed = slot_sums(up_own_sum, up_arrived, range(half_depth)) + up_summed[half_depth:]
    up_parts = [up_summed[0]] + up_parts
    up_parts += [
        links.swap_z(up_summed[turn], turn) for turn in [depth - 1] + list(range(1, half_depth))
    ]
    token_arrived = links.swap_core(token_sent)
    mlp_near, mlp_sent = product_rows([act_low], [full_down], plain, rows, jnp.float32, 9)
    context_near = jnp.concatenate([context_low, links.swap_y(context_turned)], 1)
    context_sent = turn_core(context_near)
    two_own_sum = half_product(
        [group_normed[2], group_normed[0]], [proj_grads[2], proj_grads[0]], 0
    )
    one_sent = half_product([group_normed[1]], [proj_grads[1]], 1)
    (
        two_x, up_parts, context_near, context_sent, two_own_sum, one_sent, token_near,
        token_arrived, proj_grads, mlp_near, mlp_sent,
    ) = fence(
        two_x, up_parts, context_near, context_sent, two_own_sum, one_sent, token_near,
        token_arrived, proj_grads, mlp_near, mlp_sent,
    )

    one_x = links.swap_x(one_sent)
    two_summed = slot_sums(two_own_sum, cut(two_x, (rows,) * depth), range(depth))
    two_parts = [two_summed[0]]
    two_parts += [
        links.swap_z(two_summed[turn], turn) for turn in list(range(2, depth)) + [1]
    ]
    token_sent = []
    for at in range(3):
        span = slice((2 * at + 1) * tok_count, (2 * at + 2) * tok_count)
        token_sent.append(low(token_near[span] + wide(token_arrived[span])))
    two_y = links.swap_y(token_sent[0])
    zero_y = links.swap_y(token_sent[1])
    context_far = links.swap_core(context_sent)
    order = []
    for owner in links.slots():
        place = (owner // col_blocks) ^ member
        place = (place % 2) * 2 + place // 2
        order.append(place * col_blocks + owner % col_blocks)
    (group_context,) = take_blocks(
        [[jnp.concatenate([context_near, context_far], 1)]],
        jnp.stack(order).astype(jnp.int32),
        rows,
    )
    out_weight_sent = half_product([group_context], [cot_cols], 1)
    one_own_sum = half_product([group_normed[1]], [proj_grads[1]], 0)
    mlp_grad, mlp_mom, mlp_gram = finish_gradient([up_parts, down_parts], mlp_moment)
    (
        one_x, two_parts, zero_y, two_y, group_context, out_weight_sent, one_own_sum, mlp_mom,
        mlp_gram, token_sent,
    ) = fence(
        one_x, two_parts, zero_y, two_y, group_context, out_weight_sent, one_own_sum, mlp_mom,
        mlp_gram, token_sent,
    )

    out_x = links.swap_x(out_weight_sent)
    one_summed = slot_sums(one_own_sum, cut(one_x, (rows,) * depth), range(depth))
    one_parts = [one_summed[0]]
    one_parts += [links.swap_z(one_summed[turn], turn) for turn in range(1, depth)]
    one_y = links.swap_y(token_sent[2])
    mlp_gram = links.sum_stack(mlp_gram)
    out_own_sum = half_product([group_context], [cot_cols], 0)
    attn_out = jnp.dot(group_context, full_attn[3], preferred_element_type=jnp.float32)

    def with_attn(part, addend):
        own = columns_of(part, member, attn_cols, 1) + addend
        return lax.dynamic_update_slice_in_dim(part, own, member * attn_cols, 1)

    out_sent = low(with_attn(mlp_sent, attn_out[near_tok:]))
    out_near = with_attn(mlp_near, attn_out[:near_tok])
    out_own, out_sent = halves(out_near, links.swap_core(out_sent))
    out_x, one_parts, mlp_gram, out_own_sum, out_own, out_sent, zero_y, one_y, two_y, three_y = fence(
        out_x, one_parts, mlp_gram, out_own_sum, out_own, out_sent, zero_y, one_y, two_y, three_y
    )

    out_summed = slot_sums(out_own_sum, cut(out_x, (rows,) * depth), range(depth))
    out_parts = [out_summed[0]]
    out_parts += [links.swap_z(out_summed[turn], turn) for turn in range(1, depth)]
    out_y = links.swap_y(out_sent)
    mlp_new, mlp_low = newton_update(
        mlp_gram, mlp_mom, mlp_master, LR_MUON * 0.2 * math.sqrt(FF)
    )
    out_parts, out_y, mlp_low, zero_y, one_y, two_y, three_y = fence(
        out_parts, out_y, mlp_low, zero_y, one_y, two_y, three_y
    )

    attn_parts = [
        [values[:, attn_cols:] for values in two_parts],
        one_parts,
        [values[:, :attn_cols] for values in two_parts],
        out_parts,
    ]
    attn_grad, attn_mom, attn_gram = finish_gradient(attn_parts, attn_moment)
    attn_gram = links.sum_stack(attn_gram)
    history_grad, sums, mix_weight_grad, mixing_grad = mix_backward(
        history,
        out_grad,
        tok_weight[:, None],
        [(token_near, token_arrived, at) for at in (1, 2, 0)] + [(three_near, three_arrived, 0)],
        [zero_y, one_y, two_y, three_y],
        kept,
        coef,
        inner,
        scale,
        param_low[17:],
        mixing,
        param_vals[:8],
    )
    mlp_across = links.swap_y(mlp_low)
    mlp_other = links.swap_core(mlp_low)
    layer_out = low(stream_three + out_own + wide(out_y) + (param_vals[11] + param_vals[12]))

    def placed(values, total):
        return lax.dynamic_update_slice_in_dim(
            jnp.zeros((values.shape[0], total), jnp.float32), values, member * values.shape[1], 1
        )

    param_grad = jnp.concatenate(
        [
            sums[:8],
            placed(proj_sums[:3], model_width),
            sums[8:9],
            sums[8:9],
            placed(up_sum, group * mlp_cols).reshape(-1, model_width),
            mix_weight_grad,
        ],
        0,
    )
    param_pieces_grad = jnp.moveaxis(param_grad.reshape(param_rows, members, rows), 1, 0)
    mix_size = mixing_grad.size
    mix_rows = -(-mix_size // rows)
    mix_flat = jnp.pad(mixing_grad.reshape(-1), (0, mix_rows * rows - mix_size))
    mix_flat = jnp.broadcast_to(mix_flat.reshape(1, mix_rows, rows), (members, mix_rows, rows))
    small_sent = jnp.concatenate([param_pieces_grad, mix_flat], 1)
    attn_gram, small_sent, attn_mom, mlp_across, mlp_other = fence(
        attn_gram, small_sent, attn_mom, mlp_across, mlp_other
    )

    attn_new, attn_copy = [], []
    for pair in range(2):
        fresh, attn_low = newton_update(
            attn_gram, attn_mom, attn_master, LR_MUON * 0.2 * math.sqrt(model_width), pair, 1
        )
        attn_new.append(fresh)
        attn_copy.append(
            links.gather_copies(attn_low, links.swap_y(attn_low), links.swap_core(attn_low))
        )
    attn_new = jnp.concatenate(attn_new, 0)
    attn_copy = jnp.concatenate(attn_copy, 0)
    mlp_copy = links.gather_copies(mlp_low, mlp_across, mlp_other)
    small_sent, attn_low = fence(small_sent, attn_low)
    small = lax.all_to_all(small_sent, "fsdp", 0, 0, tiled=True)
    small = links.sum_group(jnp.sum(small, 0))
    param_part = small[:param_rows]
    mixing_grad = small[param_rows:].reshape(-1)[:mix_size].reshape(mixing_grad.shape)
    params_m_new, params_v_new, params_new = adamw(params, param_part, params_m, params_v)
    mix_out_m_new, mix_out_v_new, mix_out_new = adamw(mix_out, mixing_grad, mix_out_m, mix_out_v)
    return (
        layer_out,
        history_grad,
        attn_grad,
        attn_mom,
        attn_new,
        attn_copy,
        mlp_grad,
        mlp_mom,
        mlp_new,
        mlp_copy,
        param_part,
        param_part[11:13],
        params_m_new,
        params_v_new,
        params_new,
        mixing_grad,
        mix_out_m_new,
        mix_out_v_new,
        mix_out_new,
    )


def solution(mesh):
    in_specs = (
        P(None, ("dp", "fsdp"), None),
        P(("dp", "fsdp"), None),
        P(("dp", "fsdp"), None),
        P(("dp", "fsdp"), None),
        P(),
        P(None, "fsdp", None),
        P(None, "fsdp", "dp"),
        P(None, "fsdp", "dp"),
        P(None, "fsdp", None),
        P(None, "fsdp", "dp"),
        P(None, "fsdp", "dp"),
        P(None, "fsdp"),
        P(None, "fsdp"),
        P(None, "fsdp"),
        P(),
        P(),
        P(),
    )
    out_specs = (
        P(("dp", "fsdp"), None),
        P(None, ("dp", "fsdp"), None),
        P(None, "fsdp", "dp"),
        P(None, "fsdp", "dp"),
        P(None, "fsdp", "dp"),
        P(None, "fsdp", None),
        P(None, "fsdp", "dp"),
        P(None, "fsdp", "dp"),
        P(None, "fsdp", "dp"),
        P(None, "fsdp", None),
        P(None, "fsdp"),
        P(None, "fsdp"),
        P(None, "fsdp"),
        P(None, "fsdp"),
        P(None, "fsdp"),
        P(),
        P(),
        P(),
        P(),
    )
    return jax.shard_map(body, mesh=mesh, in_specs=in_specs, out_specs=out_specs, check_vma=False)
```
